32 devices in a mesh: mp: 2 (over x), lat: 2 (over y), lon: 8 (over z, core).
Axes of the slice: x: 2, y: 2, z: 4, core: 2. Of those that a mesh axis runs over, the one named last changes fastest.
Arguments:
- adjoint: float32 [2, 2, 72, 32, 1024], P('mp', None, None, 'lat', 'lon'), may hold values from -6 to 6
- courant: float32 [2, 2, 32, 1024], P('mp', None, 'lat', 'lon'), may hold values from 0.05 to 0.45
- diffusivity: float32 [2, 71, 32, 1024], P('mp', None, 'lat', 'lon'), may hold values from 0.005 to 0.24
- coupling: float32 [2, 32, 1024], P('mp', 'lat', 'lon'), may hold values from 0.05 to 0.45
- partner: int32 [2, 2048], P('mp', ('lat', 'lon')), may hold values from 0 to 2047, as said below
- mask: int32 [2, 32, 1024], P('mp', 'lat', 'lon'), may hold values from 0 to 1, as said below
Outputs:
- result_adjoint: float32 [2, 2, 72, 32, 1024], P('mp', None, None, 'lat', 'lon')
The draws below stay inside these ranges and needn't reach their ends.
Inputs may be any that keep to these rules, and one draw needn't show every extreme that they name: partner[0, q] is the ocean tile coupled to atmosphere tile q and partner[1] is its inverse, tiles numbered as in the first step; the tiles of one device have partners on exactly 8 devices, 16 tiles on each. `mask`: 1 marks a cell over sea; coupled tiles carry the same flags cell by cell.
All inputs are finite; a program needn't handle non-finite values.
Results may differ from the reference program's by a relative error of at most 0.00002.
Values sent between devices are 32-bit elements; how exact they have to be, the bound alone decides.
No kernel may reach another device: no remote copies, remote signals or barrier semaphores. Data moves between devices by JAX's collectives and lax.ppermute only.
A program may use at most 64 MiB of HBM per device.

```python
import math
from functools import partial
import jax
import jax.numpy as jnp
from jax import lax

NTR = 2
LEV = 72
TILE = 16
LATB = 16
LONB = 128
STEPS = 4
NLAT = 32
NLON = 1024
TPD = 128
NT = 2048
CAP = 16
N_LAT = 2
N_LON = 8


def pair_tables(key):
    device_count = NT // TPD
    groups_sent = TPD // CAP
    keys_all = jax.random.split(key, 5)
    sources_order = jax.random.permutation(keys_all[0], device_count)
    targets_order = jax.random.permutation(keys_all[1], device_count)
    offsets = jax.random.permutation(keys_all[2], device_count)[:groups_sent]
    sender_perm = jax.vmap(lambda subkey: jax.random.permutation(subkey, TPD))(jax.random.split(keys_all[3], device_count))
    target_perm = jax.vmap(lambda subkey: jax.random.permutation(subkey, TPD))(jax.random.split(keys_all[4], device_count))
    group_index = sender_perm // CAP
    rank_index = sender_perm % CAP
    target = targets_order[(sources_order[:, None] + offsets[group_index]) % device_count]
    local_slot = target_perm[target, group_index * CAP + rank_index]
    forward = (target * TPD + local_slot).reshape(-1).astype(jnp.int32)
    backward = jnp.zeros((NT,), jnp.int32).at[forward].set(jnp.arange(NT, dtype=jnp.int32))
    return (forward, backward)


def draw_partner(key, part):
    forward, backward = pair_tables(jax.random.fold_in(key, 11))
    return jnp.stack([forward, backward])


def tiles_to_grid(tile_flags):
    shaped = tile_flags.reshape(N_LAT, N_LON, LATB, LONB // TILE, TILE)
    return shaped.transpose(0, 2, 1, 3, 4).reshape(NLAT, NLON)


def draw_mask(key, part):
    forward, backward = pair_tables(jax.random.fold_in(key, 11))
    atmos_flags = (jax.random.randint(jax.random.fold_in(key, 23), (NT, TILE), 0, 3) > 0).astype(jnp.int32)
    ocean_flags = atmos_flags[backward]
    return jnp.stack([tiles_to_grid(atmos_flags), tiles_to_grid(ocean_flags)])


def levels(own_key, shape, shards, smallest, top_value):
    factor_of, own = 1.0, jax.random.fold_in(own_key, 6)
    for dim, blocks in shards:
        draws = jnp.exp(jax.random.uniform(jax.random.fold_in(own, dim), (blocks,), jnp.float32, smallest / len(shards), top_value / len(shards)))
        factor_of = factor_of * jnp.repeat(draws, shape[dim] // blocks).reshape([-1 if axis == dim else 1 for axis in range(len(shape))])
    return factor_of


def gaussian(stream_key, shape, scale, limit, cuts=(), held_as=jnp.bfloat16):
    entries = jax.random.normal(stream_key, shape, jnp.float32) * scale
    if len(cuts) > 0:
        entries = levels(stream_key, shape, cuts, -0.22, 0.18) * entries
    return jnp.clip(entries, min=-limit, max=limit).astype(held_as)


def setup_inputs(seed: int = 0) -> dict:
    key_of = jax.random.split(jax.random.key(seed), 7)
    return {
        "adjoint": gaussian(key_of[0], (2, NTR, LEV, NLAT, NLON), 1.0, 6.0, ((0, 2), (3, 2), (4, 8)), jnp.float32),
        "courant": jnp.clip(0.05 + 0.39999999 * jax.random.uniform(key_of[1], (2, 2, NLAT, NLON), jnp.float32) ** levels(key_of[1], (2, 2, NLAT, NLON), ((0, 2), (2, 2), (3, 8)), -0.2, 0.2), 0.05, 0.45),
        "diffusivity": jnp.clip(jnp.exp(math.log(0.24) - 3.871201 * jax.random.uniform(key_of[2], (2, LEV - 1, NLAT, NLON), jnp.float32) ** levels(key_of[2], (2, LEV - 1, NLAT, NLON), ((0, 2), (2, 2), (3, 8)), -0.2, 0.2)), 0.005, 0.24),
        "coupling": jnp.clip(0.05 + 0.39999999 * jax.random.uniform(key_of[3], (2, NLAT, NLON), jnp.float32) ** levels(key_of[3], (2, NLAT, NLON), ((0, 2), (1, 2), (2, 8)), -0.2, 0.2), 0.05, 0.45),
        "partner": draw_partner(jax.random.fold_in(key_of[6], 71), 0),
        "mask": draw_mask(jax.random.fold_in(key_of[6], 71), 0),
    }


def advect(fields, courant_pair):
    zonal = courant_pair[0]
    meridional = courant_pair[1]
    weight = (1.0 - zonal) - meridional
    eastward = zonal * fields
    northward = meridional * fields
    east_next = jnp.roll(eastward, -1, axis=-1)
    north_next = jnp.concatenate([northward[..., 1:, :], jnp.zeros_like(northward[..., :1, :])], axis=-2)
    return (weight * fields + east_next) + north_next


def diffuse(fields, kappa):
    fluxes = kappa * (fields[1:] - fields[:-1])
    edge = jnp.zeros_like(fields[:1])
    return (fields + jnp.concatenate([fluxes, edge], 0)) - jnp.concatenate([edge, fluxes], 0)


def column_step(tracer_fields, courant_pair, kappa):
    return diffuse(advect(tracer_fields, courant_pair), kappa)


def to_tiles(surface):
    tracers = surface.shape[0]
    shaped = surface.reshape(tracers, N_LAT, LATB, N_LON, LONB // TILE, TILE)
    return shaped.transpose(1, 3, 2, 4, 0, 5).reshape(NT, tracers * TILE)


def from_tiles(tile_rows, tracers):
    shaped = tile_rows.reshape(N_LAT, N_LON, LATB, LONB // TILE, tracers, TILE)
    return shaped.transpose(4, 0, 2, 1, 3, 5).reshape(tracers, NLAT, NLON)


def reference(adjoint, courant, diffusivity, coupling, partner, mask):
    fields_all = [adjoint[0], adjoint[1]]
    wet_tiles = [to_tiles(jnp.broadcast_to(mask[model_index].astype(jnp.float32), (NTR, NLAT, NLON))) for model_index in range(2)]
    for step_index in range(STEPS):
        mixed = []
        for model_index in range(2):
            stepper = partial(column_step, courant_pair=courant[model_index], kappa=diffusivity[model_index])
            mixed.append(lax.map(stepper, fields_all[model_index]))
        own = [to_tiles(mixed[model_index][:, 0]) for model_index in range(2)]
        scaled = [to_tiles(coupling[model_index] * mixed[model_index][:, 0]) for model_index in range(2)]
        received = [scaled[1][partner[0]], scaled[0][partner[1]]]
        updated = []
        for model_index in range(2):
            new_tiles = own[model_index] + wet_tiles[model_index] * (received[model_index] - scaled[model_index])
            surface = from_tiles(new_tiles, NTR)
            updated.append(mixed[model_index].at[:, 0].set(surface))
        fields_all = updated
    return jnp.stack(fields_all)
```

```python
import functools

import jax
import jax.numpy as jnp
from jax import lax
from jax.experimental import pallas as pl
from jax.experimental.pallas import tpu as pltpu
from jax.sharding import PartitionSpec as P

TILE = 16
STEPS = 4
F32 = jnp.float32
BF16 = jnp.bfloat16


def lane_iota(shape):
    return lax.broadcasted_iota(jnp.int32, shape, len(shape) - 1)


def row_iota(shape):
    return lax.broadcasted_iota(jnp.int32, shape, len(shape) - 2)


def lane_roll(value, shift):
    return pltpu.roll(value, shift % value.shape[-1], 1)


def three_parts(value):
    high = value.astype(BF16)
    rest = value - high.astype(F32)
    middle = rest.astype(BF16)
    low = (rest - middle.astype(F32)).astype(BF16)
    return high, middle, low


def picked(one_hot, value):
    total = None
    for part in three_parts(value):
        term = jnp.dot(one_hot, part, preferred_element_type=F32)
        total = term if total is None else total + term
    return total


def next_row(value):
    return pltpu.roll(value, value.shape[0] - 1, 0)


def edges_kernel(fields_ref, courant_ref, north_ref, east_ref):
    tracers, levels, rows, cols = fields_ref.shape
    zonal = courant_ref[0]
    first_row = courant_ref[1][0:1, :]
    lane = lane_iota((rows, cols))
    for tracer in range(tracers):
        gathered = jnp.zeros((rows, cols), F32)
        for k in range(levels):
            field = fields_ref[tracer, k]
            north_ref[tracer, k : k + 1, :] = first_row * field[0:1, :]
            gathered = jnp.where(lane == k, lane_roll(zonal * field, k), gathered)
        east_ref[tracer] = gathered


def mixing_kernel(
    fields_ref, kappa_ref, courant_ref, north_in, east_in, out_ref, north_ref, east_ref
):
    tracers, levels, rows, cols = fields_ref.shape
    zonal, meridional = courant_ref[0], courant_ref[1]
    weight = (1.0 - zonal) - meridional
    first_row = meridional[0:1, :]
    lane = lane_iota((rows, cols))
    row = row_iota((rows, cols))
    for tracer in range(tracers):
        east_edges = east_in[tracer]
        gathered = jnp.zeros((rows, cols), F32)
        upper = None
        flux_above = None

        def advected(k):
            field = fields_ref[tracer, k]
            eastward = zonal * field
            northward = meridional * field
            east = jnp.where(
                lane == cols - 1, lane_roll(east_edges, cols - 1 - k), lane_roll(eastward, cols - 1)
            )
            edge = jnp.broadcast_to(north_in[tracer, k : k + 1, :], (rows, cols))
            north = jnp.where(row == rows - 1, edge, next_row(northward))
            return (weight * field + east) + north

        here = advected(0)
        for k in range(levels):
            result = here
            if k + 1 < levels:
                below = advected(k + 1)
                flux = kappa_ref[k] * (below - here)
                result = result + flux
            if k > 0:
                result = result - flux_above
            out_ref[tracer, k] = result
            if k > 0:
                north_ref[tracer, k : k + 1, :] = first_row * result[0:1, :]
                gathered = jnp.where(lane == k, lane_roll(zonal * result, k), gathered)
            else:
                north_ref[tracer, k : k + 1, :] = jnp.zeros((1, cols), F32)
            if k + 1 < levels:
                here, flux_above = below, flux
        east_ref[tracer] = gathered


def send_surface(surface, below, refs, send_ref):
    courant_ref, kappa_ref, coupling_ref, west_ref, south_ref, pack_ref = refs
    tracers = len(surface)
    zonal, meridional = courant_ref[0], courant_ref[1]
    weight = (1.0 - zonal) - meridional
    rows, cols = zonal.shape
    groups = cols // TILE
    lane = lane_iota((rows, cols))
    row = row_iota((rows, cols))
    kappa = kappa_ref[0]
    coupling = coupling_ref[...]
    group = lane // TILE
    tiles, edge_north, edge_east = [], [], []
    place = lane == (row % groups) * TILE + (TILE - 1) - row // groups
    west_a = lane_roll(west_ref[0], 1)
    west_b = lane_roll(west_ref[1], 1)
    for tracer in range(tracers):
        parts = []
        for field in (surface[tracer], below[tracer]):
            eastward, northward = zonal * field, meridional * field
            east = jnp.where(lane == cols - 1, 0.0, lane_roll(eastward, cols - 1))
            north = jnp.where(row == rows - 1, 0.0, next_row(northward))
            parts.append((eastward, northward, (weight * field + east) + north))
        (east0, north0, here), (east1, north1, under) = parts
        mixed = here + kappa * (under - here)
        scaled = coupling * mixed
        edge_north.append(
            south_ref[0, rows - 1 : rows, :] * north0[0:1] + south_ref[1, rows - 1 : rows, :] * north1[0:1]
        )
        column = west_a * east0 + west_b * east1
        column = jnp.broadcast_to(column[:, 0:1], (rows, cols))
        edge_east.append(jnp.sum(jnp.where(place, column, 0.0), axis=0, keepdims=True))
        blocks = []
        for c in range(groups):
            block = jnp.where(group == c, scaled, 0.0)
            shift = TILE
            while shift < cols:
                block = block + lane_roll(block, shift)
                shift *= 2
            blocks.append(block)
        tiles.append(jnp.concatenate(blocks, axis=0))
    slots = picked(pack_ref[...], jnp.concatenate(tiles, axis=0))
    height = slots.shape[0] // groups
    slot_group = lane_iota((height, cols)) // TILE
    packed = jnp.zeros((height, cols), F32)
    for g in range(groups):
        packed = jnp.where(slot_group == g, slots[g * height : (g + 1) * height], packed)
    devices = send_ref.shape[0] // 2
    per_device = height // devices
    edges = jnp.concatenate(edge_north + edge_east, axis=0)
    for half in range(2):
        for device in range(devices):
            send_ref[half * devices + device, 0:per_device, :] = packed[
                device * per_device : (device + 1) * per_device
            ]
            send_ref[half * devices + device, per_device : per_device + 2 * tracers, :] = edges


def receive_surface(model_ref, recv_ref, pick_ref, place_ref, surface, coupling_ref, mask_ref):
    devices = recv_ref.shape[0] // 2
    rows, cols = coupling_ref.shape
    groups = cols // TILE
    tracers = len(surface)
    other = (1 - model_ref[0]) * devices
    slab = recv_ref[pl.ds(other, devices)].reshape(devices * recv_ref.shape[1], cols)
    table = jnp.concatenate([slab, lane_roll(slab, 1)], axis=0)
    found = picked(pick_ref[...], table)
    count = rows * groups
    group = lane_iota((rows, cols)) // TILE
    wet = mask_ref[...].astype(F32)
    coupling = coupling_ref[...]
    updated = []
    for tracer in range(tracers):
        total = None
        for kind in range(3):
            start = (kind * tracers + tracer) * count
            term = jnp.where(place_ref[kind] > 0, found[start : start + count], 0.0)
            total = term if total is None else total + term
        shift = TILE
        while shift < cols:
            total = total + lane_roll(total, shift)
            shift *= 2
        received = jnp.zeros((rows, cols), F32)
        for c in range(groups):
            received = jnp.where(group == c, total[c * rows : (c + 1) * rows], received)
        own = surface[tracer]
        updated.append(own + wet * (received - coupling * own))
    return updated


def first_send_kernel(fields_ref, *refs):
    *inputs, send_ref = refs
    tracers = fields_ref.shape[0]
    surface = [fields_ref[tracer, 0] for tracer in range(tracers)]
    below = [fields_ref[tracer, 1] for tracer in range(tracers)]
    send_surface(surface, below, inputs, send_ref)


def exchange_kernel(
    model_ref, fields_ref, recv_ref, pick_ref, place_ref, mask_ref, north_in, east_in, *refs
):
    *inputs, fields_out, send_ref, north_ref, east_ref = refs
    courant_ref, _, coupling_ref = inputs[:3]
    tracers = fields_ref.shape[0]
    surface = [fields_ref[tracer, 0] for tracer in range(tracers)]
    surface = receive_surface(model_ref, recv_ref, pick_ref, place_ref, surface, coupling_ref, mask_ref)
    below = [fields_ref[tracer, 1] for tracer in range(tracers)]
    send_surface(surface, below, inputs, send_ref)
    zonal, meridional = courant_ref[0], courant_ref[1]
    lane = lane_iota(zonal.shape)
    north_ref[...] = north_in[...]
    for tracer in range(tracers):
        fields_out[tracer, 0] = surface[tracer]
        fields_out[tracer, 1] = below[tracer]
        north_ref[tracer, 0:1, :] = meridional[0:1, :] * surface[tracer][0:1, :]
        east_ref[tracer] = jnp.where(lane == 0, zonal * surface[tracer], east_in[tracer])


def last_kernel(model_ref, fields_ref, recv_ref, pick_ref, place_ref, mask_ref, coupling_ref, fields_out):
    tracers = fields_ref.shape[0]
    surface = [fields_ref[tracer, 0] for tracer in range(tracers)]
    surface = receive_surface(model_ref, recv_ref, pick_ref, place_ref, surface, coupling_ref, mask_ref)
    for tracer in range(tracers):
        fields_out[tracer, 0] = surface[tracer]


VMEM_LIMIT = 32 * 1024 * 1024


def whole(array):
    zeros = (0,) * array.ndim
    return pl.BlockSpec(array.shape, lambda i: zeros)


def top(array, levels):
    tracers, _, rows, cols = array.shape
    return pl.BlockSpec((tracers, levels, rows, cols), lambda i: (0, 0, 0, 0))


SCALAR = pl.BlockSpec(memory_space=pltpu.SMEM)


def call(kernel, operands, specs, out_shape, out_specs, name, aliases=None, flops=0, moved=0):
    return pl.pallas_call(
        kernel,
        grid=(1,),
        in_specs=specs,
        out_shape=out_shape,
        out_specs=out_specs,
        input_output_aliases=aliases or {},
        name=name,
        cost_estimate=pl.CostEstimate(flops=flops, bytes_accessed=moved, transcendentals=0),
        compiler_params=pltpu.CompilerParams(vmem_limit_bytes=VMEM_LIMIT),
    )(*operands)


def like(array):
    return jax.ShapeDtypeStruct(array.shape, array.dtype)


def routing_tables(partner, rows, cols, capacity, main_rows, tracers):
    groups = cols // TILE
    count = rows * groups
    n_lat, n_lon = lax.axis_size("lat"), lax.axis_size("lon")
    devices = n_lat * n_lon
    per_device = main_rows * tracers
    partner = partner.reshape(rows, groups).T.reshape(count)
    own = (jnp.arange(count) % rows) * groups + jnp.arange(count) // rows
    target, slot = partner // count, partner % count
    same = target[:, None] == target[None, :]
    sent = jnp.sum(same & (own[None, :] < own[:, None]), axis=1)
    came = jnp.sum(same & (slot[None, :] < slot[:, None]), axis=1)
    height = devices * per_device
    packs = []
    for tracer in range(tracers):
        index = (sent % groups) * height + target * per_device + tracer * main_rows + sent // groups
        packs.append(jnp.arange(groups * height)[:, None] == index[None, :])
    pack = jnp.concatenate(packs, axis=1).astype(BF16)
    deep = per_device + 2 * tracers
    row, group = slot // groups, slot % groups
    lat, lon = target // n_lon, target % n_lon
    north_ok = (row == rows - 1) & (lat < n_lat - 1)
    east_ok = group == groups - 1
    east_device = lat * n_lon + (lon + 1) % n_lon
    picks = []
    for tracer in range(tracers):
        picks.append(target * deep + tracer * main_rows + came // groups)
    for tracer in range(tracers):
        picks.append(jnp.where(north_ok, (target + n_lon) * deep + per_device + tracer, -1))
    for tracer in range(tracers):
        index = east_device * deep + per_device + tracers + tracer + (row // groups) * (devices * deep)
        picks.append(jnp.where(east_ok, index, -1))
    picks = jnp.concatenate(picks)
    pick = (picks[:, None] == jnp.arange(2 * devices * deep)[None, :]).astype(BF16)
    lane = jnp.arange(cols)[None, :]
    place = jnp.stack(
        [
            lane // TILE == (came % groups)[:, None],
            lane // TILE == group[:, None],
            lane == (row % groups)[:, None] * TILE + TILE - 1,
        ]
    ).astype(F32)
    return pack, pick, place


def local(adjoint, courant, diffusivity, coupling, partner, mask):
    fields = adjoint[0]
    courant, kappa, coupling, partner, mask = courant[0], diffusivity[0], coupling[0], partner[0], mask[0]
    tracers, levels, rows, cols = fields.shape
    groups = cols // TILE
    count = rows * groups
    n_lat, n_lon = lax.axis_size("lat"), lax.axis_size("lon")
    devices = n_lat * n_lon
    capacity = max(2, 2 * count // devices)
    main_rows = -(-capacity // groups)
    deep = main_rows * tracers + 2 * tracers
    model = lax.axis_index("mp").astype(jnp.int32).reshape(1)
    last_row = lax.axis_index("lat") == n_lat - 1

    top_kappa = kappa[0]
    share = jnp.stack([coupling * (1.0 - top_kappa), coupling * top_kappa])
    from_west = lax.ppermute(share, "lon", [(i, (i + 1) % n_lon) for i in range(n_lon)])
    from_south = lax.ppermute(share, "lat", [(i, (i + 1) % n_lat) for i in range(n_lat)])

    def halo(north, east):
        north = lax.ppermute(north, "lat", [((i + 1) % n_lat, i) for i in range(n_lat)])
        east = lax.ppermute(east, "lon", [((i + 1) % n_lon, i) for i in range(n_lon)])
        return jnp.where(last_row, 0.0, north), east

    north_shape = jax.ShapeDtypeStruct((tracers, levels, cols), F32)
    east_shape = jax.ShapeDtypeStruct((tracers, rows, cols), F32)
    send_shape = jax.ShapeDtypeStruct((2 * devices, deep, cols), F32)
    field_bytes = 4 * tracers * levels * rows * cols

    north, east = call(
        edges_kernel,
        (fields, courant),
        [whole(fields), whole(courant)],
        (north_shape, east_shape),
        (whole(north_shape), whole(east_shape)),
        "edges",
        flops=field_bytes,
        moved=field_bytes,
    )
    pack, pick, place = routing_tables(partner, rows, cols, capacity, main_rows, tracers)
    kappa_top = kappa[0:1]
    sending = (courant, kappa_top, coupling, from_west, from_south, pack)
    sending_specs = [whole(a) for a in sending]
    send = call(
        first_send_kernel,
        (fields, *sending),
        [top(fields, 2), *sending_specs],
        send_shape,
        whole(send_shape),
        "first_send",
    )
    for step in range(STEPS):
        recv = lax.all_to_all(send, ("mp", "lat", "lon"), split_axis=0, concat_axis=0, tiled=True)
        north_in, east_in = halo(north, east)
        fields, north, east = call(
            mixing_kernel,
            (fields, kappa, courant, north_in, east_in),
            [whole(a) for a in (fields, kappa, courant, north_in, east_in)],
            (like(fields), north_shape, east_shape),
            (whole(fields), whole(north_shape), whole(east_shape)),
            "mixing",
            flops=10 * field_bytes,
            moved=3 * field_bytes,
        )
        if step + 1 < STEPS:
            arriving = (model, fields, recv, pick, place, mask, north, east)
            specs = [SCALAR, top(fields, 2), *(whole(a) for a in arriving[2:])]
            fields, send, north, east = call(
                exchange_kernel,
                (*arriving, *sending),
                [*specs, *sending_specs],
                (like(fields), send_shape, north_shape, east_shape),
                (top(fields, 2), whole(send_shape), whole(north_shape), whole(east_shape)),
                "exchange",
                aliases={1: 0},
            )
        else:
            arriving = (model, fields, recv, pick, place, mask, coupling)
            specs = [SCALAR, top(fields, 1), *(whole(a) for a in arriving[2:])]
            fields = call(
                last_kernel,
                arriving,
                specs,
                like(fields),
                top(fields, 1),
                "last",
                aliases={1: 0},
            )
    return fields[None]


def solution(mesh):
    placed = (
        P("mp", None, None, "lat", "lon"),
        P("mp", None, "lat", "lon"),
        P("mp", None, "lat", "lon"),
        P("mp", "lat", "lon"),
        P("mp", ("lat", "lon")),
        P("mp", "lat", "lon"),
    )
    return jax.shard_map(
        local,
        mesh=mesh,
        in_specs=placed,
        out_specs=P("mp", None, None, "lat", "lon"),
        check_vma=False,
    )
```

```python
import functools

import jax
import jax.numpy as jnp
from jax import lax
from jax.experimental import pallas as pl
from jax.experimental.pallas import tpu as pltpu
from jax.sharding import PartitionSpec as P

TILE = 16
STEPS = 4
F32 = jnp.float32
BF16 = jnp.bfloat16


def lane_iota(shape):
    return lax.broadcasted_iota(jnp.int32, shape, len(shape) - 1)


def row_iota(shape):
    return lax.broadcasted_iota(jnp.int32, shape, len(shape) - 2)


def lane_roll(value, shift):
    return pltpu.roll(value, shift % value.shape[-1], 1)


def three_parts(value):
    high = value.astype(BF16)
    rest = value - high.astype(F32)
    middle = rest.astype(BF16)
    low = (rest - middle.astype(F32)).astype(BF16)
    return high, middle, low


def picked(one_hot, value):
    total = None
    for part in three_parts(value):
        term = jnp.dot(one_hot, part, preferred_element_type=F32)
        total = term if total is None else total + term
    return total


def next_row(value):
    return pltpu.roll(value, value.shape[0] - 1, 0)


def edges_kernel(fields_ref, courant_ref, north_ref, east_ref):
    tracers, levels, rows, cols = fields_ref.shape
    zonal = courant_ref[0]
    first_row = courant_ref[1][0:1, :]
    lane = lane_iota((rows, cols))
    for tracer in range(tracers):
        gathered = jnp.zeros((rows, cols), F32)
        for k in range(levels):
            field = fields_ref[tracer, k]
            north_ref[tracer, k : k + 1, :] = first_row * field[0:1, :]
            gathered = jnp.where(lane == k, lane_roll(zonal * field, k), gathered)
        east_ref[tracer] = gathered


def mixing_kernel(
    fields_ref, surface_ref, kappa_ref, courant_ref, north_in, east_in, out_ref, top_ref, north_ref, east_ref
):
    tracers, levels, rows, cols = fields_ref.shape
    zonal, meridional = courant_ref[0], courant_ref[1]
    weight = (1.0 - zonal) - meridional
    first_row = meridional[0:1, :]
    lane = lane_iota((rows, cols))
    row = row_iota((rows, cols))
    for tracer in range(tracers):
        east_edges = east_in[tracer]
        flux_above = None

        def advected(k):
            field = surface_ref[tracer] if k == 0 else fields_ref[tracer, k]
            eastward = zonal * field
            northward = meridional * field
            east = jnp.where(
                lane == cols - 1, lane_roll(east_edges, cols - 1 - k), lane_roll(eastward, cols - 1)
            )
            edge = jnp.broadcast_to(north_in[tracer, k : k + 1, :], (rows, cols))
            north = jnp.where(row == rows - 1, edge, next_row(northward))
            return (weight * field + east) + north

        here = advected(0)
        for k in range(levels):
            result = here
            if k + 1 < levels:
                below = advected(k + 1)
                flux = kappa_ref[k] * (below - here)
                result = result + flux
            if k > 0:
                result = result - flux_above
            out_ref[tracer, k] = result
            if k < 2:
                top_ref[tracer, k] = result
            north_ref[tracer, k : k + 1, :] = first_row * result[0:1, :]
            if k + 1 < levels:
                here, flux_above = below, flux
        gathered = jnp.zeros((rows, cols), F32)
        for k in range(levels):
            gathered = jnp.where(lane == k, lane_roll(zonal * out_ref[tracer, k], k), gathered)
        east_ref[tracer] = gathered


def send_surface(surface, below, refs, send_ref):
    courant_ref, kappa_ref, coupling_ref, west_ref, south_ref, pack_ref = refs
    tracers = len(surface)
    zonal, meridional = courant_ref[0], courant_ref[1]
    weight = (1.0 - zonal) - meridional
    rows, cols = zonal.shape
    groups = cols // TILE
    lane = lane_iota((rows, cols))
    row = row_iota((rows, cols))
    kappa = kappa_ref[0]
    coupling = coupling_ref[...]
    group = lane // TILE
    tiles, edge_north, edge_east = [], [], []
    place = lane == (row % groups) * TILE + (TILE - 1) - row // groups
    west_a = lane_roll(west_ref[0], 1)
    west_b = lane_roll(west_ref[1], 1)
    for tracer in range(tracers):
        parts = []
        for field in (surface[tracer], below[tracer]):
            eastward, northward = zonal * field, meridional * field
            east = jnp.where(lane == cols - 1, 0.0, lane_roll(eastward, cols - 1))
            north = jnp.where(row == rows - 1, 0.0, next_row(northward))
            parts.append((eastward, northward, (weight * field + east) + north))
        (east0, north0, here), (east1, north1, under) = parts
        mixed = here + kappa * (under - here)
        scaled = coupling * mixed
        edge_north.append(
            south_ref[0, rows - 1 : rows, :] * north0[0:1] + south_ref[1, rows - 1 : rows, :] * north1[0:1]
        )
        column = west_a * east0 + west_b * east1
        column = jnp.broadcast_to(column[:, 0:1], (rows, cols))
        edge_east.append(jnp.sum(jnp.where(place, column, 0.0), axis=0, keepdims=True))
        blocks = []
        for c in range(groups):
            block = jnp.where(group == c, scaled, 0.0)
            shift = TILE
            while shift < cols:
                block = block + lane_roll(block, shift)
                shift *= 2
            blocks.append(block)
        tiles.append(jnp.concatenate(blocks, axis=0))
    slots = picked(pack_ref[...], jnp.concatenate(tiles, axis=0))
    height = slots.shape[0] // groups
    slot_group = lane_iota((height, cols)) // TILE
    packed = jnp.zeros((height, cols), F32)
    for g in range(groups):
        packed = jnp.where(slot_group == g, slots[g * height : (g + 1) * height], packed)
    devices = send_ref.shape[0] // 2
    per_device = height // devices
    edges = jnp.concatenate(edge_north + edge_east, axis=0)
    for half in range(2):
        for device in range(devices):
            send_ref[half * devices + device, 0:per_device, :] = packed[
                device * per_device : (device + 1) * per_device
            ]
            send_ref[half * devices + device, per_device : per_device + 2 * tracers, :] = edges


def receive_surface(model_ref, recv_ref, pick_ref, place_ref, surface, coupling_ref, mask_ref):
    devices = recv_ref.shape[0] // 2
    rows, cols = coupling_ref.shape
    groups = cols // TILE
    tracers = len(surface)
    other = (1 - model_ref[0]) * devices
    slab = recv_ref[pl.ds(other, devices)].reshape(devices * recv_ref.shape[1], cols)
    table = jnp.concatenate([slab, lane_roll(slab, 1)], axis=0)
    found = picked(pick_ref[...], table)
    count = rows * groups
    group = lane_iota((rows, cols)) // TILE
    wet = mask_ref[...].astype(F32)
    coupling = coupling_ref[...]
    updated = []
    for tracer in range(tracers):
        total = None
        for kind in range(3):
            start = (kind * tracers + tracer) * count
            term = jnp.where(place_ref[kind] > 0, found[start : start + count], 0.0)
            total = term if total is None else total + term
        shift = TILE
        while shift < cols:
            total = total + lane_roll(total, shift)
            shift *= 2
        received = jnp.zeros((rows, cols), F32)
        for c in range(groups):
            received = jnp.where(group == c, total[c * rows : (c + 1) * rows], received)
        own = surface[tracer]
        updated.append(own + wet * (received - coupling * own))
    return updated


def first_send_kernel(fields_ref, *refs):
    *inputs, send_ref = refs
    tracers = fields_ref.shape[0]
    surface = [fields_ref[tracer, 0] for tracer in range(tracers)]
    below = [fields_ref[tracer, 1] for tracer in range(tracers)]
    send_surface(surface, below, inputs, send_ref)


def exchange_kernel(
    model_ref, fields_ref, recv_ref, pick_ref, place_ref, mask_ref, north_in, east_in, *refs
):
    *inputs, surface_out, send_ref, north_ref, east_ref = refs
    courant_ref, _, coupling_ref = inputs[:3]
    tracers = fields_ref.shape[0]
    surface = [fields_ref[tracer, 0] for tracer in range(tracers)]
    surface = receive_surface(model_ref, recv_ref, pick_ref, place_ref, surface, coupling_ref, mask_ref)
    below = [fields_ref[tracer, 1] for tracer in range(tracers)]
    send_surface(surface, below, inputs, send_ref)
    zonal, meridional = courant_ref[0], courant_ref[1]
    lane = lane_iota(zonal.shape)
    north_ref[...] = north_in[...]
    for tracer in range(tracers):
        surface_out[tracer] = surface[tracer]
        north_ref[tracer, 0:1, :] = meridional[0:1, :] * surface[tracer][0:1, :]
        east_ref[tracer] = jnp.where(lane == 0, zonal * surface[tracer], east_in[tracer])


def last_kernel(model_ref, fields_ref, recv_ref, pick_ref, place_ref, mask_ref, coupling_ref, fields_out):
    tracers = fields_ref.shape[0]
    surface = [fields_ref[tracer, 0] for tracer in range(tracers)]
    surface = receive_surface(model_ref, recv_ref, pick_ref, place_ref, surface, coupling_ref, mask_ref)
    for tracer in range(tracers):
        fields_out[tracer, 0] = surface[tracer]


VMEM_LIMIT = 32 * 1024 * 1024


def whole(array):
    zeros = (0,) * array.ndim
    return pl.BlockSpec(array.shape, lambda i: zeros)


def top(array, levels):
    tracers, _, rows, cols = array.shape
    return pl.BlockSpec((tracers, levels, rows, cols), lambda i: (0, 0, 0, 0))


SCALAR = pl.BlockSpec(memory_space=pltpu.SMEM)


def call(kernel, operands, specs, out_shape, out_specs, name, aliases=None, flops=0, moved=0):
    return pl.pallas_call(
        kernel,
        grid=(1,),
        in_specs=specs,
        out_shape=out_shape,
        out_specs=out_specs,
        input_output_aliases=aliases or {},
        name=name,
        cost_estimate=pl.CostEstimate(flops=flops, bytes_accessed=moved, transcendentals=0),
        compiler_params=pltpu.CompilerParams(vmem_limit_bytes=VMEM_LIMIT),
    )(*operands)


def like(array):
    return jax.ShapeDtypeStruct(array.shape, array.dtype)


def routing_tables(partner, rows, cols, capacity, main_rows, tracers):
    groups = cols // TILE
    count = rows * groups
    n_lat, n_lon = lax.axis_size("lat"), lax.axis_size("lon")
    devices = n_lat * n_lon
    per_device = main_rows * tracers
    partner = partner.reshape(rows, groups).T.reshape(count)
    own = (jnp.arange(count) % rows) * groups + jnp.arange(count) // rows
    target, slot = partner // count, partner % count
    same = target[:, None] == target[None, :]
    sent = jnp.sum(same & (own[None, :] < own[:, None]), axis=1)
    came = jnp.sum(same & (slot[None, :] < slot[:, None]), axis=1)
    height = devices * per_device
    packs = []
    for tracer in range(tracers):
        index = (sent % groups) * height + target * per_device + tracer * main_rows + sent // groups
        packs.append(jnp.arange(groups * height)[:, None] == index[None, :])
    pack = jnp.concatenate(packs, axis=1).astype(BF16)
    deep = per_device + 2 * tracers
    row, group = slot // groups, slot % groups
    lat, lon = target // n_lon, target % n_lon
    north_ok = (row == rows - 1) & (lat < n_lat - 1)
    east_ok = group == groups - 1
    east_device = lat * n_lon + (lon + 1) % n_lon
    picks = []
    for tracer in range(tracers):
        picks.append(target * deep + tracer * main_rows + came // groups)
    for tracer in range(tracers):
        picks.append(jnp.where(north_ok, (target + n_lon) * deep + per_device + tracer, -1))
    for tracer in range(tracers):
        index = east_device * deep + per_device + tracers + tracer + (row // groups) * (devices * deep)
        picks.append(jnp.where(east_ok, index, -1))
    picks = jnp.concatenate(picks)
    pick = (picks[:, None] == jnp.arange(2 * devices * deep)[None, :]).astype(BF16)
    lane = jnp.arange(cols)[None, :]
    place = jnp.stack(
        [
            lane // TILE == (came % groups)[:, None],
            lane // TILE == group[:, None],
            lane == (row % groups)[:, None] * TILE + TILE - 1,
        ]
    ).astype(F32)
    return pack, pick, place


def local(adjoint, courant, diffusivity, coupling, partner, mask):
    fields = adjoint[0]
    courant, kappa, coupling, partner, mask = courant[0], diffusivity[0], coupling[0], partner[0], mask[0]
    tracers, levels, rows, cols = fields.shape
    groups = cols // TILE
    count = rows * groups
    n_lat, n_lon = lax.axis_size("lat"), lax.axis_size("lon")
    devices = n_lat * n_lon
    capacity = max(2, 2 * count // devices)
    main_rows = -(-capacity // groups)
    deep = main_rows * tracers + 2 * tracers
    model = lax.axis_index("mp").astype(jnp.int32).reshape(1)
    last_row = lax.axis_index("lat") == n_lat - 1

    top_kappa = kappa[0]
    share = jnp.stack([coupling * (1.0 - top_kappa), coupling * top_kappa])
    from_west = lax.ppermute(share, "lon", [(i, (i + 1) % n_lon) for i in range(n_lon)])
    from_south = lax.ppermute(share, "lat", [(i, (i + 1) % n_lat) for i in range(n_lat)])

    def halo(north, east):
        north = lax.ppermute(north, "lat", [((i + 1) % n_lat, i) for i in range(n_lat)])
        east = lax.ppermute(east, "lon", [((i + 1) % n_lon, i) for i in range(n_lon)])
        return jnp.where(last_row, 0.0, north), east

    north_shape = jax.ShapeDtypeStruct((tracers, levels, cols), F32)
    east_shape = jax.ShapeDtypeStruct((tracers, rows, cols), F32)
    send_shape = jax.ShapeDtypeStruct((2 * devices, deep, cols), F32)
    field_bytes = 4 * tracers * levels * rows * cols

    north, east = call(
        edges_kernel,
        (fields, courant),
        [whole(fields), whole(courant)],
        (north_shape, east_shape),
        (whole(north_shape), whole(east_shape)),
        "edges",
        flops=field_bytes,
        moved=field_bytes,
    )
    pack, pick, place = routing_tables(partner, rows, cols, capacity, main_rows, tracers)
    kappa_top = kappa[0:1]
    sending = (courant, kappa_top, coupling, from_west, from_south, pack)
    sending_specs = [whole(a) for a in sending]
    send = call(
        first_send_kernel,
        (fields, *sending),
        [top(fields, 2), *sending_specs],
        send_shape,
        whole(send_shape),
        "first_send",
    )
    surface = fields[:, 0]
    for step in range(STEPS):
        recv = lax.all_to_all(send, ("mp", "lat", "lon"), split_axis=0, concat_axis=0, tiled=True)
        north_in, east_in = halo(north, east)
        mixing = (fields, surface, kappa, courant, north_in, east_in)
        top_shape = jax.ShapeDtypeStruct((tracers, 2, rows, cols), F32)
        shapes = (like(fields), top_shape, north_shape, east_shape)
        fields, two_levels, north, east = call(
            mixing_kernel,
            mixing,
            [whole(a) for a in mixing],
            shapes,
            tuple(whole(a) for a in shapes),
            "mixing",
            flops=10 * field_bytes,
            moved=3 * field_bytes,
        )
        if step + 1 < STEPS:
            arriving = (model, two_levels, recv, pick, place, mask, north, east)
            specs = [SCALAR, *(whole(a) for a in arriving[1:])]
            surface, send, north, east = call(
                exchange_kernel,
                (*arriving, *sending),
                [*specs, *sending_specs],
                (like(surface), send_shape, north_shape, east_shape),
                (whole(surface), whole(send_shape), whole(north_shape), whole(east_shape)),
                "exchange",
            )
        else:
            arriving = (model, fields, recv, pick, place, mask, coupling)
            specs = [SCALAR, top(fields, 1), *(whole(a) for a in arriving[2:])]
            fields = call(
                last_kernel,
                arriving,
                specs,
                like(fields),
                top(fields, 1),
                "last",
                aliases={1: 0},
            )
    return fields[None]


def solution(mesh):
    placed = (
        P("mp", None, None, "lat", "lon"),
        P("mp", None, "lat", "lon"),
        P("mp", None, "lat", "lon"),
        P("mp", "lat", "lon"),
        P("mp", ("lat", "lon")),
        P("mp", "lat", "lon"),
    )
    return jax.shard_map(
        local,
        mesh=mesh,
        in_specs=placed,
        out_specs=P("mp", None, None, "lat", "lon"),
        check_vma=False,
    )
```

```python
import functools

import jax
import jax.numpy as jnp
from jax import lax
from jax.experimental import pallas as pl
from jax.experimental.pallas import tpu as pltpu
from jax.sharding import PartitionSpec as P

TILE = 16
STEPS = 4
F32 = jnp.float32
BF16 = jnp.bfloat16
PACKED = 32


def lane_iota(shape):
    return lax.broadcasted_iota(jnp.int32, shape, len(shape) - 1)


def row_iota(shape):
    return lax.broadcasted_iota(jnp.int32, shape, len(shape) - 2)


def lane_roll(value, shift):
    shift = shift % value.shape[-1]
    return value if shift == 0 else pltpu.roll(value, shift, 1)


def next_row(value):
    return pltpu.roll(value, value.shape[0] - 1, 0)


def three_parts(value):
    high = value.astype(BF16)
    rest = value - high.astype(F32)
    middle = rest.astype(BF16)
    low = (rest - middle.astype(F32)).astype(BF16)
    return high, middle, low


def picked(one_hot, value):
    total = None
    for part in three_parts(value):
        term = jnp.dot(one_hot, part, preferred_element_type=F32)
        total = term if total is None else total + term
    return total


def halo_kernel(after_ref, fields_ref, kappa_ref, courant_ref, rows_ref, columns_ref, corner_ref):
    tracers, levels, rows, cols = fields_ref.shape
    lane = lane_iota((rows, cols))
    upper = row_iota((2 * STEPS, cols)) < STEPS
    pairs = levels // 2

    def first_rows(read, count, start):
        for pair in range(pairs):
            one = read(2 * pair)
            two = read(2 * pair + 1) if 2 * pair + 1 < count else jnp.zeros_like(one)
            rows_ref[start + pair] = jnp.where(upper, one, pltpu.roll(two, STEPS, 0))

    def first_columns(read, count, start):
        for tile in range(-(-levels // PACKED)):
            gathered = jnp.zeros((rows, cols), F32)
            for k in range(tile * PACKED, min((tile + 1) * PACKED, count)):
                place = k % PACKED
                gathered = jnp.where(lane // STEPS == place, lane_roll(read(k), place * STEPS), gathered)
            spot = slice((start + tile) * cols, (start + tile + 1) * cols)
            columns_ref[:, spot] = gathered
            corner_ref[:, spot] = gathered[0 : 2 * STEPS]

    tiles = -(-levels // PACKED)
    for tracer in range(tracers):
        first_rows(lambda k: fields_ref[tracer, k, 0 : 2 * STEPS, :], levels, tracer * pairs)
        first_columns(lambda k: fields_ref[tracer, k], levels, tracer * tiles)
    first_rows(lambda k: kappa_ref[k, 0 : 2 * STEPS, :], levels - 1, tracers * pairs)
    first_columns(lambda k: kappa_ref[k], levels - 1, tracers * tiles)
    rows_ref[(tracers + 1) * pairs] = jnp.where(
        upper,
        courant_ref[0, 0 : 2 * STEPS, :],
        pltpu.roll(courant_ref[1, 0 : 2 * STEPS, :], STEPS, 0),
    )
    for which in range(2):
        repeated = jnp.where(lane < STEPS, courant_ref[which], 0.0)
        shift = STEPS
        while shift < cols:
            repeated = repeated + lane_roll(repeated, shift)
            shift *= 2
        spot = slice(((tracers + 1) * tiles + which) * cols, ((tracers + 1) * tiles + which + 1) * cols)
        columns_ref[:, spot] = repeated
        corner_ref[:, spot] = repeated[0 : 2 * STEPS]


def wide_steps(spot_ref, refs, tracer, levels, tracers, all_levels, first_field, store, each_step):
    kappa_ref, courant_ref, rows_ref, columns_ref, corner_ref, state = refs
    rows, cols = courant_ref.shape[1:]
    pairs = all_levels // 2
    tiles = -(-all_levels // PACKED)
    used = -(-levels // PACKED)
    tall = rows + 2 * STEPS
    has_north = spot_ref[3] > 0
    lane = lane_iota((tall, cols))

    def with_rows(block, start, k):
        extra = rows_ref[start + k // 2]
        if k % 2:
            extra = pltpu.roll(extra, STEPS, 0)
        return jnp.concatenate([block, jnp.where(has_north, extra, 0.0)], axis=0)

    def strip(index):
        spot = slice(index * cols, (index + 1) * cols)
        corner = jnp.where(has_north, corner_ref[:, spot], 0.0)
        return jnp.concatenate([columns_ref[:, spot], corner], axis=0)

    last = rows_ref[(tracers + 1) * pairs]
    last = jnp.where(has_north, last, 0.0)
    zonal = jnp.concatenate([courant_ref[0], last], axis=0)
    meridional = jnp.concatenate([courant_ref[1], pltpu.roll(last, STEPS, 0)], axis=0)
    weight = (1.0 - zonal) - meridional
    side_zonal = strip((tracers + 1) * tiles)
    side_meridional = strip((tracers + 1) * tiles + 1)
    side_weight = (1.0 - side_zonal) - side_meridional
    side = [strip(tracer * tiles + i) for i in range(used)]
    side_kappa = [strip(tracers * tiles + i) for i in range(used)]
    end = (levels - (used - 1) * PACKED) * STEPS
    if levels < all_levels:
        side_kappa[-1] = jnp.where(lane < end, side_kappa[-1], 0.0)

    def lanes_on(tiles_in, shift):
        out = []
        for i, tile in enumerate(tiles_in):
            turned = lane_roll(tile, -shift)
            other = tiles_in[(i + 1 if shift > 0 else i - 1) % len(tiles_in)]
            if len(tiles_in) > 1:
                inside = lane < cols - shift if shift > 0 else lane >= -shift
                turned = jnp.where(inside, turned, lane_roll(other, -shift))
            out.append(turned)
        return out

    for step in range(STEPS):
        height = rows if step == STEPS - 1 else tall
        z, m, w = zonal[:height], meridional[:height], weight[:height]
        at_end = lane[:height] == cols - 1
        side_east = [side_zonal * tile for tile in side]

        def field_of(k):
            if step == 0:
                return with_rows(first_field(k), tracer * pairs, k)
            return state[k]

        def advected(k):
            field = field_of(k)
            edge = lane_roll(side_east[k // PACKED], cols - 1 - (k % PACKED) * STEPS)
            east = jnp.where(at_end, edge[:height], lane_roll((z * field[:height]), cols - 1))
            north = next_row(meridional * field)[:height]
            return (w * field[:height] + east) + north

        here = advected(0)
        above = None
        for k in range(levels):
            result = here
            if k + 1 < levels:
                below = advected(k + 1)
                kappa = kappa_ref[k]
                if height > rows:
                    kappa = with_rows(kappa, tracers * pairs, k)
                flux = kappa * (below - here)
                result = result + flux
            if k > 0:
                result = result - above
            if step == STEPS - 1:
                store(k, result)
            else:
                state[k] = result
            if k + 1 < levels:
                here, above = below, flux
        if step < STEPS - 1:
            east = lanes_on(side_east, 1)
            advected_side = [
                (side_weight * tile + turned) + next_row(side_meridional * tile)
                for tile, turned in zip(side, east)
            ]
            under = lanes_on(advected_side, STEPS)
            fluxes = [kap * (low - adv) for kap, low, adv in zip(side_kappa, under, advected_side)]
            over = lanes_on(fluxes, -STEPS)
            side = [(adv + flux) - up for adv, flux, up in zip(advected_side, fluxes, over)]
            if each_step is not None:
                each_step(step + 1, zonal, meridional, side_zonal, side)


def early_kernel(
    after_ref, spot_ref, fields_ref, kappa_ref, courant_ref, rows_ref, columns_ref, corner_ref,
    values_ref, north_ref, east_ref, state, *, all_levels,
):
    tracers, levels, rows, cols = fields_ref.shape
    refs = (kappa_ref, courant_ref, rows_ref, columns_ref, corner_ref, state)
    for tracer in range(tracers):

        def each_step(step, zonal, meridional, side_zonal, side):
            for j in range(2):
                k = step + j
                field = state[k]
                values_ref[step - 1, tracer, j] = field[:rows]
                line = ((step - 1) * tracers + tracer) * 2 + j
                north_ref[line : line + 1, :] = meridional[rows : rows + 1] * field[rows : rows + 1]
                east_ref[step - 1, tracer, j] = lane_roll(side_zonal * side[0], cols - 1 - k * STEPS)[:rows]

        wide_steps(
            spot_ref, refs, tracer, levels, tracers, all_levels,
            lambda k: fields_ref[tracer, k], lambda k, value: None, each_step,
        )


def deep_kernel(*refs, tracer, tracers):
    _, spot_ref, fields_ref, *rest = refs
    *halo, out_ref, state = rest[-7:] if len(rest) == 7 else rest[1:]
    levels = fields_ref.shape[1]

    def store(k, value):
        if k >= STEPS:
            out_ref[0, k] = value

    for k in range(STEPS):
        out_ref[0, k] = jnp.zeros(out_ref.shape[2:], F32)
    wide_steps(
        spot_ref, (*halo, state), tracer, levels, tracers, levels, lambda k: fields_ref[0, k], store, None
    )


def send_surface(late, below, refs, send_ref, model):
    courant_ref, kappa_ref, coupling_ref, west_ref, south_ref, pack_ref = refs
    tracers = len(late)
    zonal, meridional = courant_ref[0], courant_ref[1]
    weight = (1.0 - zonal) - meridional
    rows, cols = zonal.shape
    groups = cols // TILE
    lane = lane_iota((rows, cols))
    row = row_iota((rows, cols))
    kappa = kappa_ref[0]
    coupling = coupling_ref[...]
    group = lane // TILE
    tiles, edge_north, edge_east = [], [], []
    place = lane == (row % groups) * TILE + (TILE - 1) - row // groups
    west_a = lane_roll(west_ref[0], 1)
    west_b = lane_roll(west_ref[1], 1)
    own_north, own_east = [], jnp.zeros((rows, cols), F32)
    for tracer in range(tracers):
        parts = []
        for field in (late[tracer][0], below[tracer]):
            eastward, northward = zonal * field, meridional * field
            east = jnp.where(lane == cols - 1, 0.0, lane_roll(eastward, cols - 1))
            north = jnp.where(row == rows - 1, 0.0, next_row(northward))
            parts.append((eastward, northward, (weight * field + east) + north))
        (east0, north0, here), (east1, north1, under) = parts
        mixed = here + kappa * (under - here)
        scaled = coupling * mixed
        edge_north.append(
            south_ref[0, rows - 1 : rows, :] * north0[0:1] + south_ref[1, rows - 1 : rows, :] * north1[0:1]
        )
        column = west_a * east0 + west_b * east1
        column = jnp.broadcast_to(column[:, 0:1], (rows, cols))
        edge_east.append(jnp.sum(jnp.where(place, column, 0.0), axis=0, keepdims=True))
        for k, field in enumerate(late[tracer]):
            own_north.append(meridional[0:1] * field[0:1])
            column = jnp.broadcast_to((zonal * field)[:, 0:1], (rows, cols))
            spot = (tracer * len(late[tracer]) + k) * rows + row
            own_east = jnp.where(lane == spot, column, own_east)
        blocks = []
        for c in range(groups):
            block = jnp.where(group == c, scaled, 0.0)
            shift = TILE
            while shift < cols:
                block = block + lane_roll(block, shift)
                shift *= 2
            blocks.append(block)
        tiles.append(jnp.concatenate(blocks, axis=0))
    slots = picked(pack_ref[...], jnp.concatenate(tiles, axis=0))
    height = slots.shape[0] // groups
    slot_group = lane_iota((height, cols)) // TILE
    packed = jnp.zeros((height, cols), F32)
    for g in range(groups):
        packed = jnp.where(slot_group == g, slots[g * height : (g + 1) * height], packed)
    devices = send_ref.shape[0] // 2
    per_device = height // devices
    edges = jnp.concatenate(edge_north + edge_east, axis=0)
    deep = send_ref.shape[1]
    own = own_north + [jnp.zeros((1, cols), F32)] * (deep - 1 - len(own_north))
    own = jnp.concatenate(own + [jnp.sum(own_east, axis=0, keepdims=True)], axis=0)
    used = per_device + 2 * tracers
    for device in range(devices):
        there = (1 - model) * devices + device
        send_ref[there, 0:per_device, :] = packed[device * per_device : (device + 1) * per_device]
        send_ref[there, per_device:used, :] = edges
        if used < deep:
            send_ref[there, used:deep, :] = jnp.zeros((deep - used, cols), F32)
        send_ref[model * devices + device] = own


def receive_surface(model, recv_ref, pick_ref, place_ref, surface, coupling_ref, mask_ref):
    devices = recv_ref.shape[0] // 2
    rows, cols = coupling_ref.shape
    groups = cols // TILE
    tracers = len(surface)
    other = (1 - model) * devices
    slab = recv_ref[pl.ds(other, devices)].reshape(devices * recv_ref.shape[1], cols)
    table = jnp.concatenate([slab, lane_roll(slab, 1)], axis=0)
    found = picked(pick_ref[...], table)
    count = rows * groups
    group = lane_iota((rows, cols)) // TILE
    wet = mask_ref[...].astype(F32)
    coupling = coupling_ref[...]
    updated = []
    for tracer in range(tracers):
        total = None
        for kind in range(3):
            start = (kind * tracers + tracer) * count
            term = jnp.where(place_ref[kind] > 0, found[start : start + count], 0.0)
            total = term if total is None else total + term
        shift = TILE
        while shift < cols:
            total = total + lane_roll(total, shift)
            shift *= 2
        received = jnp.zeros((rows, cols), F32)
        for c in range(groups):
            received = jnp.where(group == c, total[c * rows : (c + 1) * rows], received)
        own = surface[tracer]
        updated.append(own + wet * (received - coupling * own))
    return updated


def upper_levels(spot_ref, recv_ref, late, early, refs):
    courant_ref, kappa_ref = refs
    zonal, meridional = courant_ref[0], courant_ref[1]
    weight = (1.0 - zonal) - meridional
    rows, cols = zonal.shape
    lane = lane_iota((rows, cols))
    row = row_iota((rows, cols))
    devices = recv_ref.shape[0] // 2
    mine = spot_ref[0] * devices
    from_east = recv_ref[mine + spot_ref[1]]
    from_north = jnp.where(spot_ref[3] > 0, recv_ref[mine + spot_ref[2]], 0.0)
    east_line = jnp.broadcast_to(from_east[from_east.shape[0] - 1 :], (rows, cols))
    stepped = []
    for tracer in range(len(late)):
        count = len(late[tracer])
        moved = []
        for k in range(count + len(early[tracer])):
            if k < count:
                field = late[tracer][k]
                index = tracer * count + k
                north_edge = from_north[index : index + 1]
                column = jnp.where(lane == index * rows + row, east_line, 0.0)
                east_edge = jnp.sum(column, axis=1, keepdims=True)
            else:
                field, north_edge, east_edge = early[tracer][k - count]
            east = jnp.where(lane == cols - 1, east_edge, lane_roll(zonal * field, cols - 1))
            north = jnp.where(row == rows - 1, north_edge, next_row(meridional * field))
            moved.append((weight * field + east) + north)
        out, above = [], None
        for k in range(len(moved) - 1):
            flux = kappa_ref[k] * (moved[k + 1] - moved[k])
            result = moved[k] + flux
            if k > 0:
                result = result - above
            out.append(result)
            above = flux
        stepped.append(out)
    return stepped


def early_levels(step, early_refs, tracer, tracers):
    if early_refs is None:
        return []
    values_ref, north_ref, east_ref = early_refs
    found = []
    for j in range(2):
        line = ((step - 1) * tracers + tracer) * 2 + j
        found.append((values_ref[step - 1, tracer, j], north_ref[line : line + 1, :], east_ref[step - 1, tracer, j]))
    return found


def first_send_kernel(spot_ref, fields_ref, *refs):
    *inputs, send_ref = refs
    tracers, levels = fields_ref.shape[:2]
    late = [[fields_ref[tracer, k] for k in range(levels)] for tracer in range(tracers)]
    send_surface(late, [values[1] for values in late], inputs, send_ref, spot_ref[0])


def exchange_kernel(spot_ref, late_ref, recv_ref, pick_ref, place_ref, mask_ref, *refs, step, last):
    early_refs, refs = (refs[:3], refs[3:]) if step > 0 else (None, refs)
    if last:
        *inputs, out_ref = refs
    else:
        *inputs, late_out, send_ref = refs
    courant_ref, kappa_ref, coupling_ref = inputs[:3]
    tracers = late_ref.shape[0]
    late = [[late_ref[tracer, k] for k in range(late_ref.shape[1])] for tracer in range(tracers)]
    early = [early_levels(step, early_refs, tracer, tracers) for tracer in range(tracers)]
    stepped = upper_levels(spot_ref, recv_ref, late, early, (courant_ref, kappa_ref))
    surface = [values[0] for values in stepped]
    surface = receive_surface(spot_ref[0], recv_ref, pick_ref, place_ref, surface, coupling_ref, mask_ref)
    for tracer in range(tracers):
        stepped[tracer][0] = surface[tracer]
    if last:
        for tracer in range(tracers):
            for k in range(STEPS):
                out_ref[tracer, k] = stepped[tracer][k]
        return
    kept = late_out.shape[1]
    for tracer in range(tracers):
        for k in range(kept):
            late_out[tracer, k] = stepped[tracer][k]
    send_surface(
        [values[:kept] for values in stepped], [values[1] for values in stepped], inputs, send_ref, spot_ref[0]
    )


VMEM_LIMIT = 32 * 1024 * 1024


def whole(array):
    zeros = (0,) * array.ndim
    return pl.BlockSpec(array.shape, lambda i: zeros)


def top(array, levels):
    tracers, _, rows, cols = array.shape
    return pl.BlockSpec((tracers, levels, rows, cols), lambda i: (0, 0, 0, 0))


SCALAR = pl.BlockSpec(memory_space=pltpu.SMEM)
UNREAD = pl.BlockSpec(memory_space=pl.ANY)


def call(kernel, operands, specs, out_shape, out_specs, name, aliases=None, scratch=(), flops=0, moved=0):
    return pl.pallas_call(
        kernel,
        grid=(1,),
        in_specs=specs,
        out_shape=out_shape,
        out_specs=out_specs,
        scratch_shapes=list(scratch),
        input_output_aliases=aliases or {},
        name=name,
        cost_estimate=pl.CostEstimate(flops=flops, bytes_accessed=moved, transcendentals=0),
        compiler_params=pltpu.CompilerParams(vmem_limit_bytes=VMEM_LIMIT),
    )(*operands)


def shaped(*shape):
    return jax.ShapeDtypeStruct(shape, F32)


def tile_order(partner, rows, groups):
    count = rows * groups
    a = lax.broadcasted_iota(jnp.int32, (count, count), 0)
    b = lax.broadcasted_iota(jnp.int32, (count, count), 1)
    turn = (a == (b % rows) * groups + b // rows).astype(BF16)
    both = jnp.concatenate([partner // count, partner % count], axis=0)
    both = jnp.concatenate([both, jnp.zeros((6, count), jnp.int32)], axis=0).astype(F32).astype(BF16)
    lines = jnp.dot(both, turn, preferred_element_type=F32)
    columns = lax.dot_general(turn, both, (((0,), (1,)), ((), ())), preferred_element_type=F32)
    lines, columns = lines.astype(jnp.int32), columns.astype(jnp.int32)
    return lines[0:1], lines[1:2], columns[:, 0:1], columns[:, 1:2]


def pack_kernel(partner_ref, pack_ref, *, rows, groups, main_rows, tracers):
    count = rows * groups
    line_target, _, column_target, _ = tile_order(partner_ref[...], rows, groups)
    a = lax.broadcasted_iota(jnp.int32, (count, count), 0)
    b = lax.broadcasted_iota(jnp.int32, (count, count), 1)
    place_a = (a % rows) * groups + a // rows
    place_b = (b % rows) * groups + b // rows
    ahead = (column_target == line_target) & (place_a < place_b)
    sent = jnp.sum(ahead.astype(F32), axis=0, keepdims=True).astype(jnp.int32)
    height = pack_ref.shape[0] // groups
    per_device = main_rows * tracers
    slot = lax.broadcasted_iota(jnp.int32, (pack_ref.shape[0], count), 0)
    for tracer in range(tracers):
        index = (sent % groups) * height + line_target * per_device + tracer * main_rows + sent // groups
        pack_ref[:, tracer * count : (tracer + 1) * count] = (slot == index).astype(F32).astype(BF16)


def pick_kernel(
    after_ref, partner_ref, pick_ref, place_ref, *, rows, groups, main_rows, tracers, n_lat, n_lon, deep
):
    count = rows * groups
    per_device = main_rows * tracers
    devices = n_lat * n_lon
    line_target, line_slot, target, slot = tile_order(partner_ref[...], rows, groups)
    ahead = (target == line_target) & (line_slot < slot)
    came = jnp.sum(ahead.astype(F32), axis=1, keepdims=True).astype(jnp.int32)
    row, group = slot // groups, slot % groups
    lat, lon = target // n_lon, target % n_lon
    north_ok = (row == rows - 1) & (lat < n_lat - 1)
    east_ok = group == groups - 1
    east_device = lat * n_lon + (lon + 1) % n_lon
    index = lax.broadcasted_iota(jnp.int32, (count, pick_ref.shape[1]), 1)
    for tracer in range(tracers):
        picks = (
            target * deep + tracer * main_rows + came // groups,
            jnp.where(north_ok, (target + n_lon) * deep + per_device + tracer, -1),
            jnp.where(
                east_ok,
                east_device * deep + per_device + tracers + tracer + (row // groups) * (devices * deep),
                -1,
            ),
        )
        for kind, pick in enumerate(picks):
            start = (kind * tracers + tracer) * count
            pick_ref[start : start + count, :] = (pick == index).astype(F32).astype(BF16)
    lane = lax.broadcasted_iota(jnp.int32, (count, groups * TILE), 1)
    place_ref[0] = (lane // TILE == came % groups).astype(F32)
    place_ref[1] = (lane // TILE == group).astype(F32)
    place_ref[2] = (lane == (row % groups) * TILE + TILE - 1).astype(F32)


def local(adjoint, courant, diffusivity, coupling, partner, mask):
    fields = adjoint[0]
    courant, kappa, coupling, mask = courant[0], diffusivity[0], coupling[0], mask[0]
    tracers, levels, rows, cols = fields.shape
    groups = cols // TILE
    count = rows * groups
    n_lat, n_lon = lax.axis_size("lat"), lax.axis_size("lon")
    devices = n_lat * n_lon
    capacity = max(2, 2 * count // devices)
    main_rows = -(-capacity // groups)
    deep = max(8, main_rows * tracers + 2 * tracers)
    lat, lon = lax.axis_index("lat"), lax.axis_index("lon")
    spot = jnp.stack(
        [
            lax.axis_index("mp"),
            lat * n_lon + (lon + 1) % n_lon,
            ((lat + 1) % n_lat) * n_lon + lon,
            (lat < n_lat - 1).astype(jnp.int32),
        ]
    ).astype(jnp.int32)

    share = jnp.stack([coupling * (1.0 - kappa[0]), coupling * kappa[0]])
    from_west = lax.ppermute(share, "lon", [(i, (i + 1) % n_lon) for i in range(n_lon)])
    from_south = lax.ppermute(share, "lat", [(i, (i + 1) % n_lat) for i in range(n_lat)])

    sizes = dict(rows=rows, groups=groups, main_rows=main_rows, tracers=tracers)
    per_device = main_rows * tracers
    pack_shape = jax.ShapeDtypeStruct((groups * devices * per_device, tracers * count), BF16)
    pack = call(
        functools.partial(pack_kernel, **sizes),
        (partner,),
        [whole(partner)],
        pack_shape,
        whole(pack_shape),
        "pack_table",
    )
    upper = kappa[:STEPS]
    sending = (courant, upper, coupling, from_west, from_south, pack)
    sending_specs = [whole(a) for a in sending]
    send_shape = shaped(2 * devices, deep, cols)
    send = call(
        first_send_kernel,
        (spot, fields, *sending),
        [SCALAR, top(fields, 3), *sending_specs],
        send_shape,
        whole(send_shape),
        "first_send",
    )
    recv = lax.all_to_all(send, ("mp", "lat", "lon"), split_axis=0, concat_axis=0, tiled=True)

    pick_shape = jax.ShapeDtypeStruct((3 * tracers * count, 2 * devices * deep), BF16)
    place_shape = shaped(3, count, cols)
    pick, place = call(
        functools.partial(pick_kernel, n_lat=n_lat, n_lon=n_lon, deep=deep, **sizes),
        (send, partner),
        [UNREAD, whole(partner)],
        (pick_shape, place_shape),
        (whole(pick_shape), whole(place_shape)),
        "pick_table",
    )
    tiles = -(-levels // PACKED)
    width = ((tracers + 1) * tiles + 2) * cols
    halo_shapes = (
        shaped((tracers + 1) * (levels // 2) + 1, 2 * STEPS, cols),
        shaped(rows, width),
        shaped(2 * STEPS, width),
    )
    north, east, corner = call(
        halo_kernel,
        (send, fields, kappa, courant),
        [UNREAD, *(whole(a) for a in (fields, kappa, courant))],
        halo_shapes,
        tuple(whole(a) for a in halo_shapes),
        "halo",
        moved=4 * fields.size,
    )
    north = lax.ppermute(north, "lat", [((i + 1) % n_lat, i) for i in range(n_lat)])
    east = lax.ppermute(east, "lon", [((i + 1) % n_lon, i) for i in range(n_lon)])
    corner = lax.ppermute(
        corner,
        ("lat", "lon"),
        [
            (((i + 1) % n_lat) * n_lon + (j + 1) % n_lon, i * n_lon + j)
            for i in range(n_lat)
            for j in range(n_lon)
        ],
    )
    halo = (courant, north, east, corner)
    halo_specs = [whole(a) for a in halo]
    field_bytes = 4 * fields.size
    tall = rows + 2 * STEPS

    late, early, out = fields, (), None
    for step in range(STEPS):
        if step > 0:
            recv = lax.all_to_all(send, ("mp", "lat", "lon"), split_axis=0, concat_axis=0, tiled=True)
        if step == 1:
            shown = 2 * STEPS
            early_shapes = (
                shaped(STEPS - 1, tracers, 2, rows, cols),
                shaped(-(-(STEPS - 1) * tracers * 2 // 8) * 8, cols),
                shaped(STEPS - 1, tracers, 2, rows, cols),
            )
            early = call(
                functools.partial(early_kernel, all_levels=levels),
                (send, spot, fields, kappa, *halo),
                [
                    UNREAD,
                    SCALAR,
                    top(fields, shown),
                    pl.BlockSpec((shown, rows, cols), lambda i: (0, 0, 0)),
                    *halo_specs,
                ],
                early_shapes,
                tuple(whole(a) for a in early_shapes),
                "early_levels",
                scratch=[pltpu.VMEM((shown, tall, cols), F32)],
                flops=field_bytes,
                moved=field_bytes,
            )
        if step > 1:
            for tracer in range(step - 2, tracers if step == STEPS - 1 else step - 1):
                before = () if out is None else (out,)
                block = pl.BlockSpec((1, levels, rows, cols), lambda i, tracer=tracer: (tracer, 0, 0, 0))
                out = call(
                    functools.partial(deep_kernel, tracer=tracer, tracers=tracers),
                    (send, spot, fields, *before, kappa, *halo),
                    [UNREAD, SCALAR, block, *(UNREAD for _ in before), whole(kappa), *halo_specs],
                    shaped(*fields.shape),
                    block,
                    "deep_levels",
                    aliases={3: 0} if before else None,
                    scratch=[pltpu.VMEM((levels, tall, cols), F32)],
                    flops=10 * field_bytes,
                    moved=field_bytes,
                )
        last = step == STEPS - 1
        kept = step + 1
        arriving = (spot, late, recv, pick, place, mask, *early)
        late_spec = top(late, 3) if step == 0 else whole(late)
        specs = [SCALAR, late_spec, *(whole(a) for a in arriving[2:])]
        kernel = functools.partial(exchange_kernel, step=step, last=last)
        if last:
            operands = (*arriving, *sending[:3], out)
            fields = call(
                lambda *refs: kernel(*refs[:-2], refs[-1]),
                operands,
                [*specs, *sending_specs[:3], UNREAD],
                shaped(*fields.shape),
                top(fields, STEPS),
                "last_exchange",
                aliases={len(operands) - 1: 0},
            )
        else:
            late_shape = shaped(tracers, kept, rows, cols)
            late, send = call(
                kernel,
                (*arriving, *sending),
                [*specs, *sending_specs],
                (late_shape, send_shape),
                (whole(late_shape), whole(send_shape)),
                "exchange",
            )
    return fields[None]


def solution(mesh):
    placed = (
        P("mp", None, None, "lat", "lon"),
        P("mp", None, "lat", "lon"),
        P("mp", None, "lat", "lon"),
        P("mp", "lat", "lon"),
        P("mp", ("lat", "lon")),
        P("mp", "lat", "lon"),
    )
    return jax.shard_map(
        local,
        mesh=mesh,
        in_specs=placed,
        out_specs=P("mp", None, None, "lat", "lon"),
        check_vma=False,
    )
```

```python
import functools

import jax
import jax.numpy as jnp
from jax import lax
from jax.experimental import pallas as pl
from jax.experimental.pallas import tpu as pltpu
from jax.sharding import PartitionSpec as P

TILE = 16
STEPS = 4
F32 = jnp.float32
BF16 = jnp.bfloat16
PACKED = 32
SLAB = 4
ZONAL, MERIDIONAL, KAPPA = 0, 1, 2
COUPLING = KAPPA + STEPS
WEST = COUPLING + 1
SOUTH = WEST + 2
WET = SOUTH + 2
PLACE = WET + 1


def lane_iota(shape):
    return lax.broadcasted_iota(jnp.int32, shape, len(shape) - 1)


def row_iota(shape):
    return lax.broadcasted_iota(jnp.int32, shape, len(shape) - 2)


def lane_roll(value, shift):
    shift = shift % value.shape[-1]
    return value if shift == 0 else pltpu.roll(value, shift, 1)


def next_row(value):
    return pltpu.roll(value, value.shape[0] - 1, 0)


def three_parts(value):
    high = value.astype(BF16)
    rest = value - high.astype(F32)
    middle = rest.astype(BF16)
    low = (rest - middle.astype(F32)).astype(BF16)
    return high, middle, low


def picked(one_hot, value):
    total = None
    for part in three_parts(value):
        term = jnp.dot(one_hot, part, preferred_element_type=F32)
        total = term if total is None else total + term
    return total


def halo_kernel(after_ref, fields_ref, kappa_ref, courant_ref, rows_ref, columns_ref, corner_ref):
    tracers, levels, rows, cols = fields_ref.shape
    lane = lane_iota((rows, cols))
    upper = row_iota((2 * STEPS, cols)) < STEPS
    pairs = levels // 2

    def first_rows(read, count, start):
        for pair in range(pairs):
            one = read(2 * pair)
            two = read(2 * pair + 1) if 2 * pair + 1 < count else jnp.zeros_like(one)
            rows_ref[start + pair] = jnp.where(upper, one, pltpu.roll(two, STEPS, 0))

    def first_columns(read, count, start):
        for tile in range(-(-levels // PACKED)):
            gathered = jnp.zeros((rows, cols), F32)
            for k in range(tile * PACKED, min((tile + 1) * PACKED, count)):
                place = k % PACKED
                gathered = jnp.where(lane // STEPS == place, lane_roll(read(k), place * STEPS), gathered)
            spot = slice((start + tile) * cols, (start + tile + 1) * cols)
            columns_ref[:, spot] = gathered
            corner_ref[:, spot] = gathered[0 : 2 * STEPS]

    tiles = -(-levels // PACKED)
    for tracer in range(tracers):
        first_rows(lambda k: fields_ref[tracer, k, 0 : 2 * STEPS, :], levels, tracer * pairs)
        first_columns(lambda k: fields_ref[tracer, k], levels, tracer * tiles)
    first_rows(lambda k: kappa_ref[k, 0 : 2 * STEPS, :], levels - 1, tracers * pairs)
    first_columns(lambda k: kappa_ref[k], levels - 1, tracers * tiles)
    rows_ref[(tracers + 1) * pairs] = jnp.where(
        upper,
        courant_ref[0, 0 : 2 * STEPS, :],
        pltpu.roll(courant_ref[1, 0 : 2 * STEPS, :], STEPS, 0),
    )
    for which in range(2):
        repeated = jnp.where(lane < STEPS, courant_ref[which], 0.0)
        shift = STEPS
        while shift < cols:
            repeated = repeated + lane_roll(repeated, shift)
            shift *= 2
        spot = slice(((tracers + 1) * tiles + which) * cols, ((tracers + 1) * tiles + which + 1) * cols)
        columns_ref[:, spot] = repeated
        corner_ref[:, spot] = repeated[0 : 2 * STEPS]


def wide_steps(spot_ref, refs, tracer, levels, tracers, all_levels, first_field, store, each_step):
    kappa_ref, courant_ref, rows_ref, columns_ref, corner_ref, state = refs
    rows, cols = courant_ref.shape[1:]
    pairs = all_levels // 2
    tiles = -(-all_levels // PACKED)
    used = -(-levels // PACKED)
    tall = rows + 2 * STEPS
    has_north = spot_ref[3] > 0
    lane = lane_iota((tall, cols))

    def with_rows(block, start, k):
        extra = rows_ref[start + k // 2]
        if k % 2:
            extra = pltpu.roll(extra, STEPS, 0)
        return jnp.concatenate([block, jnp.where(has_north, extra, 0.0)], axis=0)

    def strip(index):
        spot = slice(index * cols, (index + 1) * cols)
        corner = jnp.where(has_north, corner_ref[:, spot], 0.0)
        return jnp.concatenate([columns_ref[:, spot], corner], axis=0)

    last = rows_ref[(tracers + 1) * pairs]
    last = jnp.where(has_north, last, 0.0)
    zonal = jnp.concatenate([courant_ref[0], last], axis=0)
    meridional = jnp.concatenate([courant_ref[1], pltpu.roll(last, STEPS, 0)], axis=0)
    weight = (1.0 - zonal) - meridional
    side_zonal = strip((tracers + 1) * tiles)
    side_meridional = strip((tracers + 1) * tiles + 1)
    side_weight = (1.0 - side_zonal) - side_meridional
    side = [strip(tracer * tiles + i) for i in range(used)]
    side_kappa = [strip(tracers * tiles + i) for i in range(used)]
    end = (levels - (used - 1) * PACKED) * STEPS
    if levels < all_levels:
        side_kappa[-1] = jnp.where(lane < end, side_kappa[-1], 0.0)

    def lanes_on(tiles_in, shift):
        out = []
        for i, tile in enumerate(tiles_in):
            turned = lane_roll(tile, -shift)
            other = tiles_in[(i + 1 if shift > 0 else i - 1) % len(tiles_in)]
            if len(tiles_in) > 1:
                inside = lane < cols - shift if shift > 0 else lane >= -shift
                turned = jnp.where(inside, turned, lane_roll(other, -shift))
            out.append(turned)
        return out

    for step in range(STEPS):
        height = rows if step == STEPS - 1 else tall
        z, m, w = zonal[:height], meridional[:height], weight[:height]
        at_end = lane[:height] == cols - 1
        side_east = [side_zonal * tile for tile in side]

        def field_of(k):
            if step == 0:
                return with_rows(first_field(k), tracer * pairs, k)
            return state[k]

        def advected(k):
            field = field_of(k)
            edge = lane_roll(side_east[k // PACKED], cols - 1 - (k % PACKED) * STEPS)
            east = jnp.where(at_end, edge[:height], lane_roll((z * field[:height]), cols - 1))
            north = next_row(meridional * field)[:height]
            return (w * field[:height] + east) + north

        here = advected(0)
        above = None
        for k in range(levels):
            result = here
            if k + 1 < levels:
                below = advected(k + 1)
                kappa = kappa_ref[k]
                if height > rows:
                    kappa = with_rows(kappa, tracers * pairs, k)
                flux = kappa * (below - here)
                result = result + flux
            if k > 0:
                result = result - above
            if step == STEPS - 1:
                store(k, result)
            else:
                state[k] = result
            if k + 1 < levels:
                here, above = below, flux
        if step < STEPS - 1:
            east = lanes_on(side_east, 1)
            advected_side = [
                (side_weight * tile + turned) + next_row(side_meridional * tile)
                for tile, turned in zip(side, east)
            ]
            under = lanes_on(advected_side, STEPS)
            fluxes = [kap * (low - adv) for kap, low, adv in zip(side_kappa, under, advected_side)]
            over = lanes_on(fluxes, -STEPS)
            side = [(adv + flux) - up for adv, flux, up in zip(advected_side, fluxes, over)]
            if each_step is not None:
                each_step(step + 1, zonal, meridional, side_zonal, side)


def early_kernel(
    after_ref, spot_ref, fields_ref, kappa_ref, courant_ref, rows_ref, columns_ref, corner_ref,
    early_ref, state, *, all_levels,
):
    tracers, levels, rows, cols = fields_ref.shape
    refs = (kappa_ref, courant_ref, rows_ref, columns_ref, corner_ref, state)
    for tracer in range(tracers):

        def each_step(step, zonal, meridional, side_zonal, side):
            for j in range(2):
                k = step + j
                field = state[k]
                line = ((step - 1) * tracers + tracer) * 2 + j
                early_ref[2 * line] = field[:rows]
                early_ref[2 * line + 1] = lane_roll(side_zonal * side[0], cols - 1 - k * STEPS)[:rows]
                early_ref[early_ref.shape[0] - 1, line : line + 1, :] = (
                    meridional[rows : rows + 1] * field[rows : rows + 1]
                )

        wide_steps(
            spot_ref, refs, tracer, levels, tracers, all_levels,
            lambda k: fields_ref[tracer, k], lambda k, value: None, each_step,
        )


def deep_kernel(*refs, tracer, tracers):
    _, spot_ref, fields_ref, *rest = refs
    *halo, out_ref, state = rest[-7:] if len(rest) == 7 else rest[1:]
    levels = fields_ref.shape[1]

    def store(k, value):
        if k >= STEPS:
            out_ref[0, k] = value

    for k in range(STEPS):
        out_ref[0, k] = jnp.zeros(out_ref.shape[2:], F32)
    wide_steps(
        spot_ref, (*halo, state), tracer, levels, tracers, levels, lambda k: fields_ref[0, k], store, None
    )


def send_surface(late, below, static_ref, table_ref, send_ref, model, deep_rows):
    tracers = len(late)
    zonal, meridional = static_ref[ZONAL], static_ref[MERIDIONAL]
    weight = (1.0 - zonal) - meridional
    rows, cols = zonal.shape
    groups = cols // TILE
    lane = lane_iota((rows, cols))
    row = row_iota((rows, cols))
    kappa = static_ref[KAPPA]
    coupling = static_ref[COUPLING]
    group = lane // TILE
    tiles, edge_north, edge_east = [], [], []
    place = lane == (row % groups) * TILE + (TILE - 1) - row // groups
    west_a = lane_roll(static_ref[WEST], 1)
    west_b = lane_roll(static_ref[WEST + 1], 1)
    south_a, south_b = static_ref[SOUTH], static_ref[SOUTH + 1]
    own_north, own_east = [], jnp.zeros((rows, cols), F32)
    for tracer in range(tracers):
        parts = []
        for field in (late[tracer][0], below[tracer]):
            eastward, northward = zonal * field, meridional * field
            east = jnp.where(lane == cols - 1, 0.0, lane_roll(eastward, cols - 1))
            north = jnp.where(row == rows - 1, 0.0, next_row(northward))
            parts.append((eastward, northward, (weight * field + east) + north))
        (east0, north0, here), (east1, north1, under) = parts
        mixed = here + kappa * (under - here)
        scaled = coupling * mixed
        edge_north.append(south_a[rows - 1 : rows] * north0[0:1] + south_b[rows - 1 : rows] * north1[0:1])
        column = west_a * east0 + west_b * east1
        column = jnp.broadcast_to(column[:, 0:1], (rows, cols))
        edge_east.append(jnp.sum(jnp.where(place, column, 0.0), axis=0, keepdims=True))
        for k, field in enumerate(late[tracer]):
            own_north.append(meridional[0:1] * field[0:1])
            column = jnp.broadcast_to((zonal * field)[:, 0:1], (rows, cols))
            spot = (tracer * len(late[tracer]) + k) * rows + row
            own_east = jnp.where(lane == spot, column, own_east)
        blocks = []
        for c in range(groups):
            block = jnp.where(group == c, scaled, 0.0)
            shift = TILE
            while shift < cols:
                block = block + lane_roll(block, shift)
                shift *= 2
            blocks.append(block)
        tiles.append(jnp.concatenate(blocks, axis=0))
    devices = send_ref.shape[0] // 2
    height = devices * SLAB
    slots = picked(table_ref[deep_rows : deep_rows + groups * height, 0 : rows * groups], jnp.concatenate(tiles, axis=1))
    slot_group = (lane_iota((height, tracers * cols)) % cols) // TILE
    packed = jnp.zeros((height, tracers * cols), F32)
    for g in range(groups):
        packed = jnp.where(slot_group == g, slots[g * height : (g + 1) * height], packed)
    first, second = packed[:, :cols], packed[:, cols:]
    upper = row_iota((2 * SLAB, cols)) < SLAB
    empty = jnp.zeros((SLAB - 2, cols), F32)
    edges = jnp.concatenate(
        [empty, edge_north[0], edge_east[0], empty, edge_north[1], edge_east[1]], axis=0
    )
    own = own_north + [jnp.zeros((1, cols), F32)] * (2 * SLAB - 1 - len(own_north))
    own = jnp.concatenate(own + [jnp.sum(own_east, axis=0, keepdims=True)], axis=0)
    for pair in range(devices // 2):
        one, two = (half[pair * 2 * SLAB : (pair + 1) * 2 * SLAB] for half in (first, second))
        there = (1 - model) * devices + 2 * pair
        send_ref[there] = jnp.where(upper, one, pltpu.roll(two, SLAB, 0)) + edges
        send_ref[there + 1] = jnp.where(upper, pltpu.roll(one, SLAB, 0), two) + edges
        send_ref[model * devices + 2 * pair] = own
        send_ref[model * devices + 2 * pair + 1] = own


def receive_surface(model, recv_ref, table_ref, static_ref, surface):
    devices = recv_ref.shape[0] // 2
    rows, cols = surface[0].shape
    groups = cols // TILE
    tracers = len(surface)
    count = rows * groups
    other = (1 - model) * devices
    upper = row_iota((2 * SLAB, cols)) < SLAB
    first, second = [], []
    for pair in range(devices // 2):
        one, two = recv_ref[other + 2 * pair], recv_ref[other + 2 * pair + 1]
        first.append(jnp.where(upper, one, pltpu.roll(two, SLAB, 0)))
        second.append(jnp.where(upper, pltpu.roll(one, SLAB, 0), two))
    halves = [jnp.concatenate(half, axis=0) for half in (first, second)]
    slab = jnp.concatenate(halves, axis=1)
    shifted = jnp.concatenate([lane_roll(half, 1) for half in halves], axis=1)
    found = picked(table_ref[0 : 3 * count], jnp.concatenate([slab, shifted], axis=0))
    group = lane_iota((rows, cols)) // TILE
    wet, coupling = static_ref[WET], static_ref[COUPLING]
    updated = []
    for tracer in range(tracers):
        received = jnp.zeros((rows, cols), F32)
        for c in range(groups):
            total = None
            for kind in range(3):
                start = kind * count + c * rows
                place = static_ref[PLACE + kind * groups + c]
                term = jnp.where(
                    place > 0, found[start : start + rows, tracer * cols : (tracer + 1) * cols], 0.0
                )
                total = term if total is None else total + term
            shift = TILE
            while shift < cols:
                total = total + lane_roll(total, shift)
                shift *= 2
            received = jnp.where(group == c, total, received)
        own = surface[tracer]
        updated.append(own + wet * (received - coupling * own))
    return updated


def upper_levels(spot_ref, recv_ref, late, early, static_ref):
    zonal, meridional = static_ref[ZONAL], static_ref[MERIDIONAL]
    weight = (1.0 - zonal) - meridional
    rows, cols = zonal.shape
    lane = lane_iota((rows, cols))
    row = row_iota((rows, cols))
    devices = recv_ref.shape[0] // 2
    mine = spot_ref[0] * devices
    from_east = recv_ref[mine + spot_ref[1]]
    from_north = jnp.where(spot_ref[3] > 0, recv_ref[mine + spot_ref[2]], 0.0)
    east_line = jnp.broadcast_to(from_east[from_east.shape[0] - 1 :], (rows, cols))
    stepped = []
    for tracer in range(len(late)):
        count = len(late[tracer])
        moved = []
        for k in range(count + len(early[tracer])):
            if k < count:
                field = late[tracer][k]
                index = tracer * count + k
                north_edge = from_north[index : index + 1]
                column = jnp.where(lane == index * rows + row, east_line, 0.0)
                east_edge = jnp.sum(column, axis=1, keepdims=True)
            else:
                field, north_edge, east_edge = early[tracer][k - count]
            east = jnp.where(lane == cols - 1, east_edge, lane_roll(zonal * field, cols - 1))
            north = jnp.where(row == rows - 1, north_edge, next_row(meridional * field))
            moved.append((weight * field + east) + north)
        out, above = [], None
        for k in range(len(moved) - 1):
            flux = static_ref[KAPPA + k] * (moved[k + 1] - moved[k])
            result = moved[k] + flux
            if k > 0:
                result = result - above
            out.append(result)
            above = flux
        stepped.append(out)
    return stepped


def early_levels(step, early_ref, tracer, tracers):
    if step == 0:
        return []
    found = []
    for j in range(2):
        line = ((step - 1) * tracers + tracer) * 2 + j
        norths = early_ref[early_ref.shape[0] - 1]
        found.append((early_ref[2 * line], norths[line : line + 1], early_ref[2 * line + 1]))
    return found


def first_send_kernel(spot_ref, fields_ref, static_ref, table_ref, send_ref, *, deep_rows):
    tracers, levels = fields_ref.shape[:2]
    late = [[fields_ref[tracer, k] for k in range(levels)] for tracer in range(tracers)]
    send_surface(late, [values[1] for values in late], static_ref, table_ref, send_ref, spot_ref[0], deep_rows)


def exchange_kernel(spot_ref, late_ref, recv_ref, static_ref, table_ref, *refs, step, deep_rows, unread):
    early_ref, refs = (refs[0], refs[1:]) if step > 0 else (None, refs)
    refs = refs[unread:]
    tracers = late_ref.shape[0]
    late = [[late_ref[tracer, k] for k in range(late_ref.shape[1])] for tracer in range(tracers)]
    early = [early_levels(step, early_ref, tracer, tracers) for tracer in range(tracers)]
    stepped = upper_levels(spot_ref, recv_ref, late, early, static_ref)
    surface = [values[0] for values in stepped]
    surface = receive_surface(spot_ref[0], recv_ref, table_ref, static_ref, surface)
    for tracer in range(tracers):
        stepped[tracer][0] = surface[tracer]
    if step == STEPS - 1:
        (out_ref,) = refs
        for tracer in range(tracers):
            for k in range(STEPS):
                out_ref[tracer, k] = stepped[tracer][k]
        return
    late_out, send_ref = refs
    kept = late_out.shape[1]
    for tracer in range(tracers):
        for k in range(kept):
            late_out[tracer, k] = stepped[tracer][k]
    send_surface(
        [values[:kept] for values in stepped],
        [values[1] for values in stepped],
        static_ref,
        table_ref,
        send_ref,
        spot_ref[0],
        deep_rows,
    )


def whole(array):
    zeros = (0,) * array.ndim
    return pl.BlockSpec(array.shape, lambda i: zeros)


def top(array, levels):
    tracers, _, rows, cols = array.shape
    return pl.BlockSpec((tracers, levels, rows, cols), lambda i: (0, 0, 0, 0))


SCALAR = pl.BlockSpec(memory_space=pltpu.SMEM)
NEAR = pl.BlockSpec(memory_space=pltpu.VMEM)
UNREAD = pl.BlockSpec(memory_space=pl.ANY)


def call(kernel, operands, specs, out_shape, out_specs, name, grid=(), aliases=None, scratch=(), us=1):
    return pl.pallas_call(
        kernel,
        grid=grid,
        in_specs=specs,
        out_shape=out_shape,
        out_specs=out_specs,
        scratch_shapes=list(scratch),
        input_output_aliases=aliases or {},
        name=name,
        cost_estimate=pl.CostEstimate(flops=0, bytes_accessed=us * 3_000_000, transcendentals=0),
        compiler_params=pltpu.CompilerParams(vmem_limit_bytes=16 * 1024 * 1024),
    )(*operands)


def shaped(*shape):
    return jax.ShapeDtypeStruct(shape, F32)


def tile_order(partner, rows, groups):
    count = rows * groups
    a = lax.broadcasted_iota(jnp.int32, (count, count), 0)
    b = lax.broadcasted_iota(jnp.int32, (count, count), 1)
    turn = (a == (b % rows) * groups + b // rows).astype(BF16)
    both = jnp.concatenate([partner // count, partner % count], axis=0)
    both = jnp.concatenate([both, jnp.zeros((6, count), jnp.int32)], axis=0).astype(F32).astype(BF16)
    lines = jnp.dot(both, turn, preferred_element_type=F32)
    columns = lax.dot_general(turn, both, (((0,), (1,)), ((), ())), preferred_element_type=F32)
    lines, columns = lines.astype(jnp.int32), columns.astype(jnp.int32)
    return lines[0:1], lines[1:2], columns[:, 0:1], columns[:, 1:2]


def tables_kernel(partner_ref, table_ref, place_ref, *, rows, groups, n_lat, n_lon):
    count = rows * groups
    devices = n_lat * n_lon
    line_target, line_slot, target, slot = tile_order(partner_ref[...], rows, groups)
    a = lax.broadcasted_iota(jnp.int32, (count, count), 0)
    b = lax.broadcasted_iota(jnp.int32, (count, count), 1)
    same = target == line_target
    came = jnp.sum((same & (line_slot < slot)).astype(F32), axis=1, keepdims=True).astype(jnp.int32)
    ahead = same & ((a % rows) * groups + a // rows < (b % rows) * groups + b // rows)
    sent = jnp.sum(ahead.astype(F32), axis=0, keepdims=True).astype(jnp.int32)

    row, group = slot // groups, slot % groups
    lat, lon = target // n_lon, target % n_lon
    north_ok = (row == rows - 1) & (lat < n_lat - 1)
    east_ok = group == groups - 1
    east_device = lat * n_lon + (lon + 1) % n_lon
    east_row = (east_device + (row // groups) * devices) * SLAB + SLAB - 1
    picks = (
        target * SLAB + came // groups,
        jnp.where(north_ok, (target + n_lon) * SLAB + SLAB - 2, -1),
        jnp.where(east_ok, east_row, -1),
    )
    index = lax.broadcasted_iota(jnp.int32, (count, table_ref.shape[1]), 1)
    for kind, pick in enumerate(picks):
        table_ref[kind * count : (kind + 1) * count, :] = (pick == index).astype(F32).astype(BF16)
    height = devices * SLAB
    packing = (sent % groups) * height + line_target * SLAB + sent // groups
    slots = lax.broadcasted_iota(jnp.int32, (groups * height, count), 0)
    table_ref[3 * count :, 0:count] = (slots == packing).astype(F32).astype(BF16)
    if table_ref.shape[1] > count:
        table_ref[3 * count :, count:] = jnp.zeros((groups * height, table_ref.shape[1] - count), BF16)

    lane = lax.broadcasted_iota(jnp.int32, (count, groups * TILE), 1)
    places = (
        lane // TILE == came % groups,
        lane // TILE == group,
        lane == (row % groups) * TILE + TILE - 1,
    )
    for kind, place in enumerate(places):
        place = place.astype(F32)
        for c in range(groups):
            place_ref[kind * groups + c] = place[c * rows : (c + 1) * rows]


def static_kernel(courant_ref, kappa_ref, coupling_ref, mask_ref, west_ref, south_ref, place_ref, static_ref):
    static_ref[ZONAL] = courant_ref[0]
    static_ref[MERIDIONAL] = courant_ref[1]
    for k in range(STEPS):
        static_ref[KAPPA + k] = kappa_ref[k]
    static_ref[COUPLING] = coupling_ref[...]
    for k in range(2):
        static_ref[WEST + k] = west_ref[k]
        static_ref[SOUTH + k] = south_ref[k]
    static_ref[WET] = mask_ref[...].astype(F32)
    for k in range(place_ref.shape[0]):
        static_ref[PLACE + k] = place_ref[k]


def local(adjoint, courant, diffusivity, coupling, partner, mask):
    fields = adjoint[0]
    courant, kappa, coupling, mask = courant[0], diffusivity[0], coupling[0], mask[0]
    tracers, levels, rows, cols = fields.shape
    groups = cols // TILE
    count = rows * groups
    n_lat, n_lon = lax.axis_size("lat"), lax.axis_size("lon")
    devices = n_lat * n_lon
    lat, lon = lax.axis_index("lat"), lax.axis_index("lon")
    spot = jnp.stack(
        [
            lax.axis_index("mp"),
            lat * n_lon + (lon + 1) % n_lon,
            ((lat + 1) % n_lat) * n_lon + lon,
            (lat < n_lat - 1).astype(jnp.int32),
        ]
    ).astype(jnp.int32)

    share = jnp.stack([coupling * (1.0 - kappa[0]), coupling * kappa[0]])
    from_west = lax.ppermute(share, "lon", [(i, (i + 1) % n_lon) for i in range(n_lon)])
    from_south = lax.ppermute(share, "lat", [(i, (i + 1) % n_lat) for i in range(n_lat)])

    def exchanged(send):
        return lax.all_to_all(send, ("mp", "lat", "lon"), split_axis=0, concat_axis=0, tiled=True)

    deep_rows = 3 * count
    table_shape = jax.ShapeDtypeStruct(
        (deep_rows + groups * devices * SLAB, max(count, 2 * devices * SLAB)), BF16
    )
    place_shape = shaped(3 * groups, rows, cols)
    table, place = call(
        functools.partial(tables_kernel, rows=rows, groups=groups, n_lat=n_lat, n_lon=n_lon),
        (partner,),
        [NEAR],
        (table_shape, place_shape),
        (NEAR, NEAR),
        "tables",
    )
    gathered = (courant, kappa, coupling, mask, from_west, from_south, place)
    static_shape = shaped(PLACE + 3 * groups, rows, cols)
    static_specs = [whole(a) for a in gathered]
    static_specs[1] = pl.BlockSpec((STEPS, rows, cols), lambda i: (0, 0, 0))
    static = call(static_kernel, gathered, static_specs, static_shape, whole(static_shape), "static", grid=(1,))
    send_shape = shaped(2 * devices, 2 * SLAB, cols)
    late = fields[:, :3]
    send = call(
        functools.partial(first_send_kernel, deep_rows=deep_rows),
        (spot, late, static, table),
        [SCALAR, NEAR, NEAR, NEAR],
        send_shape,
        NEAR,
        "first_send",
    )
    recv = exchanged(send)

    tiles = -(-levels // PACKED)
    width = ((tracers + 1) * tiles + 2) * cols
    halo_shapes = (
        shaped((tracers + 1) * (levels // 2) + 1, 2 * STEPS, cols),
        shaped(rows, width),
        shaped(2 * STEPS, width),
    )
    north, east, corner = call(
        halo_kernel,
        (send, fields, kappa, courant),
        [UNREAD, *(whole(a) for a in (fields, kappa, courant))],
        halo_shapes,
        tuple(whole(a) for a in halo_shapes),
        "halo",
        grid=(1,),
        us=2,
    )
    north = lax.ppermute(north, "lat", [((i + 1) % n_lat, i) for i in range(n_lat)])
    east = lax.ppermute(east, "lon", [((i + 1) % n_lon, i) for i in range(n_lon)])
    corner = lax.ppermute(
        corner,
        ("lat", "lon"),
        [
            (((i + 1) % n_lat) * n_lon + (j + 1) % n_lon, i * n_lon + j)
            for i in range(n_lat)
            for j in range(n_lon)
        ],
    )
    halo = (courant, north, east, corner)
    halo_specs = [whole(a) for a in halo]
    tall = rows + 2 * STEPS

    early, out = (), None
    for step in range(STEPS):
        if step > 0:
            recv = exchanged(send)
        after = ()
        if step == 0:
            after = (east, corner)
        if step == 1:
            shown = 2 * STEPS
            early_shape = shaped((STEPS - 1) * tracers * 4 + 1, rows, cols)
            early = (
                call(
                    functools.partial(early_kernel, all_levels=levels),
                    (send, spot, fields, kappa, *halo),
                    [
                        UNREAD,
                        SCALAR,
                        top(fields, shown),
                        pl.BlockSpec((shown, rows, cols), lambda i: (0, 0, 0)),
                        *halo_specs,
                    ],
                    early_shape,
                    whole(early_shape),
                    "early_levels",
                    grid=(1,),
                    scratch=[pltpu.VMEM((shown, tall, cols), F32)],
                    us=2,
                ),
            )
        if step > 1:
            for tracer in range(step - 2, tracers if step == STEPS - 1 else step - 1):
                before = () if out is None else (out,)
                block = pl.BlockSpec((1, levels, rows, cols), lambda i, tracer=tracer: (tracer, 0, 0, 0))
                out = call(
                    functools.partial(deep_kernel, tracer=tracer, tracers=tracers),
                    (send, spot, fields, *before, kappa, *halo),
                    [UNREAD, SCALAR, block, *(UNREAD for _ in before), whole(kappa), *halo_specs],
                    shaped(*fields.shape),
                    block,
                    "deep_levels",
                    grid=(1,),
                    aliases={3: 0} if before else None,
                    scratch=[pltpu.VMEM((levels, tall, cols), F32)],
                    us=4,
                )
            after = (out,)
        operands = (spot, late, recv, static, table, *early, *after)
        specs = [SCALAR, *(NEAR for _ in operands[1 : len(operands) - len(after)]), *(UNREAD for _ in after)]
        kernel = functools.partial(exchange_kernel, step=step, deep_rows=deep_rows, unread=len(after))
        if step == STEPS - 1:
            specs[1 : len(operands) - len(after)] = [whole(a) for a in operands[1 : len(operands) - len(after)]]
            return call(
                kernel,
                operands,
                specs,
                shaped(*fields.shape),
                top(fields, STEPS),
                "last_exchange",
                grid=(1,),
                aliases={len(operands) - 1: 0},
            )[None]
        late, send = call(
            kernel,
            operands,
            specs,
            (shaped(tracers, step + 1, rows, cols), send_shape),
            (NEAR, NEAR),
            "exchange",
        )


def solution(mesh):
    placed = (
        P("mp", None, None, "lat", "lon"),
        P("mp", None, "lat", "lon"),
        P("mp", None, "lat", "lon"),
        P("mp", "lat", "lon"),
        P("mp", ("lat", "lon")),
        P("mp", "lat", "lon"),
    )
    return jax.shard_map(
        local,
        mesh=mesh,
        in_specs=placed,
        out_specs=P("mp", None, None, "lat", "lon"),
        check_vma=False,
    )
```

```python
import functools

import jax
import jax.numpy as jnp
from jax import lax
from jax.experimental import pallas as pl
from jax.experimental.pallas import tpu as pltpu
from jax.sharding import PartitionSpec as P

TILE = 16
STEPS = 4
F32 = jnp.float32
BF16 = jnp.bfloat16
PACKED = 32
SLAB = 4
ZONAL, MERIDIONAL, KAPPA = 0, 1, 2
COUPLING = KAPPA + STEPS
WEST = COUPLING + 1
SOUTH = WEST + 2
WET = SOUTH + 2
PLACE = WET + 1


def lane_iota(shape):
    return lax.broadcasted_iota(jnp.int32, shape, len(shape) - 1)


def row_iota(shape):
    return lax.broadcasted_iota(jnp.int32, shape, len(shape) - 2)


def lane_roll(value, shift):
    shift = shift % value.shape[-1]
    return value if shift == 0 else pltpu.roll(value, shift, 1)


def next_row(value):
    return pltpu.roll(value, value.shape[0] - 1, 0)


def three_parts(value):
    high = value.astype(BF16)
    rest = value - high.astype(F32)
    middle = rest.astype(BF16)
    low = (rest - middle.astype(F32)).astype(BF16)
    return high, middle, low


def picked(one_hot, value):
    total = None
    for part in three_parts(value):
        term = jnp.dot(one_hot, part, preferred_element_type=F32)
        total = term if total is None else total + term
    return total


def halo_kernel(after_ref, fields_ref, kappa_ref, courant_ref, rows_ref, columns_ref, corner_ref):
    tracers, levels, rows, cols = fields_ref.shape
    lane = lane_iota((rows, cols))
    upper = row_iota((2 * STEPS, cols)) < STEPS
    pairs = levels // 2

    def first_rows(read, count, start):
        for pair in range(pairs):
            one = read(2 * pair)
            two = read(2 * pair + 1) if 2 * pair + 1 < count else jnp.zeros_like(one)
            rows_ref[start + pair] = jnp.where(upper, one, pltpu.roll(two, STEPS, 0))

    def first_columns(read, count, start):
        for tile in range(-(-levels // PACKED)):
            gathered = jnp.zeros((rows, cols), F32)
            for k in range(tile * PACKED, min((tile + 1) * PACKED, count)):
                place = k % PACKED
                gathered = jnp.where(lane // STEPS == place, lane_roll(read(k), place * STEPS), gathered)
            spot = slice((start + tile) * cols, (start + tile + 1) * cols)
            columns_ref[:, spot] = gathered
            corner_ref[:, spot] = gathered[0 : 2 * STEPS]

    tiles = -(-levels // PACKED)
    for tracer in range(tracers):
        first_rows(lambda k: fields_ref[tracer, k, 0 : 2 * STEPS, :], levels, tracer * pairs)
        first_columns(lambda k: fields_ref[tracer, k], levels, tracer * tiles)
    first_rows(lambda k: kappa_ref[k, 0 : 2 * STEPS, :], levels - 1, tracers * pairs)
    first_columns(lambda k: kappa_ref[k], levels - 1, tracers * tiles)
    rows_ref[(tracers + 1) * pairs] = jnp.where(
        upper,
        courant_ref[0, 0 : 2 * STEPS, :],
        pltpu.roll(courant_ref[1, 0 : 2 * STEPS, :], STEPS, 0),
    )
    for which in range(2):
        repeated = jnp.where(lane < STEPS, courant_ref[which], 0.0)
        shift = STEPS
        while shift < cols:
            repeated = repeated + lane_roll(repeated, shift)
            shift *= 2
        spot = slice(((tracers + 1) * tiles + which) * cols, ((tracers + 1) * tiles + which + 1) * cols)
        columns_ref[:, spot] = repeated
        corner_ref[:, spot] = repeated[0 : 2 * STEPS]


def wide_steps(spot_ref, refs, tracer, levels, tracers, all_levels, first_field, store, each_step):
    kappa_ref, courant_ref, rows_ref, columns_ref, corner_ref, state = refs
    rows, cols = courant_ref.shape[1:]
    pairs = all_levels // 2
    tiles = -(-all_levels // PACKED)
    used = -(-levels // PACKED)
    tall = rows + 2 * STEPS
    has_north = spot_ref[3] > 0
    lane = lane_iota((tall, cols))

    def with_rows(block, start, k):
        extra = rows_ref[start + k // 2]
        if k % 2:
            extra = pltpu.roll(extra, STEPS, 0)
        return jnp.concatenate([block, jnp.where(has_north, extra, 0.0)], axis=0)

    def strip(index):
        spot = slice(index * cols, (index + 1) * cols)
        corner = jnp.where(has_north, corner_ref[:, spot], 0.0)
        return jnp.concatenate([columns_ref[:, spot], corner], axis=0)

    last = rows_ref[(tracers + 1) * pairs]
    last = jnp.where(has_north, last, 0.0)
    zonal = jnp.concatenate([courant_ref[0], last], axis=0)
    meridional = jnp.concatenate([courant_ref[1], pltpu.roll(last, STEPS, 0)], axis=0)
    weight = (1.0 - zonal) - meridional
    side_zonal = strip((tracers + 1) * tiles)
    side_meridional = strip((tracers + 1) * tiles + 1)
    side_weight = (1.0 - side_zonal) - side_meridional
    side = [strip(tracer * tiles + i) for i in range(used)]
    side_kappa = [strip(tracers * tiles + i) for i in range(used)]
    end = (levels - (used - 1) * PACKED) * STEPS
    if levels < all_levels:
        side_kappa[-1] = jnp.where(lane < end, side_kappa[-1], 0.0)

    def lanes_on(tiles_in, shift):
        out = []
        for i, tile in enumerate(tiles_in):
            turned = lane_roll(tile, -shift)
            other = tiles_in[(i + 1 if shift > 0 else i - 1) % len(tiles_in)]
            if len(tiles_in) > 1:
                inside = lane < cols - shift if shift > 0 else lane >= -shift
                turned = jnp.where(inside, turned, lane_roll(other, -shift))
            out.append(turned)
        return out

    for step in range(STEPS):
        height = rows if step == STEPS - 1 else tall
        z, m, w = zonal[:height], meridional[:height], weight[:height]
        at_end = lane[:height] == cols - 1
        side_east = [side_zonal * tile for tile in side]

        def field_of(k):
            if step == 0:
                return with_rows(first_field(k), tracer * pairs, k)
            return state[k]

        def advected(k):
            field = field_of(k)
            edge = lane_roll(side_east[k // PACKED], cols - 1 - (k % PACKED) * STEPS)
            east = jnp.where(at_end, edge[:height], lane_roll((z * field[:height]), cols - 1))
            north = next_row(meridional * field)[:height]
            return (w * field[:height] + east) + north

        here = advected(0)
        above = None
        for k in range(levels):
            result = here
            if k + 1 < levels:
                below = advected(k + 1)
                kappa = kappa_ref[k]
                if height > rows:
                    kappa = with_rows(kappa, tracers * pairs, k)
                flux = kappa * (below - here)
                result = result + flux
            if k > 0:
                result = result - above
            if step == STEPS - 1:
                store(k, result)
            else:
                state[k] = result
            if k + 1 < levels:
                here, above = below, flux
        if step < STEPS - 1:
            east = lanes_on(side_east, 1)
            advected_side = [
                (side_weight * tile + turned) + next_row(side_meridional * tile)
                for tile, turned in zip(side, east)
            ]
            under = lanes_on(advected_side, STEPS)
            fluxes = [kap * (low - adv) for kap, low, adv in zip(side_kappa, under, advected_side)]
            over = lanes_on(fluxes, -STEPS)
            side = [(adv + flux) - up for adv, flux, up in zip(advected_side, fluxes, over)]
            if each_step is not None:
                each_step(step + 1, zonal, meridional, side_zonal, side)


def early_kernel(
    after_ref, spot_ref, fields_ref, kappa_ref, courant_ref, rows_ref, columns_ref, corner_ref,
    early_ref, state, *, all_levels,
):
    tracers, levels, rows, cols = fields_ref.shape
    refs = (kappa_ref, courant_ref, rows_ref, columns_ref, corner_ref, state)
    for tracer in range(tracers):

        def each_step(step, zonal, meridional, side_zonal, side):
            for j in range(2):
                k = step + j
                field = state[k]
                line = ((step - 1) * tracers + tracer) * 2 + j
                early_ref[2 * line] = field[:rows]
                early_ref[2 * line + 1] = lane_roll(side_zonal * side[0], cols - 1 - k * STEPS)[:rows]
                early_ref[early_ref.shape[0] - 1, line : line + 1, :] = (
                    meridional[rows : rows + 1] * field[rows : rows + 1]
                )

        wide_steps(
            spot_ref, refs, tracer, levels, tracers, all_levels,
            lambda k: fields_ref[tracer, k], lambda k, value: None, each_step,
        )


def deep_kernel(*refs, tracer, tracers):
    _, spot_ref, fields_ref, *rest = refs
    *halo, out_ref, state = rest[-7:] if len(rest) == 7 else rest[1:]
    levels = fields_ref.shape[1]

    def store(k, value):
        if k >= STEPS:
            out_ref[0, k] = value

    for k in range(STEPS):
        out_ref[0, k] = jnp.zeros(out_ref.shape[2:], F32)
    wide_steps(
        spot_ref, (*halo, state), tracer, levels, tracers, levels, lambda k: fields_ref[0, k], store, None
    )


def send_surface(late, below, static_ref, table_ref, send_ref, model, deep_rows):
    tracers = len(late)
    zonal, meridional = static_ref[ZONAL], static_ref[MERIDIONAL]
    weight = (1.0 - zonal) - meridional
    rows, cols = zonal.shape
    groups = cols // TILE
    lane = lane_iota((rows, cols))
    row = row_iota((rows, cols))
    kappa = static_ref[KAPPA]
    coupling = static_ref[COUPLING]
    group = lane // TILE
    tiles, edge_north, edge_east = [], [], []
    place = lane == (row % groups) * TILE + (TILE - 1) - row // groups
    west_a = lane_roll(static_ref[WEST], 1)
    west_b = lane_roll(static_ref[WEST + 1], 1)
    south_a, south_b = static_ref[SOUTH], static_ref[SOUTH + 1]
    own_north, own_east = [], jnp.zeros((rows, cols), F32)
    for tracer in range(tracers):
        parts = []
        for field in (late[tracer][0], below[tracer]):
            eastward, northward = zonal * field, meridional * field
            east = jnp.where(lane == cols - 1, 0.0, lane_roll(eastward, cols - 1))
            north = jnp.where(row == rows - 1, 0.0, next_row(northward))
            parts.append((eastward, northward, (weight * field + east) + north))
        (east0, north0, here), (east1, north1, under) = parts
        mixed = here + kappa * (under - here)
        scaled = coupling * mixed
        edge_north.append(south_a[rows - 1 : rows] * north0[0:1] + south_b[rows - 1 : rows] * north1[0:1])
        column = west_a * east0 + west_b * east1
        column = jnp.broadcast_to(column[:, 0:1], (rows, cols))
        edge_east.append(jnp.sum(jnp.where(place, column, 0.0), axis=0, keepdims=True))
        for k, field in enumerate(late[tracer]):
            own_north.append(meridional[0:1] * field[0:1])
            column = jnp.broadcast_to((zonal * field)[:, 0:1], (rows, cols))
            spot = (tracer * len(late[tracer]) + k) * rows + row
            own_east = jnp.where(lane == spot, column, own_east)
        blocks = []
        for c in range(groups):
            block = jnp.where(group == c, scaled, 0.0)
            shift = TILE
            while shift < cols:
                block = block + lane_roll(block, shift)
                shift *= 2
            blocks.append(block)
        tiles.append(jnp.concatenate(blocks, axis=0))
    devices = send_ref.shape[0] // 2
    height = devices * SLAB
    slots = picked(table_ref[deep_rows : deep_rows + groups * height, 0 : rows * groups], jnp.concatenate(tiles, axis=1))
    slot_group = (lane_iota((height, tracers * cols)) % cols) // TILE
    packed = jnp.zeros((height, tracers * cols), F32)
    for g in range(groups):
        packed = jnp.where(slot_group == g, slots[g * height : (g + 1) * height], packed)
    first, second = packed[:, :cols], packed[:, cols:]
    upper = row_iota((2 * SLAB, cols)) < SLAB
    empty = jnp.zeros((SLAB - 2, cols), F32)
    edges = jnp.concatenate(
        [empty, edge_north[0], edge_east[0], empty, edge_north[1], edge_east[1]], axis=0
    )
    own = own_north + [jnp.zeros((1, cols), F32)] * (2 * SLAB - 1 - len(own_north))
    own = jnp.concatenate(own + [jnp.sum(own_east, axis=0, keepdims=True)], axis=0)
    for pair in range(devices // 2):
        one, two = (half[pair * 2 * SLAB : (pair + 1) * 2 * SLAB] for half in (first, second))
        there = (1 - model) * devices + 2 * pair
        send_ref[there] = jnp.where(upper, one, pltpu.roll(two, SLAB, 0)) + edges
        send_ref[there + 1] = jnp.where(upper, pltpu.roll(one, SLAB, 0), two) + edges
        send_ref[model * devices + 2 * pair] = own
        send_ref[model * devices + 2 * pair + 1] = own


def receive_surface(model, recv_ref, table_ref, static_ref, surface):
    devices = recv_ref.shape[0] // 2
    rows, cols = surface[0].shape
    groups = cols // TILE
    tracers = len(surface)
    count = rows * groups
    other = (1 - model) * devices
    upper = row_iota((2 * SLAB, cols)) < SLAB
    first, second = [], []
    for pair in range(devices // 2):
        one, two = recv_ref[other + 2 * pair], recv_ref[other + 2 * pair + 1]
        first.append(jnp.where(upper, one, pltpu.roll(two, SLAB, 0)))
        second.append(jnp.where(upper, pltpu.roll(one, SLAB, 0), two))
    halves = [jnp.concatenate(half, axis=0) for half in (first, second)]
    slab = jnp.concatenate(halves, axis=1)
    shifted = jnp.concatenate([lane_roll(half, 1) for half in halves], axis=1)
    found = picked(table_ref[0 : 3 * count], jnp.concatenate([slab, shifted], axis=0))
    group = lane_iota((rows, cols)) // TILE
    wet, coupling = static_ref[WET], static_ref[COUPLING]
    updated = []
    for tracer in range(tracers):
        received = jnp.zeros((rows, cols), F32)
        for c in range(groups):
            total = None
            for kind in range(3):
                start = kind * count + c * rows
                place = static_ref[PLACE + kind * groups + c]
                term = jnp.where(
                    place > 0, found[start : start + rows, tracer * cols : (tracer + 1) * cols], 0.0
                )
                total = term if total is None else total + term
            shift = TILE
            while shift < cols:
                total = total + lane_roll(total, shift)
                shift *= 2
            received = jnp.where(group == c, total, received)
        own = surface[tracer]
        updated.append(own + wet * (received - coupling * own))
    return updated


def upper_levels(spot_ref, recv_ref, late, early, static_ref):
    zonal, meridional = static_ref[ZONAL], static_ref[MERIDIONAL]
    weight = (1.0 - zonal) - meridional
    rows, cols = zonal.shape
    lane = lane_iota((rows, cols))
    row = row_iota((rows, cols))
    devices = recv_ref.shape[0] // 2
    mine = spot_ref[0] * devices
    from_east = recv_ref[mine + spot_ref[1]]
    from_north = jnp.where(spot_ref[3] > 0, recv_ref[mine + spot_ref[2]], 0.0)
    east_line = jnp.broadcast_to(from_east[from_east.shape[0] - 1 :], (rows, cols))
    stepped = []
    for tracer in range(len(late)):
        count = len(late[tracer])
        moved = []
        for k in range(count + len(early[tracer])):
            if k < count:
                field = late[tracer][k]
                index = tracer * count + k
                north_edge = from_north[index : index + 1]
                column = jnp.where(lane == index * rows + row, east_line, 0.0)
                east_edge = jnp.sum(column, axis=1, keepdims=True)
            else:
                field, north_edge, east_edge = early[tracer][k - count]
            east = jnp.where(lane == cols - 1, east_edge, lane_roll(zonal * field, cols - 1))
            north = jnp.where(row == rows - 1, north_edge, next_row(meridional * field))
            moved.append((weight * field + east) + north)
        out, above = [], None
        for k in range(len(moved) - 1):
            flux = static_ref[KAPPA + k] * (moved[k + 1] - moved[k])
            result = moved[k] + flux
            if k > 0:
                result = result - above
            out.append(result)
            above = flux
        stepped.append(out)
    return stepped


def early_levels(step, early_ref, tracer, tracers):
    if step == 0:
        return []
    found = []
    for j in range(2):
        line = ((step - 1) * tracers + tracer) * 2 + j
        norths = early_ref[early_ref.shape[0] - 1]
        found.append((early_ref[2 * line], norths[line : line + 1], early_ref[2 * line + 1]))
    return found


def first_send_kernel(spot_ref, fields_ref, static_ref, table_ref, send_ref, *, deep_rows):
    tracers, levels = fields_ref.shape[:2]
    late = [[fields_ref[tracer, k] for k in range(levels)] for tracer in range(tracers)]
    send_surface(late, [values[1] for values in late], static_ref, table_ref, send_ref, spot_ref[0], deep_rows)


def exchange_kernel(spot_ref, late_ref, recv_ref, static_ref, table_ref, *refs, step, deep_rows, unread):
    early_ref, refs = (refs[0], refs[1:]) if step > 0 else (None, refs)
    refs = refs[unread:]
    tracers = late_ref.shape[0]
    late = [[late_ref[tracer, k] for k in range(late_ref.shape[1])] for tracer in range(tracers)]
    early = [early_levels(step, early_ref, tracer, tracers) for tracer in range(tracers)]
    stepped = upper_levels(spot_ref, recv_ref, late, early, static_ref)
    surface = [values[0] for values in stepped]
    surface = receive_surface(spot_ref[0], recv_ref, table_ref, static_ref, surface)
    for tracer in range(tracers):
        stepped[tracer][0] = surface[tracer]
    if step == STEPS - 1:
        (out_ref,) = refs
        for tracer in range(tracers):
            for k in range(STEPS):
                out_ref[tracer, k] = stepped[tracer][k]
        return
    late_out, send_ref = refs
    kept = late_out.shape[1]
    for tracer in range(tracers):
        for k in range(kept):
            late_out[tracer, k] = stepped[tracer][k]
    send_surface(
        [values[:kept] for values in stepped],
        [values[1] for values in stepped],
        static_ref,
        table_ref,
        send_ref,
        spot_ref[0],
        deep_rows,
    )


def whole(array):
    zeros = (0,) * array.ndim
    return pl.BlockSpec(array.shape, lambda i: zeros)


def top(array, levels):
    tracers, _, rows, cols = array.shape
    return pl.BlockSpec((tracers, levels, rows, cols), lambda i: (0, 0, 0, 0))


SCALAR = pl.BlockSpec(memory_space=pltpu.SMEM)
NEAR = pl.BlockSpec(memory_space=pltpu.VMEM)
UNREAD = pl.BlockSpec(memory_space=pl.ANY)


def call(kernel, operands, specs, out_shape, out_specs, name, grid=(), aliases=None, scratch=(), us=1):
    return pl.pallas_call(
        kernel,
        grid=grid,
        in_specs=specs,
        out_shape=out_shape,
        out_specs=out_specs,
        scratch_shapes=list(scratch),
        input_output_aliases=aliases or {},
        name=name,
        cost_estimate=pl.CostEstimate(flops=0, bytes_accessed=us * 3_000_000, transcendentals=0),
        compiler_params=pltpu.CompilerParams(vmem_limit_bytes=16 * 1024 * 1024),
    )(*operands)


def shaped(*shape):
    return jax.ShapeDtypeStruct(shape, F32)


def tile_order(partner, rows, groups):
    count = rows * groups
    a = lax.broadcasted_iota(jnp.int32, (count, count), 0)
    b = lax.broadcasted_iota(jnp.int32, (count, count), 1)
    turn = (a == (b % rows) * groups + b // rows).astype(BF16)
    both = jnp.concatenate([partner // count, partner % count], axis=0)
    both = jnp.concatenate([both, jnp.zeros((6, count), jnp.int32)], axis=0).astype(F32).astype(BF16)
    lines = jnp.dot(both, turn, preferred_element_type=F32)
    columns = lax.dot_general(turn, both, (((0,), (1,)), ((), ())), preferred_element_type=F32)
    lines, columns = lines.astype(jnp.int32), columns.astype(jnp.int32)
    return lines[0:1], lines[1:2], columns[:, 0:1], columns[:, 1:2]


def tables_kernel(partner_ref, table_ref, place_ref, *, rows, groups, n_lat, n_lon):
    count = rows * groups
    devices = n_lat * n_lon
    line_target, line_slot, target, slot = tile_order(partner_ref[...], rows, groups)
    a = lax.broadcasted_iota(jnp.int32, (count, count), 0)
    b = lax.broadcasted_iota(jnp.int32, (count, count), 1)
    same = target == line_target
    came = jnp.sum((same & (line_slot < slot)).astype(F32), axis=1, keepdims=True).astype(jnp.int32)
    ahead = same & ((a % rows) * groups + a // rows < (b % rows) * groups + b // rows)
    sent = jnp.sum(ahead.astype(F32), axis=0, keepdims=True).astype(jnp.int32)

    row, group = slot // groups, slot % groups
    lat, lon = target // n_lon, target % n_lon
    north_ok = (row == rows - 1) & (lat < n_lat - 1)
    east_ok = group == groups - 1
    east_device = lat * n_lon + (lon + 1) % n_lon
    east_row = (east_device + (row // groups) * devices) * SLAB + SLAB - 1
    picks = (
        target * SLAB + came // groups,
        jnp.where(north_ok, (target + n_lon) * SLAB + SLAB - 2, -1),
        jnp.where(east_ok, east_row, -1),
    )
    index = lax.broadcasted_iota(jnp.int32, (count, table_ref.shape[1]), 1)
    for kind, pick in enumerate(picks):
        table_ref[kind * count : (kind + 1) * count, :] = (pick == index).astype(F32).astype(BF16)
    height = devices * SLAB
    packing = (sent % groups) * height + line_target * SLAB + sent // groups
    slots = lax.broadcasted_iota(jnp.int32, (groups * height, count), 0)
    table_ref[3 * count :, 0:count] = (slots == packing).astype(F32).astype(BF16)
    if table_ref.shape[1] > count:
        table_ref[3 * count :, count:] = jnp.zeros((groups * height, table_ref.shape[1] - count), BF16)

    lane = lax.broadcasted_iota(jnp.int32, (count, groups * TILE), 1)
    places = (
        lane // TILE == came % groups,
        lane // TILE == group,
        lane == (row % groups) * TILE + TILE - 1,
    )
    for kind, place in enumerate(places):
        place = place.astype(F32)
        for c in range(groups):
            place_ref[kind * groups + c] = place[c * rows : (c + 1) * rows]


def static_kernel(courant_ref, kappa_ref, coupling_ref, mask_ref, west_ref, south_ref, place_ref, static_ref):
    static_ref[ZONAL] = courant_ref[0]
    static_ref[MERIDIONAL] = courant_ref[1]
    for k in range(STEPS):
        static_ref[KAPPA + k] = kappa_ref[k]
    static_ref[COUPLING] = coupling_ref[...]
    for k in range(2):
        static_ref[WEST + k] = west_ref[k]
        static_ref[SOUTH + k] = south_ref[k]
    static_ref[WET] = mask_ref[...].astype(F32)
    for k in range(place_ref.shape[0]):
        static_ref[PLACE + k] = place_ref[k]


def local(adjoint, courant, diffusivity, coupling, partner, mask):
    fields = adjoint[0]
    courant, kappa, coupling, mask = courant[0], diffusivity[0], coupling[0], mask[0]
    tracers, levels, rows, cols = fields.shape
    groups = cols // TILE
    count = rows * groups
    n_lat, n_lon = lax.axis_size("lat"), lax.axis_size("lon")
    devices = n_lat * n_lon
    lat, lon = lax.axis_index("lat"), lax.axis_index("lon")
    spot = jnp.stack(
        [
            lax.axis_index("mp"),
            lat * n_lon + (lon + 1) % n_lon,
            ((lat + 1) % n_lat) * n_lon + lon,
            (lat < n_lat - 1).astype(jnp.int32),
        ]
    ).astype(jnp.int32)

    share = jnp.stack([coupling * (1.0 - kappa[0]), coupling * kappa[0]])
    from_west = lax.ppermute(share, "lon", [(i, (i + 1) % n_lon) for i in range(n_lon)])
    from_south = lax.ppermute(share, "lat", [(i, (i + 1) % n_lat) for i in range(n_lat)])

    def exchanged(send):
        return lax.all_to_all(send, ("mp", "lat", "lon"), split_axis=0, concat_axis=0, tiled=True)

    deep_rows = 3 * count
    table_shape = jax.ShapeDtypeStruct(
        (deep_rows + groups * devices * SLAB, max(count, 2 * devices * SLAB)), BF16
    )
    place_shape = shaped(3 * groups, rows, cols)
    table, place = call(
        functools.partial(tables_kernel, rows=rows, groups=groups, n_lat=n_lat, n_lon=n_lon),
        (partner,),
        [NEAR],
        (table_shape, place_shape),
        (NEAR, NEAR),
        "tables",
    )
    gathered = (courant, kappa, coupling, mask, from_west, from_south, place)
    static_shape = shaped(PLACE + 3 * groups, rows, cols)
    static_specs = [whole(a) for a in gathered]
    static_specs[1] = pl.BlockSpec((STEPS, rows, cols), lambda i: (0, 0, 0))
    static = call(static_kernel, gathered, static_specs, static_shape, whole(static_shape), "static", grid=(1,))
    send_shape = shaped(2 * devices, 2 * SLAB, cols)
    late = fields[:, :3]
    send = call(
        functools.partial(first_send_kernel, deep_rows=deep_rows),
        (spot, late, static, table),
        [SCALAR, NEAR, NEAR, NEAR],
        send_shape,
        NEAR,
        "first_send",
    )
    recv = exchanged(send)

    tiles = -(-levels // PACKED)
    width = ((tracers + 1) * tiles + 2) * cols
    halo_shapes = (
        shaped((tracers + 1) * (levels // 2) + 1, 2 * STEPS, cols),
        shaped(rows, width),
        shaped(2 * STEPS, width),
    )
    north, east, corner = call(
        halo_kernel,
        (send, fields, kappa, courant),
        [UNREAD, *(whole(a) for a in (fields, kappa, courant))],
        halo_shapes,
        tuple(whole(a) for a in halo_shapes),
        "halo",
        grid=(1,),
        us=2,
    )
    north = lax.ppermute(north, "lat", [((i + 1) % n_lat, i) for i in range(n_lat)])
    east = lax.ppermute(east, "lon", [((i + 1) % n_lon, i) for i in range(n_lon)])
    corner = lax.ppermute(
        corner,
        ("lat", "lon"),
        [
            (((i + 1) % n_lat) * n_lon + (j + 1) % n_lon, i * n_lon + j)
            for i in range(n_lat)
            for j in range(n_lon)
        ],
    )
    halo = (courant, north, east, corner)
    halo_specs = [whole(a) for a in halo]
    tall = rows + 2 * STEPS

    early, out = (), None
    for step in range(STEPS):
        if step > 0:
            recv = exchanged(send)
        after = ()
        if step == 0:
            after = (east,)
        if step == 1:
            shown = 2 * STEPS
            early_shape = shaped((STEPS - 1) * tracers * 4 + 1, rows, cols)
            early = (
                call(
                    functools.partial(early_kernel, all_levels=levels),
                    (send, spot, fields, kappa, *halo),
                    [
                        UNREAD,
                        SCALAR,
                        top(fields, shown),
                        pl.BlockSpec((shown, rows, cols), lambda i: (0, 0, 0)),
                        *halo_specs,
                    ],
                    early_shape,
                    whole(early_shape),
                    "early_levels",
                    grid=(1,),
                    scratch=[pltpu.VMEM((shown, tall, cols), F32)],
                    us=2,
                ),
            )
        if step > 1:
            for tracer in range(step - 2, tracers if step == STEPS - 1 else step - 1):
                before = () if out is None else (out,)
                block = pl.BlockSpec((1, levels, rows, cols), lambda i, tracer=tracer: (tracer, 0, 0, 0))
                out = call(
                    functools.partial(deep_kernel, tracer=tracer, tracers=tracers),
                    (send, spot, fields, *before, kappa, *halo),
                    [UNREAD, SCALAR, block, *(UNREAD for _ in before), whole(kappa), *halo_specs],
                    shaped(*fields.shape),
                    block,
                    "deep_levels",
                    grid=(1,),
                    aliases={3: 0} if before else None,
                    scratch=[pltpu.VMEM((levels, tall, cols), F32)],
                    us=4,
                )
            after = (out,)
        operands = (spot, late, recv, static, table, *early, *after)
        specs = [SCALAR, *(NEAR for _ in operands[1 : len(operands) - len(after)]), *(UNREAD for _ in after)]
        kernel = functools.partial(exchange_kernel, step=step, deep_rows=deep_rows, unread=len(after))
        if step == STEPS - 1:
            specs[1 : len(operands) - len(after)] = [whole(a) for a in operands[1 : len(operands) - len(after)]]
            return call(
                kernel,
                operands,
                specs,
                shaped(*fields.shape),
                top(fields, STEPS),
                "last_exchange",
                grid=(1,),
                aliases={len(operands) - 1: 0},
            )[None]
        late, send = call(
            kernel,
            operands,
            specs,
            (shaped(tracers, step + 1, rows, cols), send_shape),
            (NEAR, NEAR),
            "exchange",
        )


def solution(mesh):
    placed = (
        P("mp", None, None, "lat", "lon"),
        P("mp", None, "lat", "lon"),
        P("mp", None, "lat", "lon"),
        P("mp", "lat", "lon"),
        P("mp", ("lat", "lon")),
        P("mp", "lat", "lon"),
    )
    return jax.shard_map(
        local,
        mesh=mesh,
        in_specs=placed,
        out_specs=P("mp", None, None, "lat", "lon"),
        check_vma=False,
    )
```

```python
import functools

import jax
import jax.numpy as jnp
from jax import lax
from jax.experimental import pallas as pl
from jax.experimental.pallas import tpu as pltpu
from jax.sharding import PartitionSpec as P

TILE = 16
STEPS = 4
F32 = jnp.float32
BF16 = jnp.bfloat16
UPPER = 8
PACKED = 32
SLAB = 4
ZONAL, MERIDIONAL, KAPPA = 0, 1, 2
COUPLING = KAPPA + STEPS
WET = COUPLING + 1


class Place:
    def __init__(self):
        n_lat, n_lon = lax.axis_size("lat"), lax.axis_size("lon")
        lat, lon = lax.axis_index("lat"), lax.axis_index("lon")
        self.model = lax.axis_index("mp")
        self.east = lat * n_lon + lax.rem(lon + 1, n_lon)
        self.north = lax.rem(lat + 1, n_lat) * n_lon + lon
        self.has_north = lat < n_lat - 1


def lane_iota(shape):
    return lax.broadcasted_iota(jnp.int32, shape, len(shape) - 1)


def row_iota(shape):
    return lax.broadcasted_iota(jnp.int32, shape, len(shape) - 2)


def lane_roll(value, shift):
    shift = shift % value.shape[-1]
    return value if shift == 0 else pltpu.roll(value, shift, 1)


def next_row(value):
    return pltpu.roll(value, value.shape[0] - 1, 0)


def three_parts(value):
    high = value.astype(BF16)
    rest = value - high.astype(F32)
    middle = rest.astype(BF16)
    low = (rest - middle.astype(F32)).astype(BF16)
    return high, middle, low


def picked(one_hot, value):
    total = None
    for part in three_parts(value):
        term = jnp.dot(one_hot, part, preferred_element_type=F32)
        total = term if total is None else total + term
    return total


def halo_kernel(fields_ref, kappa_ref, courant_ref, upper_ref, deep_ref, columns_ref, corner_ref):
    tracers, levels, rows, cols = fields_ref.shape
    lane = lane_iota((rows, cols))
    upper = row_iota((2 * STEPS, cols)) < STEPS
    upper_pairs, deep_pairs = UPPER // 2, (levels - UPPER) // 2

    def first_rows(read, count, which):
        for pair in range(levels // 2):
            one = read(2 * pair)
            two = read(2 * pair + 1) if 2 * pair + 1 < count else jnp.zeros_like(one)
            both = jnp.where(upper, one, pltpu.roll(two, STEPS, 0))
            if pair < upper_pairs:
                upper_ref[which * upper_pairs + pair] = both
            else:
                deep_ref[which * deep_pairs + pair - upper_pairs] = both

    def first_columns(read, count, start):
        for tile in range(-(-levels // PACKED)):
            gathered = jnp.zeros((rows, cols), F32)
            for k in range(tile * PACKED, min((tile + 1) * PACKED, count)):
                place = k % PACKED
                gathered = jnp.where(lane // STEPS == place, lane_roll(read(k), place * STEPS), gathered)
            spot = slice((start + tile) * cols, (start + tile + 1) * cols)
            columns_ref[:, spot] = gathered
            corner_ref[:, spot] = gathered[0 : 2 * STEPS]

    tiles = -(-levels // PACKED)
    for tracer in range(tracers):
        first_rows(lambda k: fields_ref[tracer, k, 0 : 2 * STEPS, :], levels, tracer)
        first_columns(lambda k: fields_ref[tracer, k], levels, tracer * tiles)
    first_rows(lambda k: kappa_ref[k, 0 : 2 * STEPS, :], levels - 1, tracers)
    first_columns(lambda k: kappa_ref[k], levels - 1, tracers * tiles)
    upper_ref[(tracers + 1) * upper_pairs] = jnp.where(
        upper,
        courant_ref[0, 0 : 2 * STEPS, :],
        pltpu.roll(courant_ref[1, 0 : 2 * STEPS, :], STEPS, 0),
    )
    for which in range(2):
        repeated = jnp.where(lane < STEPS, courant_ref[which], 0.0)
        shift = STEPS
        while shift < cols:
            repeated = repeated + lane_roll(repeated, shift)
            shift *= 2
        spot = slice(((tracers + 1) * tiles + which) * cols, ((tracers + 1) * tiles + which + 1) * cols)
        columns_ref[:, spot] = repeated
        corner_ref[:, spot] = repeated[0 : 2 * STEPS]


def wide_steps(refs, tracer, levels, tracers, all_levels, first_field, store, each_step):
    kappa_ref, courant_ref, rows_refs, columns_ref, corner_ref, state = refs
    rows, cols = courant_ref.shape[1:]
    upper_pairs, deep_pairs = UPPER // 2, (all_levels - UPPER) // 2
    tiles = -(-all_levels // PACKED)
    used = -(-levels // PACKED)
    tall = rows + 2 * STEPS
    has_north = Place().has_north
    lane = lane_iota((tall, cols))

    def with_rows(block, which, k):
        if k < UPPER:
            extra = rows_refs[0][which * upper_pairs + k // 2]
        else:
            extra = rows_refs[1][which * deep_pairs + (k - UPPER) // 2]
        if k % 2:
            extra = pltpu.roll(extra, STEPS, 0)
        return jnp.concatenate([block, jnp.where(has_north, extra, 0.0)], axis=0)

    def strip(index):
        spot = slice(index * cols, (index + 1) * cols)
        corner = jnp.where(has_north, corner_ref[:, spot], 0.0)
        return jnp.concatenate([columns_ref[:, spot], corner], axis=0)

    last = rows_refs[0][(tracers + 1) * upper_pairs]
    last = jnp.where(has_north, last, 0.0)
    zonal = jnp.concatenate([courant_ref[0], last], axis=0)
    meridional = jnp.concatenate([courant_ref[1], pltpu.roll(last, STEPS, 0)], axis=0)
    weight = (1.0 - zonal) - meridional
    side_zonal = strip((tracers + 1) * tiles)
    side_meridional = strip((tracers + 1) * tiles + 1)
    side_weight = (1.0 - side_zonal) - side_meridional
    side = [strip(tracer * tiles + i) for i in range(used)]
    side_kappa = [strip(tracers * tiles + i) for i in range(used)]
    end = (levels - (used - 1) * PACKED) * STEPS
    if levels < all_levels:
        side_kappa[-1] = jnp.where(lane < end, side_kappa[-1], 0.0)

    def lanes_on(tiles_in, shift):
        out = []
        for i, tile in enumerate(tiles_in):
            turned = lane_roll(tile, -shift)
            other = tiles_in[(i + 1 if shift > 0 else i - 1) % len(tiles_in)]
            if len(tiles_in) > 1:
                inside = lane < cols - shift if shift > 0 else lane >= -shift
                turned = jnp.where(inside, turned, lane_roll(other, -shift))
            out.append(turned)
        return out

    for step in range(STEPS):
        height = rows if step == STEPS - 1 else tall
        z, m, w = zonal[:height], meridional[:height], weight[:height]
        at_end = lane[:height] == cols - 1
        side_east = [side_zonal * tile for tile in side]

        def field_of(k):
            if step == 0:
                return with_rows(first_field(k), tracer, k)
            return state[k]

        def advected(k):
            field = field_of(k)
            edge = lane_roll(side_east[k // PACKED], cols - 1 - (k % PACKED) * STEPS)
            east = jnp.where(at_end, edge[:height], lane_roll((z * field[:height]), cols - 1))
            north = next_row(meridional * field)[:height]
            return (w * field[:height] + east) + north

        here = advected(0)
        above = None
        for k in range(levels):
            result = here
            if k + 1 < levels:
                below = advected(k + 1)
                kappa = kappa_ref[k]
                if height > rows:
                    kappa = with_rows(kappa, tracers, k)
                flux = kappa * (below - here)
                result = result + flux
            if k > 0:
                result = result - above
            if step == STEPS - 1:
                store(k, result)
            else:
                state[k] = result
            if k + 1 < levels:
                here, above = below, flux
        if step < STEPS - 1:
            east = lanes_on(side_east, 1)
            advected_side = [
                (side_weight * tile + turned) + next_row(side_meridional * tile)
                for tile, turned in zip(side, east)
            ]
            under = lanes_on(advected_side, STEPS)
            fluxes = [kap * (low - adv) for kap, low, adv in zip(side_kappa, under, advected_side)]
            over = lanes_on(fluxes, -STEPS)
            side = [(adv + flux) - up for adv, flux, up in zip(advected_side, fluxes, over)]
            if each_step is not None:
                each_step(step + 1, zonal, meridional, side_zonal, side)


def early_kernel(
    fields_ref, kappa_ref, courant_ref, rows_ref, columns_ref, corner_ref, early_ref, state, *, all_levels
):
    tracers, levels, rows, cols = fields_ref.shape
    refs = (kappa_ref, courant_ref, (rows_ref,), columns_ref, corner_ref, state)
    for tracer in range(tracers):

        def each_step(step, zonal, meridional, side_zonal, side):
            for j in range(2):
                k = step + j
                field = state[k]
                line = ((step - 1) * tracers + tracer) * 2 + j
                early_ref[2 * line] = field[:rows]
                early_ref[2 * line + 1] = lane_roll(side_zonal * side[0], cols - 1 - k * STEPS)[:rows]
                early_ref[early_ref.shape[0] - 1, line : line + 1, :] = (
                    meridional[rows : rows + 1] * field[rows : rows + 1]
                )

        wide_steps(
            refs, tracer, levels, tracers, all_levels,
            lambda k: fields_ref[tracer, k], lambda k, value: None, each_step,
        )


def deep_kernel(after_ref, fields_ref, *refs, tracer, tracers):
    kappa_ref, courant_ref, *rows_refs, columns_ref, corner_ref, out_ref, token_ref, state = refs[-9:]
    levels = fields_ref.shape[1]

    def store(k, value):
        if k >= STEPS:
            out_ref[0, k] = value

    for k in range(STEPS):
        out_ref[0, k] = jnp.zeros(out_ref.shape[2:], F32)
    wide_steps(
        (kappa_ref, courant_ref, rows_refs, columns_ref, corner_ref, state),
        tracer, levels, tracers, levels, lambda k: fields_ref[0, k], store, None,
    )
    token_ref[...] = jnp.zeros(token_ref.shape, F32)


def send_surface(late, below, static_refs, table_ref, send_ref, deep_rows):
    static_ref, west_ref, south_ref, _ = static_refs
    model = Place().model
    tracers = len(late)
    zonal, meridional = static_ref[ZONAL], static_ref[MERIDIONAL]
    weight = (1.0 - zonal) - meridional
    rows, cols = zonal.shape
    groups = cols // TILE
    lane = lane_iota((rows, cols))
    row = row_iota((rows, cols))
    kappa = static_ref[KAPPA]
    coupling = static_ref[COUPLING]
    group = lane // TILE
    tiles, edge_north, edge_east = [], [], []
    place = lane == (row % groups) * TILE + (TILE - 1) - row // groups
    west_a = lane_roll(west_ref[0], 1)
    west_b = lane_roll(west_ref[1], 1)
    south_a, south_b = south_ref[0], south_ref[1]
    own_north, own_east = [], jnp.zeros((rows, cols), F32)
    for tracer in range(tracers):
        parts = []
        for field in (late[tracer][0], below[tracer]):
            eastward, northward = zonal * field, meridional * field
            east = jnp.where(lane == cols - 1, 0.0, lane_roll(eastward, cols - 1))
            north = jnp.where(row == rows - 1, 0.0, next_row(northward))
            parts.append((eastward, northward, (weight * field + east) + north))
        (east0, north0, here), (east1, north1, under) = parts
        mixed = here + kappa * (under - here)
        scaled = coupling * mixed
        edge_north.append(south_a[rows - 1 : rows] * north0[0:1] + south_b[rows - 1 : rows] * north1[0:1])
        column = west_a * east0 + west_b * east1
        column = jnp.broadcast_to(column[:, 0:1], (rows, cols))
        edge_east.append(jnp.sum(jnp.where(place, column, 0.0), axis=0, keepdims=True))
        for k, field in enumerate(late[tracer]):
            own_north.append(meridional[0:1] * field[0:1])
            column = jnp.broadcast_to((zonal * field)[:, 0:1], (rows, cols))
            spot = (tracer * len(late[tracer]) + k) * rows + row
            own_east = jnp.where(lane == spot, column, own_east)
        blocks = []
        for c in range(groups):
            block = jnp.where(group == c, scaled, 0.0)
            shift = TILE
            while shift < cols:
                block = block + lane_roll(block, shift)
                shift *= 2
            blocks.append(block)
        tiles.append(jnp.concatenate(blocks, axis=0))
    devices = send_ref.shape[0] // 2
    height = devices * SLAB
    slots = picked(table_ref[deep_rows : deep_rows + groups * height, 0 : rows * groups], jnp.concatenate(tiles, axis=1))
    slot_group = (lane_iota((height, tracers * cols)) % cols) // TILE
    packed = jnp.zeros((height, tracers * cols), F32)
    for g in range(groups):
        packed = jnp.where(slot_group == g, slots[g * height : (g + 1) * height], packed)
    first, second = packed[:, :cols], packed[:, cols:]
    upper = row_iota((2 * SLAB, cols)) < SLAB
    empty = jnp.zeros((SLAB - 2, cols), F32)
    edges = jnp.concatenate(
        [empty, edge_north[0], edge_east[0], empty, edge_north[1], edge_east[1]], axis=0
    )
    own = own_north + [jnp.zeros((1, cols), F32)] * (2 * SLAB - 1 - len(own_north))
    own = jnp.concatenate(own + [jnp.sum(own_east, axis=0, keepdims=True)], axis=0)
    for pair in range(devices // 2):
        one, two = (half[pair * 2 * SLAB : (pair + 1) * 2 * SLAB] for half in (first, second))
        there = (1 - model) * devices + 2 * pair
        send_ref[there] = jnp.where(upper, one, pltpu.roll(two, SLAB, 0)) + edges
        send_ref[there + 1] = jnp.where(upper, pltpu.roll(one, SLAB, 0), two) + edges
        send_ref[model * devices + 2 * pair] = own
        send_ref[model * devices + 2 * pair + 1] = own


def receive_surface(recv_ref, table_ref, static_refs, surface):
    devices = recv_ref.shape[0] // 2
    rows, cols = surface[0].shape
    groups = cols // TILE
    tracers = len(surface)
    count = rows * groups
    static_ref, _, _, place_ref = static_refs
    other = (1 - Place().model) * devices
    upper = row_iota((2 * SLAB, cols)) < SLAB
    first, second = [], []
    for pair in range(devices // 2):
        one, two = recv_ref[other + 2 * pair], recv_ref[other + 2 * pair + 1]
        first.append(jnp.where(upper, one, pltpu.roll(two, SLAB, 0)))
        second.append(jnp.where(upper, pltpu.roll(one, SLAB, 0), two))
    halves = [jnp.concatenate(half, axis=0) for half in (first, second)]
    slab = jnp.concatenate(halves, axis=1)
    shifted = jnp.concatenate([lane_roll(half, 1) for half in halves], axis=1)
    found = picked(table_ref[0 : 3 * count], jnp.concatenate([slab, shifted], axis=0))
    group = lane_iota((rows, cols)) // TILE
    wet, coupling = static_ref[WET], static_ref[COUPLING]
    updated = []
    for tracer in range(tracers):
        received = jnp.zeros((rows, cols), F32)
        for c in range(groups):
            total = None
            for kind in range(3):
                start = kind * count + c * rows
                place = place_ref[kind * groups + c]
                term = jnp.where(
                    place > 0, found[start : start + rows, tracer * cols : (tracer + 1) * cols], 0.0
                )
                total = term if total is None else total + term
            shift = TILE
            while shift < cols:
                total = total + lane_roll(total, shift)
                shift *= 2
            received = jnp.where(group == c, total, received)
        own = surface[tracer]
        updated.append(own + wet * (received - coupling * own))
    return updated


def upper_levels(recv_ref, late, early, static_ref):
    zonal, meridional = static_ref[ZONAL], static_ref[MERIDIONAL]
    weight = (1.0 - zonal) - meridional
    rows, cols = zonal.shape
    lane = lane_iota((rows, cols))
    row = row_iota((rows, cols))
    devices = recv_ref.shape[0] // 2
    here = Place()
    mine = here.model * devices
    from_east = recv_ref[mine + here.east]
    from_north = jnp.where(here.has_north, recv_ref[mine + here.north], 0.0)
    east_line = jnp.broadcast_to(from_east[from_east.shape[0] - 1 :], (rows, cols))
    stepped = []
    for tracer in range(len(late)):
        count = len(late[tracer])
        moved = []
        for k in range(count + len(early[tracer])):
            if k < count:
                field = late[tracer][k]
                index = tracer * count + k
                north_edge = from_north[index : index + 1]
                column = jnp.where(lane == index * rows + row, east_line, 0.0)
                east_edge = jnp.sum(column, axis=1, keepdims=True)
            else:
                field, north_edge, east_edge = early[tracer][k - count]
            east = jnp.where(lane == cols - 1, east_edge, lane_roll(zonal * field, cols - 1))
            north = jnp.where(row == rows - 1, north_edge, next_row(meridional * field))
            moved.append((weight * field + east) + north)
        out, above = [], None
        for k in range(len(moved) - 1):
            flux = static_ref[KAPPA + k] * (moved[k + 1] - moved[k])
            result = moved[k] + flux
            if k > 0:
                result = result - above
            out.append(result)
            above = flux
        stepped.append(out)
    return stepped


def early_levels(step, early_ref, tracer, tracers):
    if step == 0:
        return []
    found = []
    for j in range(2):
        line = ((step - 1) * tracers + tracer) * 2 + j
        norths = early_ref[early_ref.shape[0] - 1]
        found.append((early_ref[2 * line], norths[line : line + 1], early_ref[2 * line + 1]))
    return found


def first_send_kernel(late_ref, *refs, deep_rows, carried):
    *static_refs, table_ref = refs[:5]
    send_ref = refs[5 + carried]
    tracers, levels = late_ref.shape[:2]
    late = [[late_ref[tracer, k] for k in range(levels)] for tracer in range(tracers)]
    send_surface(late, [values[1] for values in late], static_refs, table_ref, send_ref, deep_rows)


def exchange_kernel(late_ref, recv_ref, *refs, step, deep_rows, unread, carried=0):
    static_refs, table_ref, refs = refs[:4], refs[4], refs[5:]
    early_ref, refs = (refs[0], refs[1:]) if step > 0 else (None, refs)
    refs = refs[unread:] if step == STEPS - 1 else refs[unread + carried : unread + carried + 2]
    tracers = late_ref.shape[0]
    late = [[late_ref[tracer, k] for k in range(late_ref.shape[1])] for tracer in range(tracers)]
    early = [early_levels(step, early_ref, tracer, tracers) for tracer in range(tracers)]
    stepped = upper_levels(recv_ref, late, early, static_refs[0])
    surface = [values[0] for values in stepped]
    surface = receive_surface(recv_ref, table_ref, static_refs, surface)
    for tracer in range(tracers):
        stepped[tracer][0] = surface[tracer]
    if step == STEPS - 1:
        (out_ref,) = refs
        for tracer in range(tracers):
            for k in range(STEPS):
                out_ref[tracer, k] = stepped[tracer][k]
        return
    late_out, send_ref = refs
    kept = late_out.shape[1]
    for tracer in range(tracers):
        for k in range(kept):
            late_out[tracer, k] = stepped[tracer][k]
    send_surface(
        [values[:kept] for values in stepped],
        [values[1] for values in stepped],
        static_refs,
        table_ref,
        send_ref,
        deep_rows,
    )


def whole(array):
    zeros = (0,) * array.ndim
    return pl.BlockSpec(array.shape, lambda i: zeros)


def top(array, levels):
    tracers, _, rows, cols = array.shape
    return pl.BlockSpec((tracers, levels, rows, cols), lambda i: (0, 0, 0, 0))


NEAR = pl.BlockSpec(memory_space=pltpu.VMEM)
UNREAD = pl.BlockSpec(memory_space=pl.ANY)


def call(kernel, operands, specs, out_shape, out_specs, name, grid=(), aliases=None, scratch=(), us=1):
    return pl.pallas_call(
        kernel,
        grid=grid,
        in_specs=specs,
        out_shape=out_shape,
        out_specs=out_specs,
        scratch_shapes=list(scratch),
        input_output_aliases=aliases or {},
        name=name,
        cost_estimate=pl.CostEstimate(flops=0, bytes_accessed=us * 3_000_000, transcendentals=0),
        compiler_params=pltpu.CompilerParams(vmem_limit_bytes=16 * 1024 * 1024),
    )(*operands)


def shaped(*shape):
    return jax.ShapeDtypeStruct(shape, F32)


def tile_order(partner, rows, groups):
    count = rows * groups
    a = lax.broadcasted_iota(jnp.int32, (count, count), 0)
    b = lax.broadcasted_iota(jnp.int32, (count, count), 1)
    turn = (a == (b % rows) * groups + b // rows).astype(BF16)
    both = jnp.concatenate([partner // count, partner % count], axis=0)
    both = jnp.concatenate([both, jnp.zeros((6, count), jnp.int32)], axis=0).astype(F32).astype(BF16)
    lines = jnp.dot(both, turn, preferred_element_type=F32)
    columns = lax.dot_general(turn, both, (((0,), (1,)), ((), ())), preferred_element_type=F32)
    lines, columns = lines.astype(jnp.int32), columns.astype(jnp.int32)
    return lines[0:1], lines[1:2], columns[:, 0:1], columns[:, 1:2]


def tables_kernel(partner_ref, table_ref, place_ref, *, rows, groups, n_lat, n_lon):
    count = rows * groups
    devices = n_lat * n_lon
    line_target, line_slot, target, slot = tile_order(partner_ref[...], rows, groups)
    a = lax.broadcasted_iota(jnp.int32, (count, count), 0)
    b = lax.broadcasted_iota(jnp.int32, (count, count), 1)
    same = target == line_target
    came = jnp.sum((same & (line_slot < slot)).astype(F32), axis=1, keepdims=True).astype(jnp.int32)
    ahead = same & ((a % rows) * groups + a // rows < (b % rows) * groups + b // rows)
    sent = jnp.sum(ahead.astype(F32), axis=0, keepdims=True).astype(jnp.int32)

    row, group = slot // groups, slot % groups
    lat, lon = target // n_lon, target % n_lon
    north_ok = (row == rows - 1) & (lat < n_lat - 1)
    east_ok = group == groups - 1
    east_device = lat * n_lon + (lon + 1) % n_lon
    east_row = (east_device + (row // groups) * devices) * SLAB + SLAB - 1
    picks = (
        target * SLAB + came // groups,
        jnp.where(north_ok, (target + n_lon) * SLAB + SLAB - 2, -1),
        jnp.where(east_ok, east_row, -1),
    )
    index = lax.broadcasted_iota(jnp.int32, (count, table_ref.shape[1]), 1)
    for kind, pick in enumerate(picks):
        table_ref[kind * count : (kind + 1) * count, :] = (pick == index).astype(F32).astype(BF16)
    height = devices * SLAB
    packing = (sent % groups) * height + line_target * SLAB + sent // groups
    slots = lax.broadcasted_iota(jnp.int32, (groups * height, count), 0)
    table_ref[3 * count :, 0:count] = (slots == packing).astype(F32).astype(BF16)
    if table_ref.shape[1] > count:
        table_ref[3 * count :, count:] = jnp.zeros((groups * height, table_ref.shape[1] - count), BF16)

    lane = lax.broadcasted_iota(jnp.int32, (count, groups * TILE), 1)
    places = (
        lane // TILE == came % groups,
        lane // TILE == group,
        lane == (row % groups) * TILE + TILE - 1,
    )
    for kind, place in enumerate(places):
        place = place.astype(F32)
        for c in range(groups):
            place_ref[kind * groups + c] = place[c * rows : (c + 1) * rows]


def local(adjoint, courant, diffusivity, coupling, partner, mask):
    fields = adjoint[0]
    courant, kappa, coupling, mask = courant[0], diffusivity[0], coupling[0], mask[0]
    tracers, levels, rows, cols = fields.shape
    groups = cols // TILE
    count = rows * groups
    n_lat, n_lon = lax.axis_size("lat"), lax.axis_size("lon")
    devices = n_lat * n_lon

    share = jnp.stack([coupling * (1.0 - kappa[0]), coupling * kappa[0]])
    from_west = lax.ppermute(share, "lon", [(i, (i + 1) % n_lon) for i in range(n_lon)])
    from_south = lax.ppermute(share, "lat", [(i, (i + 1) % n_lat) for i in range(n_lat)])

    def exchanged(send):
        return lax.all_to_all(send, ("mp", "lat", "lon"), split_axis=0, concat_axis=0, tiled=True)

    deep_rows = 3 * count
    table_shape = jax.ShapeDtypeStruct(
        (deep_rows + groups * devices * SLAB, max(count, 2 * devices * SLAB)), BF16
    )
    table, place = call(
        functools.partial(tables_kernel, rows=rows, groups=groups, n_lat=n_lat, n_lon=n_lon),
        (partner,),
        [NEAR],
        (table_shape, shaped(3 * groups, rows, cols)),
        (NEAR, NEAR),
        "tables",
    )
    planes = jnp.concatenate([courant, kappa[:STEPS], coupling[None], mask[None].astype(F32)], axis=0)
    statics = (planes, from_west, from_south, place, table)

    tiles = -(-levels // PACKED)
    width = ((tracers + 1) * tiles + 2) * cols
    halo_shapes = (
        shaped((tracers + 1) * (UPPER // 2) + 1, 2 * STEPS, cols),
        shaped((tracers + 1) * ((levels - UPPER) // 2), 2 * STEPS, cols),
        shaped(rows, width),
        shaped(2 * STEPS, width),
    )
    packed = call(
        halo_kernel,
        (fields, kappa, courant),
        [whole(a) for a in (fields, kappa, courant)],
        halo_shapes,
        tuple(whole(a) for a in halo_shapes),
        "halo",
        grid=(1,),
        us=2,
    )
    send_shape = shaped(2 * devices, 2 * SLAB, cols)
    late = fields[:, :3]
    carried = (packed[0], packed[2], packed[3])
    send, *carried = call(
        functools.partial(first_send_kernel, deep_rows=deep_rows, carried=len(carried)),
        (late, *statics, *carried),
        [*(NEAR for _ in range(6)), *(UNREAD for _ in carried)],
        (send_shape, *(shaped(*a.shape) for a in carried)),
        (NEAR, *(UNREAD for _ in carried)),
        "first_send",
        aliases={6 + i: 1 + i for i in range(len(carried))},
    )
    recv = exchanged(send)
    upper, east, corner = carried
    from_north = [((i + 1) % n_lat, i) for i in range(n_lat)]
    upper = lax.ppermute(upper, "lat", from_north)
    east = lax.ppermute(east, "lon", [((i + 1) % n_lon, i) for i in range(n_lon)])
    corner = lax.ppermute(
        corner,
        ("lat", "lon"),
        [
            (((i + 1) % n_lat) * n_lon + (j + 1) % n_lon, i * n_lon + j)
            for i in range(n_lat)
            for j in range(n_lon)
        ],
    )
    tall = rows + 2 * STEPS

    early, out, after = (), None, (upper, east, corner)
    for step in range(STEPS):
        if step > 0:
            recv = exchanged(send)
        if step == 1:
            deep = lax.ppermute(deep, "lat", from_north)
            early_shape = shaped((STEPS - 1) * tracers * 4 + 1, rows, cols)
            early = (
                call(
                    functools.partial(early_kernel, all_levels=levels),
                    (fields, kappa, courant, upper, east, corner),
                    [
                        top(fields, UPPER),
                        pl.BlockSpec((UPPER, rows, cols), lambda i: (0, 0, 0)),
                        *(whole(a) for a in (courant, upper, east, corner)),
                    ],
                    early_shape,
                    whole(early_shape),
                    "early_levels",
                    grid=(1,),
                    scratch=[pltpu.VMEM((UPPER, tall, cols), F32)],
                    us=2,
                ),
            )
        if step > 1:
            halo = (kappa, courant, upper, deep, east, corner)
            for tracer in range(step - 2, tracers if step == STEPS - 1 else step - 1):
                before = () if out is None else (out,)
                block = pl.BlockSpec((1, levels, rows, cols), lambda i, tracer=tracer: (tracer, 0, 0, 0))
                token = shaped(8, cols)
                out, token = call(
                    functools.partial(deep_kernel, tracer=tracer, tracers=tracers),
                    (send, fields, *before, *halo),
                    [UNREAD, block, *(UNREAD for _ in before), *(whole(a) for a in halo)],
                    (shaped(*fields.shape), token),
                    (block, whole(token)),
                    "deep_levels",
                    grid=(1,),
                    aliases={2: 0} if before else None,
                    scratch=[pltpu.VMEM((levels, tall, cols), F32)],
                    us=4,
                )
            after = (token,)
        if step == STEPS - 1:
            after = (out,)
        operands = (late, recv, *statics, *early, *after)
        near = len(operands) - len(after)
        kernel = functools.partial(exchange_kernel, step=step, deep_rows=deep_rows, unread=len(after))
        if step == STEPS - 1:
            return call(
                kernel,
                operands,
                [*(whole(a) for a in operands[:near]), UNREAD],
                shaped(*fields.shape),
                top(fields, STEPS),
                "last_exchange",
                grid=(1,),
                aliases={near: 0},
            )[None]
        carry = (packed[1],) if step == 0 else ()
        late, send, *carry = call(
            functools.partial(kernel, carried=len(carry)),
            (*operands, *carry),
            [*(NEAR for _ in range(near)), *(UNREAD for _ in (*after, *carry))],
            (shaped(tracers, step + 1, rows, cols), send_shape, *(shaped(*a.shape) for a in carry)),
            (NEAR, NEAR, *(UNREAD for _ in carry)),
            "exchange",
            aliases={len(operands): 2} if carry else None,
        )
        if carry:
            (deep,) = carry
        after = ()


def solution(mesh):
    placed = (
        P("mp", None, None, "lat", "lon"),
        P("mp", None, "lat", "lon"),
        P("mp", None, "lat", "lon"),
        P("mp", "lat", "lon"),
        P("mp", ("lat", "lon")),
        P("mp", "lat", "lon"),
    )
    return jax.shard_map(
        local,
        mesh=mesh,
        in_specs=placed,
        out_specs=P("mp", None, None, "lat", "lon"),
        check_vma=False,
    )
```

```python
import functools

import jax
import jax.numpy as jnp
from jax import lax
from jax.experimental import pallas as pl
from jax.experimental.pallas import tpu as pltpu
from jax.sharding import PartitionSpec as P

TILE = 16
STEPS = 4
F32 = jnp.float32
BF16 = jnp.bfloat16
UPPER = 8
PACKED = 32
SLAB = 4
ZONAL, MERIDIONAL, KAPPA = 0, 1, 2
COUPLING = KAPPA + STEPS
WET = COUPLING + 1
WEST = WET + 1
SOUTH = WEST + 2
LATE = SOUTH + 2


class Place:
    def __init__(self):
        n_lat, n_lon = lax.axis_size("lat"), lax.axis_size("lon")
        lat, lon = lax.axis_index("lat"), lax.axis_index("lon")
        self.model = lax.axis_index("mp")
        self.east = lat * n_lon + lax.rem(lon + 1, n_lon)
        self.west = lat * n_lon + lax.rem(lon + n_lon - 1, n_lon)
        self.north = lax.rem(lat + 1, n_lat) * n_lon + lon
        self.has_north = lat < n_lat - 1


def lane_iota(shape):
    return lax.broadcasted_iota(jnp.int32, shape, len(shape) - 1)


def row_iota(shape):
    return lax.broadcasted_iota(jnp.int32, shape, len(shape) - 2)


def lane_roll(value, shift):
    shift = shift % value.shape[-1]
    return value if shift == 0 else pltpu.roll(value, shift, 1)


def next_row(value):
    return pltpu.roll(value, value.shape[0] - 1, 0)


def three_parts(value):
    high = value.astype(BF16)
    rest = value - high.astype(F32)
    middle = rest.astype(BF16)
    low = (rest - middle.astype(F32)).astype(BF16)
    return high, middle, low


def picked(one_hot, value):
    total = None
    for part in three_parts(value):
        term = jnp.dot(one_hot, part, preferred_element_type=F32)
        total = term if total is None else total + term
    return total


def pack_halo(fields_ref, kappa_ref, courant_ref, rows_ref, columns_ref):
    tracers, levels, rows, cols = fields_ref.shape
    lane = lane_iota((rows, cols))
    upper = row_iota((2 * STEPS, cols)) < STEPS
    pairs = levels // 2

    def first_rows(read, count, which):
        for pair in range(pairs):
            one = read(2 * pair)
            two = read(2 * pair + 1) if 2 * pair + 1 < count else jnp.zeros_like(one)
            rows_ref[which * pairs + pair] = jnp.where(upper, one, pltpu.roll(two, STEPS, 0))

    def first_columns(read, count, start):
        for tile in range(-(-levels // PACKED)):
            gathered = jnp.zeros((rows, cols), F32)
            for k in range(tile * PACKED, min((tile + 1) * PACKED, count)):
                place = k % PACKED
                gathered = jnp.where(lane // STEPS == place, lane_roll(read(k), place * STEPS), gathered)
            spot = slice((start + tile) * cols, (start + tile + 1) * cols)
            columns_ref[:, spot] = gathered

    tiles = -(-levels // PACKED)
    for tracer in range(tracers):
        first_rows(lambda k: fields_ref[tracer, k, 0 : 2 * STEPS, :], levels, tracer)
        first_columns(lambda k: fields_ref[tracer, k], levels, tracer * tiles)
    first_rows(lambda k: kappa_ref[k, 0 : 2 * STEPS, :], levels - 1, tracers)
    first_columns(lambda k: kappa_ref[k], levels - 1, tracers * tiles)
    rows_ref[(tracers + 1) * pairs] = jnp.where(
        upper,
        courant_ref[0, 0 : 2 * STEPS, :],
        pltpu.roll(courant_ref[1, 0 : 2 * STEPS, :], STEPS, 0),
    )
    for which in range(2):
        repeated = jnp.where(lane < STEPS, courant_ref[which], 0.0)
        shift = STEPS
        while shift < cols:
            repeated = repeated + lane_roll(repeated, shift)
            shift *= 2
        spot = slice(((tracers + 1) * tiles + which) * cols, ((tracers + 1) * tiles + which + 1) * cols)
        columns_ref[:, spot] = repeated


def wide_steps(refs, tracer, levels, tracers, all_levels, first_field, store, each_step):
    kappa_ref, courant_ref, rows_ref, columns_ref, state = refs
    rows, cols = courant_ref.shape[1:]
    pairs = all_levels // 2
    tiles = -(-all_levels // PACKED)
    used = -(-levels // PACKED)
    tall = rows + 2 * STEPS
    has_north = Place().has_north
    lane = lane_iota((tall, cols))

    def with_rows(block, which, k):
        extra = rows_ref[which * pairs + k // 2]
        if k % 2:
            extra = pltpu.roll(extra, STEPS, 0)
        return jnp.concatenate([block, jnp.where(has_north, extra, 0.0)], axis=0)

    def strip(index):
        spot = slice(index * cols, (index + 1) * cols)
        corner = jnp.where(has_north, rows_ref[(tracers + 1) * pairs + 1 + index], 0.0)
        return jnp.concatenate([columns_ref[:, spot], corner], axis=0)

    last = rows_ref[(tracers + 1) * pairs]
    last = jnp.where(has_north, last, 0.0)
    zonal = jnp.concatenate([courant_ref[0], last], axis=0)
    meridional = jnp.concatenate([courant_ref[1], pltpu.roll(last, STEPS, 0)], axis=0)
    weight = (1.0 - zonal) - meridional
    side_zonal = strip((tracers + 1) * tiles)
    side_meridional = strip((tracers + 1) * tiles + 1)
    side_weight = (1.0 - side_zonal) - side_meridional
    side = [strip(tracer * tiles + i) for i in range(used)]
    side_kappa = [strip(tracers * tiles + i) for i in range(used)]
    end = (levels - (used - 1) * PACKED) * STEPS
    if levels < all_levels:
        side_kappa[-1] = jnp.where(lane < end, side_kappa[-1], 0.0)

    def lanes_on(tiles_in, shift):
        out = []
        for i, tile in enumerate(tiles_in):
            turned = lane_roll(tile, -shift)
            other = tiles_in[(i + 1 if shift > 0 else i - 1) % len(tiles_in)]
            if len(tiles_in) > 1:
                inside = lane < cols - shift if shift > 0 else lane >= -shift
                turned = jnp.where(inside, turned, lane_roll(other, -shift))
            out.append(turned)
        return out

    for step in range(STEPS):
        height = rows if step == STEPS - 1 else tall
        z, m, w = zonal[:height], meridional[:height], weight[:height]
        at_end = lane[:height] == cols - 1
        side_east = [side_zonal * tile for tile in side]

        def field_of(k):
            if step == 0:
                return with_rows(first_field(k), tracer, k)
            return state[k]

        def advected(k):
            field = field_of(k)
            edge = lane_roll(side_east[k // PACKED], cols - 1 - (k % PACKED) * STEPS)
            east = jnp.where(at_end, edge[:height], lane_roll((z * field[:height]), cols - 1))
            north = next_row(meridional * field)[:height]
            return (w * field[:height] + east) + north

        here = advected(0)
        above = None
        for k in range(levels):
            result = here
            if k + 1 < levels:
                below = advected(k + 1)
                kappa = kappa_ref[k]
                if height > rows:
                    kappa = with_rows(kappa, tracers, k)
                flux = kappa * (below - here)
                result = result + flux
            if k > 0:
                result = result - above
            if step == STEPS - 1:
                store(k, result)
            else:
                state[k] = result
            if k + 1 < levels:
                here, above = below, flux
        if step < STEPS - 1:
            east = lanes_on(side_east, 1)
            advected_side = [
                (side_weight * tile + turned) + next_row(side_meridional * tile)
                for tile, turned in zip(side, east)
            ]
            under = lanes_on(advected_side, STEPS)
            fluxes = [kap * (low - adv) for kap, low, adv in zip(side_kappa, under, advected_side)]
            over = lanes_on(fluxes, -STEPS)
            side = [(adv + flux) - up for adv, flux, up in zip(advected_side, fluxes, over)]
            if each_step is not None:
                each_step(step + 1, zonal, meridional, side_zonal, side)


def early_kernel(
    fields_ref, kappa_ref, courant_ref, rows_ref, columns_ref, early_ref, state, *, all_levels
):
    tracers, levels, rows, cols = fields_ref.shape
    refs = (kappa_ref, courant_ref, rows_ref, columns_ref, state)
    for tracer in range(tracers):

        def each_step(step, zonal, meridional, side_zonal, side):
            for j in range(2 if step >= 2 else 0):
                k = step + j
                field = state[k]
                line = ((step - 2) * tracers + tracer) * 2 + j
                early_ref[2 * line] = field[:rows]
                early_ref[2 * line + 1] = lane_roll(side_zonal * side[0], cols - 1 - k * STEPS)[:rows]
                early_ref[early_ref.shape[0] - 1, line : line + 1, :] = (
                    meridional[rows : rows + 1] * field[rows : rows + 1]
                )

        wide_steps(
            refs, tracer, levels, tracers, all_levels,
            lambda k: fields_ref[tracer, k], lambda k, value: None, each_step,
        )


def deep_kernel(after_ref, fields_ref, *refs, tracer, tracers):
    kappa_ref, courant_ref, rows_ref, columns_ref, out_ref, token_ref, state = refs[-7:]
    levels = fields_ref.shape[1]

    def store(k, value):
        if k >= STEPS:
            out_ref[0, k] = value

    for k in range(STEPS):
        out_ref[0, k] = jnp.zeros(out_ref.shape[2:], F32)
    wide_steps(
        (kappa_ref, courant_ref, rows_ref, columns_ref, state),
        tracer, levels, tracers, levels, lambda k: fields_ref[0, k], store, None,
    )
    token_ref[...] = jnp.zeros(token_ref.shape, F32)


def send_surface(late, below, static_ref, table_ref, send_ref, deep_rows):
    here = Place()
    model = here.model
    tracers = len(late)
    zonal, meridional = static_ref[ZONAL], static_ref[MERIDIONAL]
    weight = (1.0 - zonal) - meridional
    rows, cols = zonal.shape
    groups = cols // TILE
    lane = lane_iota((rows, cols))
    row = row_iota((rows, cols))
    kappa = static_ref[KAPPA]
    coupling = static_ref[COUPLING]
    group = lane // TILE
    tiles, edge_north, edge_east = [], [], []
    place = lane == (row % groups) * TILE + (TILE - 1) - row // groups
    west_a = lane_roll(static_ref[WEST], 1)
    west_b = lane_roll(static_ref[WEST + 1], 1)
    south_a, south_b = static_ref[SOUTH], static_ref[SOUTH + 1]
    own_north, own_east = [], jnp.zeros((rows, cols), F32)
    for tracer in range(tracers):
        parts = []
        for field in (late[tracer][0], below[tracer]):
            eastward, northward = zonal * field, meridional * field
            east = jnp.where(lane == cols - 1, 0.0, lane_roll(eastward, cols - 1))
            north = jnp.where(row == rows - 1, 0.0, next_row(northward))
            parts.append((eastward, northward, (weight * field + east) + north))
        (east0, north0, over), (east1, north1, under) = parts
        mixed = over + kappa * (under - over)
        scaled = coupling * mixed
        edge_north.append(south_a[rows - 1 : rows] * north0[0:1] + south_b[rows - 1 : rows] * north1[0:1])
        column = west_a * east0 + west_b * east1
        column = jnp.broadcast_to(column[:, 0:1], (rows, cols))
        edge_east.append(jnp.sum(jnp.where(place, column, 0.0), axis=0, keepdims=True))
        for k, field in enumerate(late[tracer]):
            own_north.append(meridional[0:1] * field[0:1])
            column = jnp.broadcast_to((zonal * field)[:, 0:1], (rows, cols))
            spot = (tracer * len(late[tracer]) + k) * rows + row
            own_east = jnp.where(lane == spot, column, own_east)
        blocks = []
        for c in range(groups):
            block = jnp.where(group == c, scaled, 0.0)
            shift = TILE
            while shift < cols:
                block = block + lane_roll(block, shift)
                shift *= 2
            blocks.append(block)
        tiles.append(jnp.concatenate(blocks, axis=0))
    devices = send_ref.shape[0] // 2
    height = devices * SLAB
    slots = picked(table_ref[deep_rows : deep_rows + groups * height, 0 : rows * groups], jnp.concatenate(tiles, axis=1))
    slot_group = (lane_iota((height, tracers * cols)) % cols) // TILE
    packed = jnp.zeros((height, tracers * cols), F32)
    for g in range(groups):
        packed = jnp.where(slot_group == g, slots[g * height : (g + 1) * height], packed)
    first, second = packed[:, :cols], packed[:, cols:]
    upper = row_iota((2 * SLAB, cols)) < SLAB
    empty = jnp.zeros((SLAB - 2, cols), F32)
    edges = jnp.concatenate(
        [empty, edge_north[0], edge_east[0], empty, edge_north[1], edge_east[1]], axis=0
    )
    empty = [jnp.zeros((1, cols), F32)] * (2 * SLAB - 1)
    own_north = jnp.concatenate((own_north + empty)[: 2 * SLAB], axis=0)
    own_east = jnp.concatenate(empty + [jnp.sum(own_east, axis=0, keepdims=True)], axis=0)
    for pair in range(devices // 2):
        one, two = (half[pair * 2 * SLAB : (pair + 1) * 2 * SLAB] for half in (first, second))
        there = (1 - model) * devices + 2 * pair
        send_ref[there] = jnp.where(upper, one, pltpu.roll(two, SLAB, 0)) + edges
        send_ref[there + 1] = jnp.where(upper, pltpu.roll(one, SLAB, 0), two) + edges
        send_ref[model * devices + 2 * pair] = own_north
        send_ref[model * devices + 2 * pair + 1] = own_north
    send_ref[model * devices + here.west] = own_east


def receive_surface(recv_ref, table_ref, static_ref, surface):
    devices = recv_ref.shape[0] // 2
    rows, cols = surface[0].shape
    groups = cols // TILE
    tracers = len(surface)
    count = rows * groups
    other = (1 - Place().model) * devices
    upper = row_iota((2 * SLAB, cols)) < SLAB
    first, second = [], []
    for pair in range(devices // 2):
        one, two = recv_ref[other + 2 * pair], recv_ref[other + 2 * pair + 1]
        first.append(jnp.where(upper, one, pltpu.roll(two, SLAB, 0)))
        second.append(jnp.where(upper, pltpu.roll(one, SLAB, 0), two))
    halves = [jnp.concatenate(half, axis=0) for half in (first, second)]
    slab = jnp.concatenate(halves, axis=1)
    shifted = jnp.concatenate([lane_roll(half, 1) for half in halves], axis=1)
    found = picked(table_ref[0 : 3 * count], jnp.concatenate([slab, shifted], axis=0))
    group = lane_iota((rows, cols)) // TILE
    wet, coupling = static_ref[WET], static_ref[COUPLING]
    updated = []
    for tracer in range(tracers):
        received = jnp.zeros((rows, cols), F32)
        for c in range(groups):
            total = None
            for kind in range(3):
                start = kind * count + c * rows
                place = static_ref[LATE + tracers * STEPS + kind * groups + c]
                term = jnp.where(
                    place > 0, found[start : start + rows, tracer * cols : (tracer + 1) * cols], 0.0
                )
                total = term if total is None else total + term
            shift = TILE
            while shift < cols:
                total = total + lane_roll(total, shift)
                shift *= 2
            received = jnp.where(group == c, total, received)
        own = surface[tracer]
        updated.append(own + wet * (received - coupling * own))
    return updated


def upper_levels(recv_ref, late, early, static_ref):
    zonal, meridional = static_ref[ZONAL], static_ref[MERIDIONAL]
    weight = (1.0 - zonal) - meridional
    rows, cols = zonal.shape
    lane = lane_iota((rows, cols))
    row = row_iota((rows, cols))
    devices = recv_ref.shape[0] // 2
    here = Place()
    mine = here.model * devices
    from_east = recv_ref[mine + here.east]
    from_north = jnp.where(here.has_north, recv_ref[mine + here.north], 0.0)
    east_line = jnp.broadcast_to(from_east[from_east.shape[0] - 1 :], (rows, cols))
    stepped = []
    for tracer in range(len(late)):
        count = len(late[tracer])
        moved = []
        for k in range(count + len(early[tracer])):
            if k < count:
                field = late[tracer][k]
                index = tracer * count + k
                north_edge = from_north[index : index + 1]
                column = jnp.where(lane == index * rows + row, east_line, 0.0)
                east_edge = jnp.sum(column, axis=1, keepdims=True)
            else:
                field, north_edge, east_edge = early[tracer][k - count]
            east = jnp.where(lane == cols - 1, east_edge, lane_roll(zonal * field, cols - 1))
            north = jnp.where(row == rows - 1, north_edge, next_row(meridional * field))
            moved.append((weight * field + east) + north)
        out, above = [], None
        for k in range(len(moved) - 1):
            flux = static_ref[KAPPA + k] * (moved[k + 1] - moved[k])
            result = moved[k] + flux
            if k > 0:
                result = result - above
            out.append(result)
            above = flux
        stepped.append(out)
    return stepped


def early_levels(step, early_ref, tracer, tracers):
    if step < 2:
        return []
    found = []
    for j in range(2):
        line = ((step - 2) * tracers + tracer) * 2 + j
        norths = early_ref[early_ref.shape[0] - 1]
        found.append((early_ref[2 * line], norths[line : line + 1], early_ref[2 * line + 1]))
    return found


def first_send_kernel(west_ref, south_ref, table_ref, static_in, send_ref, static_ref, *, tracers, deep_rows):
    for k in range(2):
        static_ref[WEST + k] = west_ref[k]
        static_ref[SOUTH + k] = south_ref[k]
    late = [[static_in[LATE + tracer * STEPS + k] for k in range(STEPS)] for tracer in range(tracers)]
    send_surface(late, [values[1] for values in late], static_ref, table_ref, send_ref, deep_rows)


def exchange_kernel(static_in, recv_ref, table_ref, *refs, step, tracers, count, deep_rows, unread=0):
    early_ref, refs = (refs[0], refs[1:]) if step >= 2 else (None, refs)
    if step == 0:
        east_ref, _, *refs, rows_ref, sems = refs
        cols = rows_ref.shape[2]
        tiles = east_ref.shape[1] // cols
        corner = [
            pltpu.make_async_copy(
                east_ref.at[0 : 2 * STEPS, tile * cols : (tile + 1) * cols],
                rows_ref.at[rows_ref.shape[0] - tiles + tile],
                sems.at[tile],
            )
            for tile in range(tiles)
        ]
        for copy in corner:
            copy.start()
    refs = refs[unread:]
    late = [[static_in[LATE + tracer * STEPS + k] for k in range(count)] for tracer in range(tracers)]
    early = [early_levels(step, early_ref, tracer, tracers) for tracer in range(tracers)]
    stepped = upper_levels(recv_ref, late, early, static_in)
    surface = [values[0] for values in stepped]
    surface = receive_surface(recv_ref, table_ref, static_in, surface)
    for tracer in range(tracers):
        stepped[tracer][0] = surface[tracer]
    if step == STEPS - 1:
        (out_ref,) = refs
        for tracer in range(tracers):
            for k in range(STEPS):
                out_ref[tracer, k] = stepped[tracer][k]
        return
    static_ref, send_ref = refs
    for tracer in range(tracers):
        for k, value in enumerate(stepped[tracer]):
            static_ref[LATE + tracer * STEPS + k] = value
    send_surface(stepped, [values[1] for values in stepped], static_in, table_ref, send_ref, deep_rows)
    if step == 0:
        for copy in corner:
            copy.wait()


def whole(array):
    zeros = (0,) * array.ndim
    return pl.BlockSpec(array.shape, lambda i: zeros)


def top(array, levels):
    tracers, _, rows, cols = array.shape
    return pl.BlockSpec((tracers, levels, rows, cols), lambda i: (0, 0, 0, 0))


NEAR = pl.BlockSpec(memory_space=pltpu.VMEM)
FAR = pl.BlockSpec(memory_space=pltpu.HBM)
UNREAD = pl.BlockSpec(memory_space=pl.ANY)


def call(kernel, operands, specs, out_shape, out_specs, name, grid=(), aliases=None, scratch=(), us=1, mib=16):
    return pl.pallas_call(
        kernel,
        grid=grid,
        in_specs=specs,
        out_shape=out_shape,
        out_specs=out_specs,
        scratch_shapes=list(scratch),
        input_output_aliases=aliases or {},
        name=name,
        cost_estimate=pl.CostEstimate(flops=0, bytes_accessed=us * 3_000_000, transcendentals=0),
        compiler_params=pltpu.CompilerParams(vmem_limit_bytes=mib * 1024 * 1024),
    )(*operands)


def shaped(*shape):
    return jax.ShapeDtypeStruct(shape, F32)


def tile_order(partner, rows, groups):
    count = rows * groups
    a = lax.broadcasted_iota(jnp.int32, (count, count), 0)
    b = lax.broadcasted_iota(jnp.int32, (count, count), 1)
    turn = (a == (b % rows) * groups + b // rows).astype(BF16)
    both = jnp.concatenate([partner // count, partner % count], axis=0)
    both = jnp.concatenate([both, jnp.zeros((6, count), jnp.int32)], axis=0).astype(F32).astype(BF16)
    lines = jnp.dot(both, turn, preferred_element_type=F32)
    columns = lax.dot_general(turn, both, (((0,), (1,)), ((), ())), preferred_element_type=F32)
    lines, columns = lines.astype(jnp.int32), columns.astype(jnp.int32)
    return lines[0:1], lines[1:2], columns[:, 0:1], columns[:, 1:2]


def write_tables(partner, table_ref, planes_ref, start, rows, groups, n_lat, n_lon):
    count = rows * groups
    devices = n_lat * n_lon
    line_target, line_slot, target, slot = tile_order(partner, rows, groups)
    a = lax.broadcasted_iota(jnp.int32, (count, count), 0)
    b = lax.broadcasted_iota(jnp.int32, (count, count), 1)
    same = target == line_target
    came = jnp.sum((same & (line_slot < slot)).astype(F32), axis=1, keepdims=True).astype(jnp.int32)
    ahead = same & ((a % rows) * groups + a // rows < (b % rows) * groups + b // rows)
    sent = jnp.sum(ahead.astype(F32), axis=0, keepdims=True).astype(jnp.int32)

    row, group = slot // groups, slot % groups
    lat, lon = target // n_lon, target % n_lon
    north_ok = (row == rows - 1) & (lat < n_lat - 1)
    east_ok = group == groups - 1
    east_device = lat * n_lon + (lon + 1) % n_lon
    east_row = (east_device + (row // groups) * devices) * SLAB + SLAB - 1
    picks = (
        target * SLAB + came // groups,
        jnp.where(north_ok, (target + n_lon) * SLAB + SLAB - 2, -1),
        jnp.where(east_ok, east_row, -1),
    )
    index = lax.broadcasted_iota(jnp.int32, (count, table_ref.shape[1]), 1)
    for kind, pick in enumerate(picks):
        table_ref[kind * count : (kind + 1) * count, :] = (pick == index).astype(F32).astype(BF16)
    height = devices * SLAB
    packing = (sent % groups) * height + line_target * SLAB + sent // groups
    slots = lax.broadcasted_iota(jnp.int32, (groups * height, count), 0)
    table_ref[3 * count :, 0:count] = (slots == packing).astype(F32).astype(BF16)
    if table_ref.shape[1] > count:
        table_ref[3 * count :, count:] = jnp.zeros((groups * height, table_ref.shape[1] - count), BF16)

    lane = lax.broadcasted_iota(jnp.int32, (count, groups * TILE), 1)
    places = (
        lane // TILE == came % groups,
        lane // TILE == group,
        lane == (row % groups) * TILE + TILE - 1,
    )
    for kind, place in enumerate(places):
        place = place.astype(F32)
        for c in range(groups):
            planes_ref[start + kind * groups + c] = place[c * rows : (c + 1) * rows]


def prepare_kernel(*refs, n_lat, n_lon):
    sources, refs = refs[:6], refs[6:]
    (table_ref, planes_ref, rows_ref, columns_ref), refs = refs[:4], refs[4:]
    buffers, sems = refs[:6], refs[6]
    copies = [
        pltpu.make_async_copy(source, buffer, sems.at[i])
        for i, (source, buffer) in enumerate(zip(sources, buffers))
    ]
    for copy in copies:
        copy.start()
    fields, kappa, courant, coupling, mask, partner = buffers
    tracers, _, rows, cols = fields.shape
    copies[5].wait()
    write_tables(partner[...], table_ref, planes_ref, LATE + tracers * STEPS, rows, cols // TILE, n_lat, n_lon)
    for copy in copies[1:5]:
        copy.wait()
    planes_ref[ZONAL] = courant[0]
    planes_ref[MERIDIONAL] = courant[1]
    for k in range(STEPS):
        planes_ref[KAPPA + k] = kappa[k]
    planes_ref[COUPLING] = coupling[...]
    planes_ref[WET] = mask[...].astype(F32)
    copies[0].wait()
    for tracer in range(tracers):
        for k in range(STEPS):
            planes_ref[LATE + tracer * STEPS + k] = fields[tracer, k]
    pack_halo(fields, kappa, courant, rows_ref, columns_ref)


def local(adjoint, courant, diffusivity, coupling, partner, mask):
    fields = adjoint[0]
    courant, kappa, coupling, mask = courant[0], diffusivity[0], coupling[0], mask[0]
    tracers, levels, rows, cols = fields.shape
    groups = cols // TILE
    count = rows * groups
    n_lat, n_lon = lax.axis_size("lat"), lax.axis_size("lon")
    devices = n_lat * n_lon

    share = jnp.stack([coupling * (1.0 - kappa[0]), coupling * kappa[0]])
    from_west = lax.ppermute(share, "lon", [(i, (i + 1) % n_lon) for i in range(n_lon)])
    from_south = lax.ppermute(share, "lat", [(i, (i + 1) % n_lat) for i in range(n_lat)])

    def exchanged(send):
        return lax.all_to_all(send, ("mp", "lat", "lon"), split_axis=0, concat_axis=0, tiled=True)

    deep_rows = 3 * count
    width = ((tracers + 1) * -(-levels // PACKED) + 2) * cols
    sources = (fields, kappa, courant, coupling, mask, partner)
    table_shape = jax.ShapeDtypeStruct(
        (deep_rows + groups * devices * SLAB, max(count, 2 * devices * SLAB)), BF16
    )
    planes_shape = shaped(LATE + tracers * STEPS + 3 * groups, rows, cols)
    north_shape = shaped((tracers + 1) * (levels // 2) + 1 + width // cols, 2 * STEPS, cols)
    table, planes, north, east = call(
        functools.partial(prepare_kernel, n_lat=n_lat, n_lon=n_lon),
        sources,
        [FAR for _ in sources],
        (table_shape, planes_shape, north_shape, shaped(rows, width)),
        (NEAR, NEAR, NEAR, NEAR),
        "prepare",
        scratch=[*(pltpu.VMEM(a.shape, a.dtype) for a in sources), pltpu.SemaphoreType.DMA((len(sources),))],
        us=2,
        mib=53,
    )
    send_shape = shaped(2 * devices, 2 * SLAB, cols)
    send, planes = call(
        functools.partial(first_send_kernel, tracers=tracers, deep_rows=deep_rows),
        (from_west, from_south, table, planes),
        [NEAR, NEAR, NEAR, NEAR],
        (send_shape, planes_shape),
        (NEAR, NEAR),
        "first_send",
        aliases={3: 1},
    )
    recv = exchanged(send)
    east = lax.ppermute(east, "lon", [((i + 1) % n_lon, i) for i in range(n_lon)])
    tall = rows + 2 * STEPS

    def deep_levels(tracer, before, halo):
        block = pl.BlockSpec((1, levels, rows, cols), lambda i: (tracer, 0, 0, 0))
        token = shaped(8, cols)
        return call(
            functools.partial(deep_kernel, tracer=tracer, tracers=tracers),
            (send, fields, *before, *halo),
            [UNREAD, block, *(UNREAD for _ in before), *(whole(a) for a in halo)],
            (shaped(*fields.shape), token),
            (block, whole(token)),
            "deep_levels",
            grid=(1,),
            aliases={2: 0} if before else None,
            scratch=[pltpu.VMEM((levels, tall, cols), F32)],
            us=4,
        )

    reached = (STEPS, STEPS - 1, 2, 3)
    for step in range(STEPS):
        if step > 0:
            recv = exchanged(send)
        kernel = functools.partial(
            exchange_kernel, step=step, tracers=tracers, count=reached[step], deep_rows=deep_rows
        )
        operands = (planes, recv, table)
        if step == 0:
            planes, send, north = call(
                kernel,
                (*operands, east, north),
                [*[NEAR] * 4, UNREAD],
                (planes_shape, send_shape, north_shape),
                (NEAR, NEAR, UNREAD),
                "exchange",
                aliases={0: 0, 4: 2},
                scratch=[pltpu.SemaphoreType.DMA((width // cols,))],
            )
            north = lax.ppermute(north, "lat", [((i + 1) % n_lat, i) for i in range(n_lat)])
            halo = (kappa, courant, north, east)
        if step == 1:
            planes, send = call(
                kernel, operands, [NEAR] * 3, (planes_shape, send_shape), (NEAR, NEAR), "exchange", aliases={0: 0}
            )
        if step == 2:
            early_shape = shaped((STEPS - 2) * tracers * 4 + 1, rows, cols)
            early = call(
                functools.partial(early_kernel, all_levels=levels),
                (fields, *halo),
                [
                    top(fields, UPPER),
                    pl.BlockSpec((UPPER, rows, cols), lambda i: (0, 0, 0)),
                    *(whole(a) for a in halo[1:]),
                ],
                early_shape,
                whole(early_shape),
                "early_levels",
                grid=(1,),
                scratch=[pltpu.VMEM((UPPER, tall, cols), F32)],
                us=2,
            )
            out, token = deep_levels(0, (), halo)
            planes, send = call(
                functools.partial(kernel, unread=1),
                (*operands, early, token),
                [*[NEAR] * 4, UNREAD],
                (planes_shape, send_shape),
                (NEAR, NEAR),
                "exchange",
                aliases={0: 0},
            )
        if step == 3:
            for tracer in range(1, tracers):
                out, token = deep_levels(tracer, (out,), halo)
            operands = (*operands, early)
            return call(
                functools.partial(kernel, unread=1),
                (*operands, out),
                [*(whole(a) for a in operands), UNREAD],
                shaped(*fields.shape),
                top(fields, STEPS),
                "last_exchange",
                grid=(1,),
                aliases={len(operands): 0},
            )[None]


def solution(mesh):
    placed = (
        P("mp", None, None, "lat", "lon"),
        P("mp", None, "lat", "lon"),
        P("mp", None, "lat", "lon"),
        P("mp", "lat", "lon"),
        P("mp", ("lat", "lon")),
        P("mp", "lat", "lon"),
    )
    return jax.shard_map(
        local,
        mesh=mesh,
        in_specs=placed,
        out_specs=P("mp", None, None, "lat", "lon"),
        check_vma=False,
    )
```

```python
import functools

import jax
import jax.numpy as jnp
from jax import lax
from jax.experimental import pallas as pl
from jax.experimental.pallas import tpu as pltpu
from jax.sharding import PartitionSpec as P

TILE = 16
STEPS = 4
F32 = jnp.float32
BF16 = jnp.bfloat16
UPPER = 8
PACKED = 32
SLAB = 4
ZONAL, MERIDIONAL, KAPPA = 0, 1, 2
COUPLING = KAPPA + STEPS
WET = COUPLING + 1
SOUTH = WET + 1
LATE = SOUTH + 2


class Place:
    def __init__(self):
        n_lat, n_lon = lax.axis_size("lat"), lax.axis_size("lon")
        lat, lon = lax.axis_index("lat"), lax.axis_index("lon")
        self.model = lax.axis_index("mp")
        self.east = lat * n_lon + lax.rem(lon + 1, n_lon)
        self.west = lat * n_lon + lax.rem(lon + n_lon - 1, n_lon)
        self.north = lax.rem(lat + 1, n_lat) * n_lon + lon
        self.has_north = lat < n_lat - 1


def lane_iota(shape):
    return lax.broadcasted_iota(jnp.int32, shape, len(shape) - 1)


def row_iota(shape):
    return lax.broadcasted_iota(jnp.int32, shape, len(shape) - 2)


def lane_roll(value, shift):
    shift = shift % value.shape[-1]
    return value if shift == 0 else pltpu.roll(value, shift, 1)


def picked_by(value, one_hot):
    total = None
    for part in three_parts(value):
        term = jnp.dot(part, one_hot, preferred_element_type=F32)
        total = term if total is None else total + term
    return total


def next_row(value):
    return pltpu.roll(value, value.shape[0] - 1, 0)


def three_parts(value):
    high = value.astype(BF16)
    rest = value - high.astype(F32)
    middle = rest.astype(BF16)
    low = (rest - middle.astype(F32)).astype(BF16)
    return high, middle, low


def picked(one_hot, value):
    total = None
    for part in three_parts(value):
        term = jnp.dot(one_hot, part, preferred_element_type=F32)
        total = term if total is None else total + term
    return total


def pack_halo(fields_ref, kappa_ref, courant_ref, rows_ref, columns_ref):
    tracers, levels, rows, cols = fields_ref.shape
    lane = lane_iota((rows, cols))
    upper = row_iota((2 * STEPS, cols)) < STEPS
    pairs = levels // 2

    def first_rows(read, count, which):
        for pair in range(pairs):
            one = read(2 * pair)
            two = read(2 * pair + 1) if 2 * pair + 1 < count else jnp.zeros_like(one)
            rows_ref[which * pairs + pair] = jnp.where(upper, one, pltpu.roll(two, STEPS, 0))

    def first_columns(read, count, start):
        for tile in range(-(-levels // PACKED)):
            gathered = jnp.zeros((rows, cols), F32)
            for k in range(tile * PACKED, min((tile + 1) * PACKED, count)):
                place = k % PACKED
                gathered = jnp.where(lane // STEPS == place, lane_roll(read(k), place * STEPS), gathered)
            spot = slice((start + tile) * cols, (start + tile + 1) * cols)
            columns_ref[:, spot] = gathered

    tiles = -(-levels // PACKED)
    for tracer in range(tracers):
        first_rows(lambda k: fields_ref[tracer, k, 0 : 2 * STEPS, :], levels, tracer)
        first_columns(lambda k: fields_ref[tracer, k], levels, tracer * tiles)
    first_rows(lambda k: kappa_ref[k, 0 : 2 * STEPS, :], levels - 1, tracers)
    first_columns(lambda k: kappa_ref[k], levels - 1, tracers * tiles)
    rows_ref[(tracers + 1) * pairs] = jnp.where(
        upper,
        courant_ref[0, 0 : 2 * STEPS, :],
        pltpu.roll(courant_ref[1, 0 : 2 * STEPS, :], STEPS, 0),
    )
    for which in range(2):
        repeated = jnp.where(lane < STEPS, courant_ref[which], 0.0)
        shift = STEPS
        while shift < cols:
            repeated = repeated + lane_roll(repeated, shift)
            shift *= 2
        spot = slice(((tracers + 1) * tiles + which) * cols, ((tracers + 1) * tiles + which + 1) * cols)
        columns_ref[:, spot] = repeated


def wide_steps(refs, tracer, levels, tracers, all_levels, first_field, store, each_step):
    kappa_ref, courant_ref, rows_ref, columns_ref, state = refs
    rows, cols = courant_ref.shape[1:]
    pairs = all_levels // 2
    tiles = -(-all_levels // PACKED)
    used = -(-levels // PACKED)
    tall = rows + 2 * STEPS
    has_north = Place().has_north
    lane = lane_iota((tall, cols))

    def with_rows(block, which, k):
        extra = rows_ref[which * pairs + k // 2]
        if k % 2:
            extra = pltpu.roll(extra, STEPS, 0)
        return jnp.concatenate([block, jnp.where(has_north, extra, 0.0)], axis=0)

    def strip(index):
        spot = slice(index * cols, (index + 1) * cols)
        corner = jnp.where(has_north, rows_ref[(tracers + 1) * pairs + 1 + index], 0.0)
        return jnp.concatenate([columns_ref[:, spot], corner], axis=0)

    last = rows_ref[(tracers + 1) * pairs]
    last = jnp.where(has_north, last, 0.0)
    zonal = jnp.concatenate([courant_ref[0], last], axis=0)
    meridional = jnp.concatenate([courant_ref[1], pltpu.roll(last, STEPS, 0)], axis=0)
    weight = (1.0 - zonal) - meridional
    side_zonal = strip((tracers + 1) * tiles)
    side_meridional = strip((tracers + 1) * tiles + 1)
    side_weight = (1.0 - side_zonal) - side_meridional
    side = [strip(tracer * tiles + i) for i in range(used)]
    side_kappa = [strip(tracers * tiles + i) for i in range(used)]
    end = (levels - (used - 1) * PACKED) * STEPS
    if levels < all_levels:
        side_kappa[-1] = jnp.where(lane < end, side_kappa[-1], 0.0)

    def lanes_on(tiles_in, shift):
        out = []
        for i, tile in enumerate(tiles_in):
            turned = lane_roll(tile, -shift)
            other = tiles_in[(i + 1 if shift > 0 else i - 1) % len(tiles_in)]
            if len(tiles_in) > 1:
                inside = lane < cols - shift if shift > 0 else lane >= -shift
                turned = jnp.where(inside, turned, lane_roll(other, -shift))
            out.append(turned)
        return out

    for step in range(STEPS):
        height = rows if step == STEPS - 1 else tall
        z, m, w = zonal[:height], meridional[:height], weight[:height]
        at_end = lane[:height] == cols - 1
        side_east = [side_zonal * tile for tile in side]

        def field_of(k):
            if step == 0:
                return with_rows(first_field(k), tracer, k)
            return state[k]

        def advected(k):
            field = field_of(k)
            edge = lane_roll(side_east[k // PACKED], cols - 1 - (k % PACKED) * STEPS)
            east = jnp.where(at_end, edge[:height], lane_roll((z * field[:height]), cols - 1))
            north = next_row(meridional * field)[:height]
            return (w * field[:height] + east) + north

        here = advected(0)
        above = None
        for k in range(levels):
            result = here
            if k + 1 < levels:
                below = advected(k + 1)
                kappa = kappa_ref[k]
                if height > rows:
                    kappa = with_rows(kappa, tracers, k)
                flux = kappa * (below - here)
                result = result + flux
            if k > 0:
                result = result - above
            if step == STEPS - 1:
                store(k, result)
            else:
                state[k] = result
            if k + 1 < levels:
                here, above = below, flux
        if step < STEPS - 1:
            east = lanes_on(side_east, 1)
            advected_side = [
                (side_weight * tile + turned) + next_row(side_meridional * tile)
                for tile, turned in zip(side, east)
            ]
            under = lanes_on(advected_side, STEPS)
            fluxes = [kap * (low - adv) for kap, low, adv in zip(side_kappa, under, advected_side)]
            over = lanes_on(fluxes, -STEPS)
            side = [(adv + flux) - up for adv, flux, up in zip(advected_side, fluxes, over)]
            if each_step is not None:
                each_step(step + 1, zonal, meridional, side_zonal, side)


def early_kernel(
    fields_ref, kappa_ref, courant_ref, rows_ref, columns_ref, early_ref, state, *, all_levels
):
    tracers, levels, rows, cols = fields_ref.shape
    refs = (kappa_ref, courant_ref, rows_ref, columns_ref, state)
    for tracer in range(tracers):

        def each_step(step, zonal, meridional, side_zonal, side):
            for j in range(2 if step >= 2 else 0):
                k = step + j
                field = state[k]
                line = ((step - 2) * tracers + tracer) * 2 + j
                early_ref[2 * line] = field[:rows]
                early_ref[2 * line + 1] = lane_roll(side_zonal * side[0], cols - 1 - k * STEPS)[:rows]
                early_ref[early_ref.shape[0] - 1, line : line + 1, :] = (
                    meridional[rows : rows + 1] * field[rows : rows + 1]
                )

        wide_steps(
            refs, tracer, levels, tracers, all_levels,
            lambda k: fields_ref[tracer, k], lambda k, value: None, each_step,
        )


def deep_kernel(after_ref, fields_ref, *refs, tracer, tracers):
    kappa_ref, courant_ref, rows_ref, columns_ref, out_ref, token_ref, state = refs[-7:]
    levels = fields_ref.shape[1]

    def store(k, value):
        if k >= STEPS:
            out_ref[0, k] = value

    for k in range(STEPS):
        out_ref[0, k] = jnp.zeros(out_ref.shape[2:], F32)
    wide_steps(
        (kappa_ref, courant_ref, rows_ref, columns_ref, state),
        tracer, levels, tracers, levels, lambda k: fields_ref[0, k], store, None,
    )
    token_ref[...] = jnp.zeros(token_ref.shape, F32)


def send_surface(late, below, static_ref, table_ref, send_ref, deep_rows):
    here = Place()
    model = here.model
    tracers = len(late)
    zonal, meridional = static_ref[ZONAL], static_ref[MERIDIONAL]
    weight = (1.0 - zonal) - meridional
    rows, cols = zonal.shape
    groups = cols // TILE
    lane = lane_iota((rows, cols))
    row = row_iota((rows, cols))
    kappa = static_ref[KAPPA]
    coupling = static_ref[COUPLING]
    group = lane // TILE
    tiles, edge_north = [], []
    share = (coupling * (1.0 - kappa), coupling * kappa)
    raw_east, factors = jnp.zeros((rows, cols), F32), jnp.zeros((rows, cols), F32)
    south_a, south_b = static_ref[SOUTH], static_ref[SOUTH + 1]
    own_north, own_east = [], jnp.zeros((rows, cols), F32)
    for tracer in range(tracers):
        parts = []
        for field in (late[tracer][0], below[tracer]):
            eastward, northward = zonal * field, meridional * field
            east = jnp.where(lane == cols - 1, 0.0, lane_roll(eastward, cols - 1))
            north = jnp.where(row == rows - 1, 0.0, next_row(northward))
            parts.append((eastward, northward, (weight * field + east) + north))
        (east0, north0, over), (east1, north1, under) = parts
        mixed = over + kappa * (under - over)
        scaled = coupling * mixed
        edge_north.append(south_a[rows - 1 : rows] * north0[0:1] + south_b[rows - 1 : rows] * north1[0:1])
        for level, edge in enumerate((east0, east1)):
            place = lane == (tracer * 2 + level) * rows + row
            raw_east = jnp.where(place, jnp.broadcast_to(edge[:, 0:1], (rows, cols)), raw_east)
            factor = jnp.broadcast_to(share[level][:, cols - 1 : cols], (rows, cols))
            factors = jnp.where(place, factor, factors)
        for k, field in enumerate(late[tracer]):
            own_north.append(meridional[0:1] * field[0:1])
            column = jnp.broadcast_to((zonal * field)[:, 0:1], (rows, cols))
            spot = (tracer * len(late[tracer]) + k) * rows + row
            own_east = jnp.where(lane == spot, column, own_east)
        blocks = []
        for c in range(groups):
            block = jnp.where(group == c, scaled, 0.0)
            shift = TILE
            while shift < cols:
                block = block + lane_roll(block, shift)
                shift *= 2
            blocks.append(block)
        tiles.append(jnp.concatenate(blocks, axis=0))
    devices = send_ref.shape[0] // 2
    height = devices * SLAB
    slots = picked(table_ref[deep_rows : deep_rows + groups * height, 0 : rows * groups], jnp.concatenate(tiles, axis=1))
    slot_group = (lane_iota((height, tracers * cols)) % cols) // TILE
    packed = jnp.zeros((height, tracers * cols), F32)
    for g in range(groups):
        packed = jnp.where(slot_group == g, slots[g * height : (g + 1) * height], packed)
    first, second = packed[:, :cols], packed[:, cols:]
    upper = row_iota((2 * SLAB, cols)) < SLAB
    empty = jnp.zeros((SLAB - 2, cols), F32)
    edge_east = [jnp.sum(edge, axis=0, keepdims=True) for edge in (raw_east, factors)]
    edges = jnp.concatenate(
        [empty, edge_north[0], edge_east[0], empty, edge_north[1], edge_east[1]], axis=0
    )
    empty = [jnp.zeros((1, cols), F32)] * (2 * SLAB - 1)
    own_north = jnp.concatenate((own_north + empty)[: 2 * SLAB], axis=0)
    own_east = jnp.concatenate(empty + [jnp.sum(own_east, axis=0, keepdims=True)], axis=0)
    for pair in range(devices // 2):
        one, two = (half[pair * 2 * SLAB : (pair + 1) * 2 * SLAB] for half in (first, second))
        there = (1 - model) * devices + 2 * pair
        send_ref[there] = jnp.where(upper, one, pltpu.roll(two, SLAB, 0)) + edges
        send_ref[there + 1] = jnp.where(upper, pltpu.roll(one, SLAB, 0), two) + edges
        send_ref[model * devices + 2 * pair] = own_north
        send_ref[model * devices + 2 * pair + 1] = own_north
    send_ref[model * devices + here.west] = own_east


def receive_surface(recv_ref, table_ref, static_ref, surface):
    devices = recv_ref.shape[0] // 2
    rows, cols = surface[0].shape
    groups = cols // TILE
    tracers = len(surface)
    count = rows * groups
    other = (1 - Place().model) * devices
    upper = row_iota((2 * SLAB, cols)) < SLAB
    first, second = [], []
    for pair in range(devices // 2):
        one, two = recv_ref[other + 2 * pair], recv_ref[other + 2 * pair + 1]
        first.append(jnp.where(upper, one, pltpu.roll(two, SLAB, 0)))
        second.append(jnp.where(upper, pltpu.roll(one, SLAB, 0), two))
    slab = jnp.concatenate([jnp.concatenate(half, axis=0) for half in (first, second)], axis=1)
    found = picked(table_ref[0 : 4 * count, 0 : slab.shape[0]], slab)

    def place(kind):
        start = LATE + tracers * STEPS + kind * groups
        return static_ref[start : start + groups].reshape(count, cols) > 0

    edge = found[2 * count : 3 * count, :cols] * found[3 * count :, cols:]
    edge = jnp.where(place(2), edge, 0.0)
    shape = (cols, tracers * cols)
    source, lane = row_iota(shape), lane_iota(shape)
    spread = (source // (2 * rows) == lane // cols) & (lane % TILE == TILE - 1)
    edge = picked_by(edge, spread.astype(F32).astype(BF16))
    main, north = place(0), place(1)
    group = lane_iota((rows, cols)) // TILE
    wet, coupling = static_ref[WET], static_ref[COUPLING]
    updated = []
    for tracer in range(tracers):
        spot = slice(tracer * cols, (tracer + 1) * cols)
        total = jnp.where(main, found[:count, spot], 0.0) + jnp.where(north, found[count : 2 * count, spot], 0.0)
        shift = TILE
        while shift < cols:
            total = total + lane_roll(total, shift)
            shift *= 2
        total = total + edge[:, spot]
        received = jnp.zeros((rows, cols), F32)
        for c in range(groups):
            received = jnp.where(group == c, total[c * rows : (c + 1) * rows], received)
        own = surface[tracer]
        updated.append(own + wet * (received - coupling * own))
    return updated


def upper_levels(recv_ref, late, early, static_ref):
    zonal, meridional = static_ref[ZONAL], static_ref[MERIDIONAL]
    weight = (1.0 - zonal) - meridional
    rows, cols = zonal.shape
    lane = lane_iota((rows, cols))
    row = row_iota((rows, cols))
    devices = recv_ref.shape[0] // 2
    here = Place()
    mine = here.model * devices
    from_east = recv_ref[mine + here.east]
    from_north = jnp.where(here.has_north, recv_ref[mine + here.north], 0.0)
    east_line = jnp.broadcast_to(from_east[from_east.shape[0] - 1 :], (rows, cols))
    stepped = []
    for tracer in range(len(late)):
        count = len(late[tracer])
        moved = []
        for k in range(count + len(early[tracer])):
            if k < count:
                field = late[tracer][k]
                index = tracer * count + k
                north_edge = from_north[index : index + 1]
                column = jnp.where(lane == index * rows + row, east_line, 0.0)
                east_edge = jnp.sum(column, axis=1, keepdims=True)
            else:
                field, north_edge, east_edge = early[tracer][k - count]
            east = jnp.where(lane == cols - 1, east_edge, lane_roll(zonal * field, cols - 1))
            north = jnp.where(row == rows - 1, north_edge, next_row(meridional * field))
            moved.append((weight * field + east) + north)
        out, above = [], None
        for k in range(len(moved) - 1):
            flux = static_ref[KAPPA + k] * (moved[k + 1] - moved[k])
            result = moved[k] + flux
            if k > 0:
                result = result - above
            out.append(result)
            above = flux
        stepped.append(out)
    return stepped


def early_levels(step, early_ref, tracer, tracers):
    if step < 2:
        return []
    found = []
    for j in range(2):
        line = ((step - 2) * tracers + tracer) * 2 + j
        norths = early_ref[early_ref.shape[0] - 1]
        found.append((early_ref[2 * line], norths[line : line + 1], early_ref[2 * line + 1]))
    return found


def first_pack_kernel(table_ref, planes_ref, send_ref, *, tracers, deep_rows):
    late = [[planes_ref[LATE + tracer * STEPS + k] for k in range(STEPS)] for tracer in range(tracers)]
    send_surface(late, [values[1] for values in late], planes_ref, table_ref, send_ref, deep_rows)


def first_send_kernel(pack_ref, south_ref, static_in, send_ref, static_ref, *, tracers):
    for k in range(2):
        static_ref[SOUTH + k] = south_ref[k]
    devices = send_ref.shape[0] // 2
    rows, cols = static_in.shape[1:]
    factor = static_in[MERIDIONAL, 0:1, :]
    lines = []
    for tracer in range(tracers):
        north = [factor * static_in[LATE + tracer * STEPS + k, 0:1, :] for k in range(2)]
        lines.append(south_ref[0, rows - 1 : rows] * north[0] + south_ref[1, rows - 1 : rows] * north[1])
    row = row_iota((2 * SLAB, cols))
    edge = jnp.where(row == SLAB - 2, lines[0], jnp.where(row == 2 * SLAB - 2, lines[1], 0.0))
    model = Place().model
    for device in range(devices):
        there = (1 - model) * devices + device
        send_ref[there] = pack_ref[there] + edge
        here = model * devices + device
        send_ref[here] = pack_ref[here]


def exchange_kernel(static_in, recv_ref, table_ref, *refs, step, tracers, count, deep_rows, unread=0):
    early_ref, refs = (refs[0], refs[1:]) if step >= 2 else (None, refs)
    refs = refs[unread:]
    static_in = static_in if step == STEPS - 1 else refs[0]
    late = [[static_in[LATE + tracer * STEPS + k] for k in range(count)] for tracer in range(tracers)]
    early = [early_levels(step, early_ref, tracer, tracers) for tracer in range(tracers)]
    stepped = upper_levels(recv_ref, late, early, static_in)
    surface = [values[0] for values in stepped]
    surface = receive_surface(recv_ref, table_ref, static_in, surface)
    for tracer in range(tracers):
        stepped[tracer][0] = surface[tracer]
    if step == STEPS - 1:
        (out_ref,) = refs
        for tracer in range(tracers):
            for k in range(STEPS):
                out_ref[tracer, k] = stepped[tracer][k]
        return
    static_ref, send_ref = refs
    for tracer in range(tracers):
        for k, value in enumerate(stepped[tracer]):
            static_ref[LATE + tracer * STEPS + k] = value
    send_surface(stepped, [values[1] for values in stepped], static_in, table_ref, send_ref, deep_rows)


def whole(array):
    zeros = (0,) * array.ndim
    return pl.BlockSpec(array.shape, lambda i: zeros)


def top(array, levels):
    tracers, _, rows, cols = array.shape
    return pl.BlockSpec((tracers, levels, rows, cols), lambda i: (0, 0, 0, 0))


NEAR = pl.BlockSpec(memory_space=pltpu.VMEM)
FAR = pl.BlockSpec(memory_space=pltpu.HBM)
UNREAD = pl.BlockSpec(memory_space=pl.ANY)


def call(kernel, operands, specs, out_shape, out_specs, name, grid=(), aliases=None, scratch=(), us=1, mib=16):
    return pl.pallas_call(
        kernel,
        grid=grid,
        in_specs=specs,
        out_shape=out_shape,
        out_specs=out_specs,
        scratch_shapes=list(scratch),
        input_output_aliases=aliases or {},
        name=name,
        cost_estimate=pl.CostEstimate(flops=0, bytes_accessed=us * 3_000_000, transcendentals=0),
        compiler_params=pltpu.CompilerParams(vmem_limit_bytes=mib * 1024 * 1024),
    )(*operands)


def shaped(*shape):
    return jax.ShapeDtypeStruct(shape, F32)


def tile_order(partner, rows, groups):
    count = rows * groups
    a = lax.broadcasted_iota(jnp.int32, (count, count), 0)
    b = lax.broadcasted_iota(jnp.int32, (count, count), 1)
    turn = (a == (b % rows) * groups + b // rows).astype(BF16)
    both = jnp.concatenate([partner // count, partner % count], axis=0)
    both = jnp.concatenate([both, jnp.zeros((6, count), jnp.int32)], axis=0).astype(F32).astype(BF16)
    lines = jnp.dot(both, turn, preferred_element_type=F32)
    columns = lax.dot_general(turn, both, (((0,), (1,)), ((), ())), preferred_element_type=F32)
    lines, columns = lines.astype(jnp.int32), columns.astype(jnp.int32)
    return lines[0:1], lines[1:2], columns[:, 0:1], columns[:, 1:2]


def write_tables(partner, table_ref, planes_ref, start, rows, groups, n_lat, n_lon):
    count = rows * groups
    devices = n_lat * n_lon
    line_target, line_slot, target, slot = tile_order(partner, rows, groups)
    a = lax.broadcasted_iota(jnp.int32, (count, count), 0)
    b = lax.broadcasted_iota(jnp.int32, (count, count), 1)
    same = target == line_target
    came = jnp.sum((same & (line_slot < slot)).astype(F32), axis=1, keepdims=True).astype(jnp.int32)
    ahead = same & ((a % rows) * groups + a // rows < (b % rows) * groups + b // rows)
    sent = jnp.sum(ahead.astype(F32), axis=0, keepdims=True).astype(jnp.int32)

    row, group = slot // groups, slot % groups
    lat, lon = target // n_lon, target % n_lon
    north_ok = (row == rows - 1) & (lat < n_lat - 1)
    east_ok = group == groups - 1
    east_device = lat * n_lon + (lon + 1) % n_lon
    picks = (
        target * SLAB + came // groups,
        jnp.where(north_ok, (target + n_lon) * SLAB + SLAB - 2, -1),
        jnp.where(east_ok, east_device * SLAB + SLAB - 1, -1),
        jnp.where(east_ok, target * SLAB + SLAB - 1, -1),
    )
    index = lax.broadcasted_iota(jnp.int32, (count, table_ref.shape[1]), 1)
    for kind, pick in enumerate(picks):
        table_ref[kind * count : (kind + 1) * count, :] = (pick == index).astype(F32).astype(BF16)
    height = devices * SLAB
    packing = (sent % groups) * height + line_target * SLAB + sent // groups
    slots = lax.broadcasted_iota(jnp.int32, (groups * height, count), 0)
    table_ref[4 * count :, 0:count] = (slots == packing).astype(F32).astype(BF16)
    if table_ref.shape[1] > count:
        table_ref[4 * count :, count:] = jnp.zeros((groups * height, table_ref.shape[1] - count), BF16)

    lane = lax.broadcasted_iota(jnp.int32, (count, groups * TILE), 1)
    places = (
        lane // TILE == came % groups,
        lane // TILE == group,
        (lane % rows == row) & (lane < 2 * 2 * rows),
    )
    for kind, place in enumerate(places):
        place = place.astype(F32)
        for c in range(groups):
            planes_ref[start + kind * groups + c] = place[c * rows : (c + 1) * rows]


def prepare_kernel(*refs, n_lat, n_lon):
    fields, kappa, courant, coupling, mask, partner, table_ref, planes_ref, small, flags, line, sems = refs
    tracers, _, rows, cols = fields.shape
    copies = [pltpu.make_async_copy(partner, line, sems.at[0]), pltpu.make_async_copy(mask, flags, sems.at[1])]
    sources = [(courant, ZONAL, 2), (kappa.at[0:STEPS], KAPPA, STEPS)]
    sources += [(fields.at[tracer, 0:STEPS], LATE + tracer * STEPS, STEPS) for tracer in range(tracers)]
    for i, (source, plane, planes) in enumerate(sources):
        copies.append(pltpu.make_async_copy(source, planes_ref.at[plane : plane + planes], sems.at[2 + i]))
    copies.append(pltpu.make_async_copy(coupling, small, sems.at[2 + len(sources)]))
    for copy in copies:
        copy.start()
    copies[0].wait()
    write_tables(line[...], table_ref, planes_ref, LATE + tracers * STEPS, rows, cols // TILE, n_lat, n_lon)
    for k in range(2):
        planes_ref[SOUTH + k] = jnp.zeros((rows, cols), F32)
    for copy in copies[1:]:
        copy.wait()
    planes_ref[COUPLING] = small[...]
    planes_ref[WET] = flags[...].astype(F32)


def corner_kernel(after_ref, east_ref, rows_in, rows_ref, sems):
    cols = rows_ref.shape[2]
    tiles = east_ref.shape[1] // cols
    copies = [
        pltpu.make_async_copy(
            east_ref.at[0 : 2 * STEPS, tile * cols : (tile + 1) * cols],
            rows_ref.at[rows_ref.shape[0] - tiles + tile],
            sems.at[tile],
        )
        for tile in range(tiles)
    ]
    for copy in copies:
        copy.start()
    for copy in copies:
        copy.wait()


def halo_kernel(after_ref, fields_ref, kappa_ref, courant_ref, rows_ref, columns_ref):
    pack_halo(fields_ref, kappa_ref, courant_ref, rows_ref, columns_ref)


def local(adjoint, courant, diffusivity, coupling, partner, mask):
    fields = adjoint[0]
    courant, kappa, coupling, mask = courant[0], diffusivity[0], coupling[0], mask[0]
    tracers, levels, rows, cols = fields.shape
    groups = cols // TILE
    count = rows * groups
    n_lat, n_lon = lax.axis_size("lat"), lax.axis_size("lon")
    devices = n_lat * n_lon

    share = jnp.stack([coupling * (1.0 - kappa[0]), coupling * kappa[0]])
    from_south = lax.ppermute(share, "lat", [(i, (i + 1) % n_lat) for i in range(n_lat)])

    def exchanged(send):
        return lax.all_to_all(send, ("mp", "lat", "lon"), split_axis=0, concat_axis=0, tiled=True)

    deep_rows = 4 * count
    width = ((tracers + 1) * -(-levels // PACKED) + 2) * cols
    sources = (fields, kappa, courant, coupling, mask, partner)
    table_shape = jax.ShapeDtypeStruct(
        (deep_rows + groups * devices * SLAB, max(count, devices * SLAB)), BF16
    )
    planes_shape = shaped(LATE + tracers * STEPS + 3 * groups, rows, cols)
    north_shape = shaped((tracers + 1) * (levels // 2) + 1 + width // cols, 2 * STEPS, cols)
    table, planes = call(
        functools.partial(prepare_kernel, n_lat=n_lat, n_lon=n_lon),
        sources,
        [FAR for _ in sources],
        (table_shape, planes_shape),
        (NEAR, NEAR),
        "prepare",
        scratch=[
            pltpu.VMEM((rows, cols), F32),
            pltpu.VMEM((rows, cols), jnp.int32),
            pltpu.VMEM(partner.shape, jnp.int32),
            pltpu.SemaphoreType.DMA((5 + tracers,)),
        ],
        us=2,
        mib=53,
    )
    send_shape = shaped(2 * devices, 2 * SLAB, cols)
    pack = call(
        functools.partial(first_pack_kernel, tracers=tracers, deep_rows=deep_rows),
        (table, planes),
        [NEAR, NEAR],
        send_shape,
        NEAR,
        "first_pack",
    )
    send, planes = call(
        functools.partial(first_send_kernel, tracers=tracers),
        (pack, from_south, planes),
        [NEAR, NEAR, NEAR],
        (send_shape, planes_shape),
        (NEAR, NEAR),
        "first_send",
        aliases={2: 1},
    )
    recv = exchanged(send)
    halo_shapes = (north_shape, shaped(rows, width))
    north, east = call(
        halo_kernel,
        (send, fields, kappa, courant),
        [UNREAD, *(whole(a) for a in (fields, kappa, courant))],
        halo_shapes,
        tuple(whole(a) for a in halo_shapes),
        "halo",
        grid=(1,),
        us=2,
        mib=53,
    )
    east = lax.ppermute(east, "lon", [((i + 1) % n_lon, i) for i in range(n_lon)])
    tall = rows + 2 * STEPS

    def deep_levels(tracer, before, halo):
        block = pl.BlockSpec((1, levels, rows, cols), lambda i: (tracer, 0, 0, 0))
        token = shaped(8, cols)
        return call(
            functools.partial(deep_kernel, tracer=tracer, tracers=tracers),
            (send, fields, *before, *halo),
            [UNREAD, block, *(UNREAD for _ in before), *(whole(a) for a in halo)],
            (shaped(*fields.shape), token),
            (block, whole(token)),
            "deep_levels",
            grid=(1,),
            aliases={2: 0} if before else None,
            scratch=[pltpu.VMEM((levels, tall, cols), F32)],
            us=4,
        )

    reached = (STEPS, STEPS - 1, 2, 3)
    for step in range(STEPS):
        if step > 0:
            recv = exchanged(send)
        kernel = functools.partial(
            exchange_kernel, step=step, tracers=tracers, count=reached[step], deep_rows=deep_rows
        )
        operands = (planes, recv, table)
        if step == 0:
            planes, send = call(
                kernel, operands, [NEAR] * 3, (planes_shape, send_shape), (NEAR, NEAR), "exchange", aliases={0: 0}
            )
            north = call(
                corner_kernel,
                (send, east, north),
                [UNREAD, NEAR, UNREAD],
                north_shape,
                UNREAD,
                "corner",
                aliases={2: 0},
                scratch=[pltpu.SemaphoreType.DMA((width // cols,))],
            )
            north = lax.ppermute(north, "lat", [((i + 1) % n_lat, i) for i in range(n_lat)])
            halo = (kappa, courant, north, east)
        if step == 1:
            planes, send = call(
                kernel, operands, [NEAR] * 3, (planes_shape, send_shape), (NEAR, NEAR), "exchange", aliases={0: 0}
            )
        if step == 2:
            early_shape = shaped((STEPS - 2) * tracers * 4 + 1, rows, cols)
            early = call(
                functools.partial(early_kernel, all_levels=levels),
                (fields, *halo),
                [
                    top(fields, UPPER),
                    pl.BlockSpec((UPPER, rows, cols), lambda i: (0, 0, 0)),
                    *(whole(a) for a in halo[1:]),
                ],
                early_shape,
                whole(early_shape),
                "early_levels",
                grid=(1,),
                scratch=[pltpu.VMEM((UPPER, tall, cols), F32)],
                us=2,
            )
            out, token = deep_levels(0, (), halo)
            planes, send = call(
                functools.partial(kernel, unread=1),
                (*operands, early, token),
                [*[NEAR] * 4, UNREAD],
                (planes_shape, send_shape),
                (NEAR, NEAR),
                "exchange",
                aliases={0: 0},
            )
        if step == 3:
            for tracer in range(1, tracers):
                out, token = deep_levels(tracer, (out,), halo)
            operands = (*operands, early)
            return call(
                functools.partial(kernel, unread=1),
                (*operands, out),
                [*(whole(a) for a in operands), UNREAD],
                shaped(*fields.shape),
                top(fields, STEPS),
                "last_exchange",
                grid=(1,),
                aliases={len(operands): 0},
            )[None]


def solution(mesh):
    placed = (
        P("mp", None, None, "lat", "lon"),
        P("mp", None, "lat", "lon"),
        P("mp", None, "lat", "lon"),
        P("mp", "lat", "lon"),
        P("mp", ("lat", "lon")),
        P("mp", "lat", "lon"),
    )
    return jax.shard_map(
        local,
        mesh=mesh,
        in_specs=placed,
        out_specs=P("mp", None, None, "lat", "lon"),
        check_vma=False,
    )
```

```python
import functools

import jax
import jax.numpy as jnp
from jax import lax
from jax.experimental import pallas as pl
from jax.experimental.pallas import tpu as pltpu
from jax.sharding import PartitionSpec as P

TILE = 16
STEPS = 4
F32 = jnp.float32
BF16 = jnp.bfloat16
UPPER = 8
PACKED = 32
SLAB = 4
ZONAL, MERIDIONAL, KAPPA = 0, 1, 2
COUPLING = KAPPA + STEPS
WET = COUPLING + 1
SOUTH = WET + 1
LATE = SOUTH + 2


class Place:
    def __init__(self):
        n_lat, n_lon = lax.axis_size("lat"), lax.axis_size("lon")
        lat, lon = lax.axis_index("lat"), lax.axis_index("lon")
        self.model = lax.axis_index("mp")
        self.east = lat * n_lon + lax.rem(lon + 1, n_lon)
        self.west = lat * n_lon + lax.rem(lon + n_lon - 1, n_lon)
        self.north = lax.rem(lat + 1, n_lat) * n_lon + lon
        self.has_north = lat < n_lat - 1


def lane_iota(shape):
    return lax.broadcasted_iota(jnp.int32, shape, len(shape) - 1)


def row_iota(shape):
    return lax.broadcasted_iota(jnp.int32, shape, len(shape) - 2)


def lane_roll(value, shift):
    shift = shift % value.shape[-1]
    return value if shift == 0 else pltpu.roll(value, shift, 1)


def picked_by(value, one_hot):
    total = None
    for part in three_parts(value):
        term = jnp.dot(part, one_hot, preferred_element_type=F32)
        total = term if total is None else total + term
    return total


def next_row(value):
    return pltpu.roll(value, value.shape[0] - 1, 0)


def three_parts(value):
    high = value.astype(BF16)
    rest = value - high.astype(F32)
    middle = rest.astype(BF16)
    low = (rest - middle.astype(F32)).astype(BF16)
    return high, middle, low


def picked(one_hot, value):
    total = None
    for part in three_parts(value):
        term = jnp.dot(one_hot, part, preferred_element_type=F32)
        total = term if total is None else total + term
    return total


def pack_halo(fields_ref, kappa_ref, courant_ref, rows_ref, columns_ref):
    tracers, levels, rows, cols = fields_ref.shape
    lane = lane_iota((rows, cols))
    upper = row_iota((2 * STEPS, cols)) < STEPS
    pairs = levels // 2

    def first_rows(read, count, which):
        for pair in range(pairs):
            one = read(2 * pair)
            two = read(2 * pair + 1) if 2 * pair + 1 < count else jnp.zeros_like(one)
            rows_ref[which * pairs + pair] = jnp.where(upper, one, pltpu.roll(two, STEPS, 0))

    def first_columns(read, count, start):
        for tile in range(-(-levels // PACKED)):
            gathered = jnp.zeros((rows, cols), F32)
            for k in range(tile * PACKED, min((tile + 1) * PACKED, count)):
                place = k % PACKED
                gathered = jnp.where(lane // STEPS == place, lane_roll(read(k), place * STEPS), gathered)
            spot = slice((start + tile) * cols, (start + tile + 1) * cols)
            columns_ref[:, spot] = gathered

    tiles = -(-levels // PACKED)
    for tracer in range(tracers):
        first_rows(lambda k: fields_ref[tracer, k, 0 : 2 * STEPS, :], levels, tracer)
        first_columns(lambda k: fields_ref[tracer, k], levels, tracer * tiles)
    first_rows(lambda k: kappa_ref[k, 0 : 2 * STEPS, :], levels - 1, tracers)
    first_columns(lambda k: kappa_ref[k], levels - 1, tracers * tiles)
    rows_ref[(tracers + 1) * pairs] = jnp.where(
        upper,
        courant_ref[0, 0 : 2 * STEPS, :],
        pltpu.roll(courant_ref[1, 0 : 2 * STEPS, :], STEPS, 0),
    )
    for which in range(2):
        repeated = jnp.where(lane < STEPS, courant_ref[which], 0.0)
        shift = STEPS
        while shift < cols:
            repeated = repeated + lane_roll(repeated, shift)
            shift *= 2
        spot = slice(((tracers + 1) * tiles + which) * cols, ((tracers + 1) * tiles + which + 1) * cols)
        columns_ref[:, spot] = repeated


def wide_steps(refs, tracer, levels, tracers, all_levels, first_field, store, each_step):
    kappa_ref, courant_ref, rows_ref, columns_ref, state = refs
    rows, cols = courant_ref.shape[1:]
    pairs = all_levels // 2
    tiles = -(-all_levels // PACKED)
    used = -(-levels // PACKED)
    tall = rows + 2 * STEPS
    has_north = Place().has_north
    lane = lane_iota((tall, cols))

    def with_rows(block, which, k):
        extra = rows_ref[which * pairs + k // 2]
        if k % 2:
            extra = pltpu.roll(extra, STEPS, 0)
        return jnp.concatenate([block, jnp.where(has_north, extra, 0.0)], axis=0)

    def strip(index):
        spot = slice(index * cols, (index + 1) * cols)
        corner = jnp.where(has_north, rows_ref[(tracers + 1) * pairs + 1 + index], 0.0)
        return jnp.concatenate([columns_ref[:, spot], corner], axis=0)

    last = rows_ref[(tracers + 1) * pairs]
    last = jnp.where(has_north, last, 0.0)
    zonal = jnp.concatenate([courant_ref[0], last], axis=0)
    meridional = jnp.concatenate([courant_ref[1], pltpu.roll(last, STEPS, 0)], axis=0)
    weight = (1.0 - zonal) - meridional
    side_zonal = strip((tracers + 1) * tiles)
    side_meridional = strip((tracers + 1) * tiles + 1)
    side_weight = (1.0 - side_zonal) - side_meridional
    side = [strip(tracer * tiles + i) for i in range(used)]
    side_kappa = [strip(tracers * tiles + i) for i in range(used)]
    end = (levels - (used - 1) * PACKED) * STEPS
    if levels < all_levels:
        side_kappa[-1] = jnp.where(lane < end, side_kappa[-1], 0.0)

    def lanes_on(tiles_in, shift):
        out = []
        for i, tile in enumerate(tiles_in):
            turned = lane_roll(tile, -shift)
            other = tiles_in[(i + 1 if shift > 0 else i - 1) % len(tiles_in)]
            if len(tiles_in) > 1:
                inside = lane < cols - shift if shift > 0 else lane >= -shift
                turned = jnp.where(inside, turned, lane_roll(other, -shift))
            out.append(turned)
        return out

    for step in range(STEPS):
        height = rows if step == STEPS - 1 else tall
        z, m, w = zonal[:height], meridional[:height], weight[:height]
        at_end = lane[:height] == cols - 1
        side_east = [side_zonal * tile for tile in side]

        def field_of(k):
            if step == 0:
                return with_rows(first_field(k), tracer, k)
            return state[k]

        def advected(k):
            field = field_of(k)
            edge = lane_roll(side_east[k // PACKED], cols - 1 - (k % PACKED) * STEPS)
            east = jnp.where(at_end, edge[:height], lane_roll((z * field[:height]), cols - 1))
            north = next_row(meridional * field)[:height]
            return (w * field[:height] + east) + north

        here = advected(0)
        above = None
        for k in range(levels):
            result = here
            if k + 1 < levels:
                below = advected(k + 1)
                kappa = kappa_ref[k]
                if height > rows:
                    kappa = with_rows(kappa, tracers, k)
                flux = kappa * (below - here)
                result = result + flux
            if k > 0:
                result = result - above
            if step == STEPS - 1:
                store(k, result)
            else:
                state[k] = result
            if k + 1 < levels:
                here, above = below, flux
        if step < STEPS - 1:
            east = lanes_on(side_east, 1)
            advected_side = [
                (side_weight * tile + turned) + next_row(side_meridional * tile)
                for tile, turned in zip(side, east)
            ]
            under = lanes_on(advected_side, STEPS)
            fluxes = [kap * (low - adv) for kap, low, adv in zip(side_kappa, under, advected_side)]
            over = lanes_on(fluxes, -STEPS)
            side = [(adv + flux) - up for adv, flux, up in zip(advected_side, fluxes, over)]
            if each_step is not None:
                each_step(step + 1, zonal, meridional, side_zonal, side)


def early_kernel(
    fields_ref, kappa_ref, courant_ref, rows_ref, columns_ref, early_ref, state, *, all_levels
):
    tracers, levels, rows, cols = fields_ref.shape
    refs = (kappa_ref, courant_ref, rows_ref, columns_ref, state)
    for tracer in range(tracers):

        def each_step(step, zonal, meridional, side_zonal, side):
            for j in range(2 if step >= 2 else 0):
                k = step + j
                field = state[k]
                line = ((step - 2) * tracers + tracer) * 2 + j
                early_ref[2 * line] = field[:rows]
                early_ref[2 * line + 1] = lane_roll(side_zonal * side[0], cols - 1 - k * STEPS)[:rows]
                early_ref[early_ref.shape[0] - 1, line : line + 1, :] = (
                    meridional[rows : rows + 1] * field[rows : rows + 1]
                )

        wide_steps(
            refs, tracer, levels, tracers, all_levels,
            lambda k: fields_ref[tracer, k], lambda k, value: None, each_step,
        )


def deep_kernel(after_ref, fields_ref, *refs, tracer, tracers):
    kappa_ref, courant_ref, rows_ref, columns_ref, out_ref, token_ref, state = refs[-7:]
    levels = fields_ref.shape[1]

    def store(k, value):
        if k >= STEPS:
            out_ref[0, k] = value

    for k in range(STEPS):
        out_ref[0, k] = jnp.zeros(out_ref.shape[2:], F32)
    wide_steps(
        (kappa_ref, courant_ref, rows_ref, columns_ref, state),
        tracer, levels, tracers, levels, lambda k: fields_ref[0, k], store, None,
    )
    token_ref[...] = jnp.zeros(token_ref.shape, F32)


def send_surface(late, below, static_ref, table_ref, send_ref, deep_rows):
    here = Place()
    model = here.model
    tracers = len(late)
    zonal, meridional = static_ref[ZONAL], static_ref[MERIDIONAL]
    weight = (1.0 - zonal) - meridional
    rows, cols = zonal.shape
    groups = cols // TILE
    lane = lane_iota((rows, cols))
    row = row_iota((rows, cols))
    kappa = static_ref[KAPPA]
    coupling = static_ref[COUPLING]
    group = lane // TILE
    tiles, edge_north = [], []
    share = (coupling * (1.0 - kappa), coupling * kappa)
    raw_east, factors = jnp.zeros((rows, cols), F32), jnp.zeros((rows, cols), F32)
    south_a, south_b = static_ref[SOUTH], static_ref[SOUTH + 1]
    own_north, own_east = [], jnp.zeros((rows, cols), F32)
    for tracer in range(tracers):
        parts = []
        for field in (late[tracer][0], below[tracer]):
            eastward, northward = zonal * field, meridional * field
            east = jnp.where(lane == cols - 1, 0.0, lane_roll(eastward, cols - 1))
            north = jnp.where(row == rows - 1, 0.0, next_row(northward))
            parts.append((eastward, northward, (weight * field + east) + north))
        (east0, north0, over), (east1, north1, under) = parts
        mixed = over + kappa * (under - over)
        scaled = coupling * mixed
        edge_north.append(south_a[rows - 1 : rows] * north0[0:1] + south_b[rows - 1 : rows] * north1[0:1])
        for level, edge in enumerate((east0, east1)):
            place = lane == (tracer * 2 + level) * rows + row
            raw_east = jnp.where(place, jnp.broadcast_to(edge[:, 0:1], (rows, cols)), raw_east)
            factor = jnp.broadcast_to(share[level][:, cols - 1 : cols], (rows, cols))
            factors = jnp.where(place, factor, factors)
        for k, field in enumerate(late[tracer]):
            own_north.append(meridional[0:1] * field[0:1])
            column = jnp.broadcast_to((zonal * field)[:, 0:1], (rows, cols))
            spot = (tracer * len(late[tracer]) + k) * rows + row
            own_east = jnp.where(lane == spot, column, own_east)
        blocks = []
        for c in range(groups):
            block = jnp.where(group == c, scaled, 0.0)
            shift = TILE
            while shift < cols:
                block = block + lane_roll(block, shift)
                shift *= 2
            blocks.append(block)
        tiles.append(jnp.concatenate(blocks, axis=0))
    devices = send_ref.shape[0] // 2
    height = devices * SLAB
    slots = picked(table_ref[deep_rows : deep_rows + groups * height, 0 : rows * groups], jnp.concatenate(tiles, axis=1))
    slot_group = (lane_iota((height, tracers * cols)) % cols) // TILE
    packed = jnp.zeros((height, tracers * cols), F32)
    for g in range(groups):
        packed = jnp.where(slot_group == g, slots[g * height : (g + 1) * height], packed)
    first, second = packed[:, :cols], packed[:, cols:]
    upper = row_iota((2 * SLAB, cols)) < SLAB
    empty = jnp.zeros((SLAB - 2, cols), F32)
    edge_east = [jnp.sum(edge, axis=0, keepdims=True) for edge in (raw_east, factors)]
    edges = jnp.concatenate(
        [empty, edge_north[0], edge_east[0], empty, edge_north[1], edge_east[1]], axis=0
    )
    empty = [jnp.zeros((1, cols), F32)] * (2 * SLAB - 1)
    own_north = jnp.concatenate((own_north + empty)[: 2 * SLAB], axis=0)
    own_east = jnp.concatenate(empty + [jnp.sum(own_east, axis=0, keepdims=True)], axis=0)
    for pair in range(devices // 2):
        one, two = (half[pair * 2 * SLAB : (pair + 1) * 2 * SLAB] for half in (first, second))
        there = (1 - model) * devices + 2 * pair
        send_ref[there] = jnp.where(upper, one, pltpu.roll(two, SLAB, 0)) + edges
        send_ref[there + 1] = jnp.where(upper, pltpu.roll(one, SLAB, 0), two) + edges
        send_ref[model * devices + 2 * pair] = own_north
        send_ref[model * devices + 2 * pair + 1] = own_north
    send_ref[model * devices + here.west] = own_east


def receive_surface(recv_ref, table_ref, static_ref, surface):
    devices = recv_ref.shape[0] // 2
    rows, cols = surface[0].shape
    groups = cols // TILE
    tracers = len(surface)
    count = rows * groups
    other = (1 - Place().model) * devices
    upper = row_iota((2 * SLAB, cols)) < SLAB
    first, second = [], []
    for pair in range(devices // 2):
        one, two = recv_ref[other + 2 * pair], recv_ref[other + 2 * pair + 1]
        first.append(jnp.where(upper, one, pltpu.roll(two, SLAB, 0)))
        second.append(jnp.where(upper, pltpu.roll(one, SLAB, 0), two))
    slab = jnp.concatenate([jnp.concatenate(half, axis=0) for half in (first, second)], axis=1)
    found = picked(table_ref[0 : 4 * count, 0 : slab.shape[0]], slab)

    def place(kind):
        start = LATE + tracers * STEPS + kind * groups
        return static_ref[start : start + groups].reshape(count, cols) > 0

    edge = found[2 * count : 3 * count, :cols] * found[3 * count :, cols:]
    edge = jnp.where(place(2), edge, 0.0)
    shape = (cols, tracers * cols)
    source, lane = row_iota(shape), lane_iota(shape)
    spread = (source // (2 * rows) == lane // cols) & (lane % TILE == TILE - 1)
    edge = picked_by(edge, spread.astype(F32).astype(BF16))
    main, north = place(0), place(1)
    group = lane_iota((rows, cols)) // TILE
    wet, coupling = static_ref[WET], static_ref[COUPLING]
    updated = []
    for tracer in range(tracers):
        spot = slice(tracer * cols, (tracer + 1) * cols)
        total = jnp.where(main, found[:count, spot], 0.0) + jnp.where(north, found[count : 2 * count, spot], 0.0)
        shift = TILE
        while shift < cols:
            total = total + lane_roll(total, shift)
            shift *= 2
        total = total + edge[:, spot]
        received = jnp.zeros((rows, cols), F32)
        for c in range(groups):
            received = jnp.where(group == c, total[c * rows : (c + 1) * rows], received)
        own = surface[tracer]
        updated.append(own + wet * (received - coupling * own))
    return updated


def upper_levels(recv_ref, late, early, static_ref):
    zonal, meridional = static_ref[ZONAL], static_ref[MERIDIONAL]
    weight = (1.0 - zonal) - meridional
    rows, cols = zonal.shape
    lane = lane_iota((rows, cols))
    row = row_iota((rows, cols))
    devices = recv_ref.shape[0] // 2
    here = Place()
    mine = here.model * devices
    from_east = recv_ref[mine + here.east]
    from_north = jnp.where(here.has_north, recv_ref[mine + here.north], 0.0)
    east_line = jnp.broadcast_to(from_east[from_east.shape[0] - 1 :], (rows, cols))
    stepped = []
    for tracer in range(len(late)):
        count = len(late[tracer])
        moved = []
        for k in range(count + len(early[tracer])):
            if k < count:
                field = late[tracer][k]
                index = tracer * count + k
                north_edge = from_north[index : index + 1]
                column = jnp.where(lane == index * rows + row, east_line, 0.0)
                east_edge = jnp.sum(column, axis=1, keepdims=True)
            else:
                field, north_edge, east_edge = early[tracer][k - count]
            east = jnp.where(lane == cols - 1, east_edge, lane_roll(zonal * field, cols - 1))
            north = jnp.where(row == rows - 1, north_edge, next_row(meridional * field))
            moved.append((weight * field + east) + north)
        out, above = [], None
        for k in range(len(moved) - 1):
            flux = static_ref[KAPPA + k] * (moved[k + 1] - moved[k])
            result = moved[k] + flux
            if k > 0:
                result = result - above
            out.append(result)
            above = flux
        stepped.append(out)
    return stepped


def early_levels(step, early_ref, tracer, tracers):
    if step < 2:
        return []
    found = []
    for j in range(2):
        line = ((step - 2) * tracers + tracer) * 2 + j
        norths = early_ref[early_ref.shape[0] - 1]
        found.append((early_ref[2 * line], norths[line : line + 1], early_ref[2 * line + 1]))
    return found


def first_pack_kernel(table_ref, planes_ref, send_ref, *, tracers, deep_rows):
    late = [[planes_ref[LATE + tracer * STEPS + k] for k in range(STEPS)] for tracer in range(tracers)]
    send_surface(late, [values[1] for values in late], planes_ref, table_ref, send_ref, deep_rows)


def first_send_kernel(pack_ref, south_ref, static_in, send_ref, static_ref, *, tracers):
    for k in range(2):
        static_ref[SOUTH + k] = south_ref[k]
    devices = send_ref.shape[0] // 2
    rows, cols = static_in.shape[1:]
    factor = static_in[MERIDIONAL, 0:1, :]
    lines = []
    for tracer in range(tracers):
        north = [factor * static_in[LATE + tracer * STEPS + k, 0:1, :] for k in range(2)]
        lines.append(south_ref[0, rows - 1 : rows] * north[0] + south_ref[1, rows - 1 : rows] * north[1])
    row = row_iota((2 * SLAB, cols))
    edge = jnp.where(row == SLAB - 2, lines[0], jnp.where(row == 2 * SLAB - 2, lines[1], 0.0))
    model = Place().model
    for device in range(devices):
        there = (1 - model) * devices + device
        send_ref[there] = pack_ref[there] + edge
        here = model * devices + device
        send_ref[here] = pack_ref[here]


def exchange_kernel(static_in, recv_ref, table_ref, *refs, step, tracers, count, deep_rows, unread=0):
    early_ref, refs = (refs[0], refs[1:]) if step >= 2 else (None, refs)
    refs = refs[unread:]
    static_in = static_in if step == STEPS - 1 else refs[0]
    late = [[static_in[LATE + tracer * STEPS + k] for k in range(count)] for tracer in range(tracers)]
    early = [early_levels(step, early_ref, tracer, tracers) for tracer in range(tracers)]
    stepped = upper_levels(recv_ref, late, early, static_in)
    surface = [values[0] for values in stepped]
    surface = receive_surface(recv_ref, table_ref, static_in, surface)
    for tracer in range(tracers):
        stepped[tracer][0] = surface[tracer]
    if step == STEPS - 1:
        (out_ref,) = refs
        for tracer in range(tracers):
            for k in range(STEPS):
                out_ref[tracer, k] = stepped[tracer][k]
        return
    static_ref, send_ref = refs
    for tracer in range(tracers):
        for k, value in enumerate(stepped[tracer]):
            static_ref[LATE + tracer * STEPS + k] = value
    send_surface(stepped, [values[1] for values in stepped], static_in, table_ref, send_ref, deep_rows)


def whole(array):
    zeros = (0,) * array.ndim
    return pl.BlockSpec(array.shape, lambda i: zeros)


def top(array, levels):
    tracers, _, rows, cols = array.shape
    return pl.BlockSpec((tracers, levels, rows, cols), lambda i: (0, 0, 0, 0))


NEAR = pl.BlockSpec(memory_space=pltpu.VMEM)
FAR = pl.BlockSpec(memory_space=pltpu.HBM)
UNREAD = pl.BlockSpec(memory_space=pl.ANY)


def call(kernel, operands, specs, out_shape, out_specs, name, grid=(), aliases=None, scratch=(), us=1, mib=16):
    return pl.pallas_call(
        kernel,
        grid=grid,
        in_specs=specs,
        out_shape=out_shape,
        out_specs=out_specs,
        scratch_shapes=list(scratch),
        input_output_aliases=aliases or {},
        name=name,
        cost_estimate=pl.CostEstimate(flops=0, bytes_accessed=us * 3_000_000, transcendentals=0),
        compiler_params=pltpu.CompilerParams(vmem_limit_bytes=mib * 1024 * 1024),
    )(*operands)


def shaped(*shape):
    return jax.ShapeDtypeStruct(shape, F32)


def tile_order(partner, rows, groups):
    count = rows * groups
    a = lax.broadcasted_iota(jnp.int32, (count, count), 0)
    b = lax.broadcasted_iota(jnp.int32, (count, count), 1)
    turn = (a == (b % rows) * groups + b // rows).astype(BF16)
    both = jnp.concatenate([partner // count, partner % count], axis=0)
    both = jnp.concatenate([both, jnp.zeros((6, count), jnp.int32)], axis=0).astype(F32).astype(BF16)
    lines = jnp.dot(both, turn, preferred_element_type=F32)
    columns = lax.dot_general(turn, both, (((0,), (1,)), ((), ())), preferred_element_type=F32)
    lines, columns = lines.astype(jnp.int32), columns.astype(jnp.int32)
    return lines[0:1], lines[1:2], columns[:, 0:1], columns[:, 1:2]


def write_tables(partner, table_ref, planes_ref, start, rows, groups, n_lat, n_lon):
    count = rows * groups
    devices = n_lat * n_lon
    line_target, line_slot, target, slot = tile_order(partner, rows, groups)
    a = lax.broadcasted_iota(jnp.int32, (count, count), 0)
    b = lax.broadcasted_iota(jnp.int32, (count, count), 1)
    same = target == line_target
    came = jnp.sum((same & (line_slot < slot)).astype(F32), axis=1, keepdims=True).astype(jnp.int32)
    ahead = same & ((a % rows) * groups + a // rows < (b % rows) * groups + b // rows)
    sent = jnp.sum(ahead.astype(F32), axis=0, keepdims=True).astype(jnp.int32)

    row, group = slot // groups, slot % groups
    lat, lon = target // n_lon, target % n_lon
    north_ok = (row == rows - 1) & (lat < n_lat - 1)
    east_ok = group == groups - 1
    east_device = lat * n_lon + (lon + 1) % n_lon
    picks = (
        target * SLAB + came // groups,
        jnp.where(north_ok, (target + n_lon) * SLAB + SLAB - 2, -1),
        jnp.where(east_ok, east_device * SLAB + SLAB - 1, -1),
        jnp.where(east_ok, target * SLAB + SLAB - 1, -1),
    )
    index = lax.broadcasted_iota(jnp.int32, (count, table_ref.shape[1]), 1)
    for kind, pick in enumerate(picks):
        table_ref[kind * count : (kind + 1) * count, :] = (pick == index).astype(F32).astype(BF16)
    height = devices * SLAB
    packing = (sent % groups) * height + line_target * SLAB + sent // groups
    slots = lax.broadcasted_iota(jnp.int32, (groups * height, count), 0)
    table_ref[4 * count :, 0:count] = (slots == packing).astype(F32).astype(BF16)
    if table_ref.shape[1] > count:
        table_ref[4 * count :, count:] = jnp.zeros((groups * height, table_ref.shape[1] - count), BF16)

    lane = lax.broadcasted_iota(jnp.int32, (count, groups * TILE), 1)
    places = (
        lane // TILE == came % groups,
        lane // TILE == group,
        (lane % rows == row) & (lane < 2 * 2 * rows),
    )
    for kind, place in enumerate(places):
        place = place.astype(F32)
        for c in range(groups):
            planes_ref[start + kind * groups + c] = place[c * rows : (c + 1) * rows]


def prepare_kernel(*refs, n_lat, n_lon):
    fields, kappa, courant, share_ref, wet_share_ref, partner, table_ref, planes_ref, sems = refs
    tracers, _, rows, cols = fields.shape
    sources = [(kappa.at[0:STEPS], KAPPA, STEPS)]
    sources += [(fields.at[tracer, 0:STEPS], LATE + tracer * STEPS, STEPS) for tracer in range(tracers)]
    copies = [
        pltpu.make_async_copy(source, planes_ref.at[plane : plane + planes], sems.at[i])
        for i, (source, plane, planes) in enumerate(sources)
    ]
    for copy in copies:
        copy.start()
    write_tables(partner[...], table_ref, planes_ref, LATE + tracers * STEPS, rows, cols // TILE, n_lat, n_lon)
    planes_ref[ZONAL] = courant[0]
    planes_ref[MERIDIONAL] = courant[1]
    planes_ref[COUPLING] = share_ref[0] + share_ref[1]
    planes_ref[WET] = (wet_share_ref[...] > 0).astype(F32)
    for k in (SOUTH, SOUTH + 1):
        planes_ref[k] = jnp.zeros((rows, cols), F32)
    for copy in copies:
        copy.wait()


def corner_kernel(after_ref, east_ref, rows_in, rows_ref, sems):
    cols = rows_ref.shape[2]
    tiles = east_ref.shape[1] // cols
    copies = [
        pltpu.make_async_copy(
            east_ref.at[0 : 2 * STEPS, tile * cols : (tile + 1) * cols],
            rows_ref.at[rows_ref.shape[0] - tiles + tile],
            sems.at[tile],
        )
        for tile in range(tiles)
    ]
    for copy in copies:
        copy.start()
    for copy in copies:
        copy.wait()


def halo_kernel(after_ref, fields_ref, kappa_ref, courant_ref, rows_ref, columns_ref):
    pack_halo(fields_ref, kappa_ref, courant_ref, rows_ref, columns_ref)


def local(adjoint, courant, diffusivity, coupling, partner, mask):
    fields = adjoint[0]
    courant, kappa, coupling, mask = courant[0], diffusivity[0], coupling[0], mask[0]
    tracers, levels, rows, cols = fields.shape
    groups = cols // TILE
    count = rows * groups
    n_lat, n_lon = lax.axis_size("lat"), lax.axis_size("lon")
    devices = n_lat * n_lon

    share = jnp.stack([coupling * (1.0 - kappa[0]), coupling * kappa[0]])
    wet_share = mask.astype(F32) * coupling
    from_south = lax.ppermute(share, "lat", [(i, (i + 1) % n_lat) for i in range(n_lat)])

    def exchanged(send):
        return lax.all_to_all(send, ("mp", "lat", "lon"), split_axis=0, concat_axis=0, tiled=True)

    deep_rows = 4 * count
    width = ((tracers + 1) * -(-levels // PACKED) + 2) * cols
    table_shape = jax.ShapeDtypeStruct(
        (deep_rows + groups * devices * SLAB, max(count, devices * SLAB)), BF16
    )
    planes_shape = shaped(LATE + tracers * STEPS + 3 * groups, rows, cols)
    north_shape = shaped((tracers + 1) * (levels // 2) + 1 + width // cols, 2 * STEPS, cols)
    table, planes = call(
        functools.partial(prepare_kernel, n_lat=n_lat, n_lon=n_lon),
        (fields, kappa, courant, share, wet_share, partner),
        [FAR, FAR, NEAR, NEAR, NEAR, NEAR],
        (table_shape, planes_shape),
        (NEAR, NEAR),
        "prepare",
        scratch=[pltpu.SemaphoreType.DMA((1 + tracers,))],
        us=2,
        mib=53,
    )
    send_shape = shaped(2 * devices, 2 * SLAB, cols)
    pack = call(
        functools.partial(first_pack_kernel, tracers=tracers, deep_rows=deep_rows),
        (table, planes),
        [NEAR, NEAR],
        send_shape,
        NEAR,
        "first_pack",
    )
    send, planes = call(
        functools.partial(first_send_kernel, tracers=tracers),
        (pack, from_south, planes),
        [NEAR, NEAR, NEAR],
        (send_shape, planes_shape),
        (NEAR, NEAR),
        "first_send",
        aliases={2: 1},
    )
    recv = exchanged(send)
    halo_shapes = (north_shape, shaped(rows, width))
    north, east = call(
        halo_kernel,
        (send, fields, kappa, courant),
        [UNREAD, *(whole(a) for a in (fields, kappa, courant))],
        halo_shapes,
        tuple(whole(a) for a in halo_shapes),
        "halo",
        grid=(1,),
        us=2,
        mib=53,
    )
    east = lax.ppermute(east, "lon", [((i + 1) % n_lon, i) for i in range(n_lon)])
    tall = rows + 2 * STEPS

    def deep_levels(tracer, before, halo):
        block = pl.BlockSpec((1, levels, rows, cols), lambda i: (tracer, 0, 0, 0))
        token = shaped(8, cols)
        return call(
            functools.partial(deep_kernel, tracer=tracer, tracers=tracers),
            (send, fields, *before, *halo),
            [UNREAD, block, *(UNREAD for _ in before), *(whole(a) for a in halo)],
            (shaped(*fields.shape), token),
            (block, whole(token)),
            "deep_levels",
            grid=(1,),
            aliases={2: 0} if before else None,
            scratch=[pltpu.VMEM((levels, tall, cols), F32)],
            us=4,
        )

    reached = (STEPS, STEPS - 1, 2, 3)
    for step in range(STEPS):
        if step > 0:
            recv = exchanged(send)
        kernel = functools.partial(
            exchange_kernel, step=step, tracers=tracers, count=reached[step], deep_rows=deep_rows
        )
        operands = (planes, recv, table)
        if step == 0:
            planes, send = call(
                kernel, operands, [NEAR] * 3, (planes_shape, send_shape), (NEAR, NEAR), "exchange", aliases={0: 0}
            )
            north = call(
                corner_kernel,
                (send, east, north),
                [UNREAD, NEAR, UNREAD],
                north_shape,
                UNREAD,
                "corner",
                aliases={2: 0},
                scratch=[pltpu.SemaphoreType.DMA((width // cols,))],
            )
            north = lax.ppermute(north, "lat", [((i + 1) % n_lat, i) for i in range(n_lat)])
            halo = (kappa, courant, north, east)
        if step == 1:
            planes, send = call(
                kernel, operands, [NEAR] * 3, (planes_shape, send_shape), (NEAR, NEAR), "exchange", aliases={0: 0}
            )
        if step == 2:
            early_shape = shaped((STEPS - 2) * tracers * 4 + 1, rows, cols)
            early = call(
                functools.partial(early_kernel, all_levels=levels),
                (fields, *halo),
                [
                    top(fields, UPPER),
                    pl.BlockSpec((UPPER, rows, cols), lambda i: (0, 0, 0)),
                    *(whole(a) for a in halo[1:]),
                ],
                early_shape,
                whole(early_shape),
                "early_levels",
                grid=(1,),
                scratch=[pltpu.VMEM((UPPER, tall, cols), F32)],
                us=2,
            )
            out, token = deep_levels(0, (), halo)
            planes, send = call(
                functools.partial(kernel, unread=1),
                (*operands, early, token),
                [*[NEAR] * 4, UNREAD],
                (planes_shape, send_shape),
                (NEAR, NEAR),
                "exchange",
                aliases={0: 0},
            )
        if step == 3:
            for tracer in range(1, tracers):
                out, token = deep_levels(tracer, (out,), halo)
            operands = (*operands, early)
            return call(
                functools.partial(kernel, unread=1),
                (*operands, out),
                [*(whole(a) for a in operands), UNREAD],
                shaped(*fields.shape),
                top(fields, STEPS),
                "last_exchange",
                grid=(1,),
                aliases={len(operands): 0},
            )[None]


def solution(mesh):
    placed = (
        P("mp", None, None, "lat", "lon"),
        P("mp", None, "lat", "lon"),
        P("mp", None, "lat", "lon"),
        P("mp", "lat", "lon"),
        P("mp", ("lat", "lon")),
        P("mp", "lat", "lon"),
    )
    return jax.shard_map(
        local,
        mesh=mesh,
        in_specs=placed,
        out_specs=P("mp", None, None, "lat", "lon"),
        check_vma=False,
    )
```

```python
import functools

import jax
import jax.numpy as jnp
from jax import lax
from jax.experimental import pallas as pl
from jax.experimental.pallas import tpu as pltpu
from jax.sharding import PartitionSpec as P

TILE = 16
STEPS = 4
F32 = jnp.float32
BF16 = jnp.bfloat16
UPPER = 8
PARTS = 2
PACKED = 32
SLAB = 4
ZONAL, MERIDIONAL, KAPPA = 0, 1, 2
COUPLING = KAPPA + STEPS
WET = COUPLING + 1
SOUTH = WET + 1
LATE = SOUTH + 2


class Place:
    def __init__(self):
        n_lat, n_lon = lax.axis_size("lat"), lax.axis_size("lon")
        lat, lon = lax.axis_index("lat"), lax.axis_index("lon")
        self.model = lax.axis_index("mp")
        self.east = lat * n_lon + lax.rem(lon + 1, n_lon)
        self.west = lat * n_lon + lax.rem(lon + n_lon - 1, n_lon)
        self.north = lax.rem(lat + 1, n_lat) * n_lon + lon
        self.has_north = lat < n_lat - 1


def lane_iota(shape):
    return lax.broadcasted_iota(jnp.int32, shape, len(shape) - 1)


def row_iota(shape):
    return lax.broadcasted_iota(jnp.int32, shape, len(shape) - 2)


def lane_roll(value, shift):
    shift = shift % value.shape[-1]
    return value if shift == 0 else pltpu.roll(value, shift, 1)


def next_row(value):
    return pltpu.roll(value, value.shape[0] - 1, 0)


def three_parts(value):
    high = value.astype(BF16)
    rest = value - high.astype(F32)
    middle = rest.astype(BF16)
    low = (rest - middle.astype(F32)).astype(BF16)
    return high, middle, low


def picked(one_hot, value):
    return jnp.dot(one_hot, jnp.concatenate(three_parts(value), axis=0), preferred_element_type=F32)


def spread_by(value, one_hot):
    one_hot = jnp.concatenate([one_hot] * 3, axis=0)
    return jnp.dot(jnp.concatenate(three_parts(value), axis=1), one_hot, preferred_element_type=F32)


def pack_halo(fields_ref, kappa_ref, courant_ref, rows_ref, columns_ref):
    tracers, levels, rows, cols = fields_ref.shape
    lane = lane_iota((rows, cols))
    upper = row_iota((2 * STEPS, cols)) < STEPS
    pairs = levels // 2

    def first_rows(read, count, which):
        for pair in range(pairs):
            one = read(2 * pair)
            two = read(2 * pair + 1) if 2 * pair + 1 < count else jnp.zeros_like(one)
            rows_ref[which * pairs + pair] = jnp.where(upper, one, pltpu.roll(two, STEPS, 0))

    def first_columns(read, count, start):
        for tile in range(-(-levels // PACKED)):
            gathered = jnp.zeros((rows, cols), F32)
            for k in range(tile * PACKED, min((tile + 1) * PACKED, count)):
                place = k % PACKED
                gathered = jnp.where(lane // STEPS == place, lane_roll(read(k), place * STEPS), gathered)
            spot = slice((start + tile) * cols, (start + tile + 1) * cols)
            columns_ref[:, spot] = gathered

    tiles = -(-levels // PACKED)
    for tracer in range(tracers):
        first_rows(lambda k: fields_ref[tracer, k, 0 : 2 * STEPS, :], levels, tracer)
        first_columns(lambda k: fields_ref[tracer, k], levels, tracer * tiles)
    first_rows(lambda k: kappa_ref[k, 0 : 2 * STEPS, :], levels - 1, tracers)
    first_columns(lambda k: kappa_ref[k], levels - 1, tracers * tiles)
    rows_ref[(tracers + 1) * pairs] = jnp.where(
        upper,
        courant_ref[0, 0 : 2 * STEPS, :],
        pltpu.roll(courant_ref[1, 0 : 2 * STEPS, :], STEPS, 0),
    )
    for which in range(2):
        repeated = jnp.where(lane < STEPS, courant_ref[which], 0.0)
        shift = STEPS
        while shift < cols:
            repeated = repeated + lane_roll(repeated, shift)
            shift *= 2
        spot = slice(((tracers + 1) * tiles + which) * cols, ((tracers + 1) * tiles + which + 1) * cols)
        columns_ref[:, spot] = repeated


def wide_steps(refs, tracer, levels, tracers, all_levels, first_field, store, each_step):
    kappa_ref, courant_ref, rows_ref, columns_ref, state = refs
    rows, cols = courant_ref.shape[1:]
    pairs = all_levels // 2
    tiles = -(-all_levels // PACKED)
    used = -(-levels // PACKED)
    tall = rows + 2 * STEPS
    has_north = Place().has_north
    lane = lane_iota((tall, cols))

    def with_rows(block, which, k):
        extra = rows_ref[which * pairs + k // 2]
        if k % 2:
            extra = pltpu.roll(extra, STEPS, 0)
        return jnp.concatenate([block, jnp.where(has_north, extra, 0.0)], axis=0)

    def strip(index):
        spot = slice(index * cols, (index + 1) * cols)
        corner = jnp.where(has_north, rows_ref[(tracers + 1) * pairs + 1 + index], 0.0)
        return jnp.concatenate([columns_ref[:, spot], corner], axis=0)

    last = rows_ref[(tracers + 1) * pairs]
    last = jnp.where(has_north, last, 0.0)
    zonal = jnp.concatenate([courant_ref[0], last], axis=0)
    meridional = jnp.concatenate([courant_ref[1], pltpu.roll(last, STEPS, 0)], axis=0)
    weight = (1.0 - zonal) - meridional
    side_zonal = strip((tracers + 1) * tiles)
    side_meridional = strip((tracers + 1) * tiles + 1)
    side_weight = (1.0 - side_zonal) - side_meridional
    side = [strip(tracer * tiles + i) for i in range(used)]
    side_kappa = [strip(tracers * tiles + i) for i in range(used)]
    end = (levels - (used - 1) * PACKED) * STEPS
    if levels < all_levels:
        side_kappa[-1] = jnp.where(lane < end, side_kappa[-1], 0.0)

    def lanes_on(tiles_in, shift):
        out = []
        for i, tile in enumerate(tiles_in):
            turned = lane_roll(tile, -shift)
            other = tiles_in[(i + 1 if shift > 0 else i - 1) % len(tiles_in)]
            if len(tiles_in) > 1:
                inside = lane < cols - shift if shift > 0 else lane >= -shift
                turned = jnp.where(inside, turned, lane_roll(other, -shift))
            out.append(turned)
        return out

    for step in range(STEPS):
        height = rows if step == STEPS - 1 else tall
        z, m, w = zonal[:height], meridional[:height], weight[:height]
        at_end = lane[:height] == cols - 1
        side_east = [side_zonal * tile for tile in side]

        def field_of(k):
            if step == 0:
                return with_rows(first_field(k), tracer, k)
            return state[k]

        def advected(k):
            field = field_of(k)
            edge = lane_roll(side_east[k // PACKED], cols - 1 - (k % PACKED) * STEPS)
            east = jnp.where(at_end, edge[:height], lane_roll((z * field[:height]), cols - 1))
            north = next_row(meridional * field)[:height]
            return (w * field[:height] + east) + north

        here = advected(0)
        above = None
        for k in range(levels):
            result = here
            if k + 1 < levels:
                below = advected(k + 1)
                kappa = kappa_ref[k]
                if height > rows:
                    kappa = with_rows(kappa, tracers, k)
                flux = kappa * (below - here)
                result = result + flux
            if k > 0:
                result = result - above
            if step == STEPS - 1:
                store(k, result)
            else:
                state[k] = result
            if k + 1 < levels:
                here, above = below, flux
        if step < STEPS - 1:
            east = lanes_on(side_east, 1)
            advected_side = [
                (side_weight * tile + turned) + next_row(side_meridional * tile)
                for tile, turned in zip(side, east)
            ]
            under = lanes_on(advected_side, STEPS)
            fluxes = [kap * (low - adv) for kap, low, adv in zip(side_kappa, under, advected_side)]
            over = lanes_on(fluxes, -STEPS)
            side = [(adv + flux) - up for adv, flux, up in zip(advected_side, fluxes, over)]
            if each_step is not None:
                each_step(step + 1, zonal, meridional, side_zonal, side)


def early_kernel(
    fields_ref, kappa_ref, courant_ref, rows_ref, columns_ref, early_ref, state, *, all_levels
):
    tracers, levels, rows, cols = fields_ref.shape
    refs = (kappa_ref, courant_ref, rows_ref, columns_ref, state)
    for tracer in range(tracers):

        def each_step(step, zonal, meridional, side_zonal, side):
            for j in range(2 if step >= 2 else 0):
                k = step + j
                field = state[k]
                line = ((step - 2) * tracers + tracer) * 2 + j
                early_ref[2 * line] = field[:rows]
                early_ref[2 * line + 1] = lane_roll(side_zonal * side[0], cols - 1 - k * STEPS)[:rows]
                early_ref[early_ref.shape[0] - 1, line : line + 1, :] = (
                    meridional[rows : rows + 1] * field[rows : rows + 1]
                )

        wide_steps(
            refs, tracer, levels, tracers, all_levels,
            lambda k: fields_ref[tracer, k], lambda k, value: None, each_step,
        )


def deep_kernel(after_ref, fields_ref, *refs, tracer, tracers):
    kappa_ref, courant_ref, rows_ref, columns_ref, out_ref, state = refs[-6:]
    levels = fields_ref.shape[1]

    def store(k, value):
        if k >= STEPS:
            out_ref[0, k] = value

    for k in range(STEPS):
        out_ref[0, k] = jnp.zeros(out_ref.shape[2:], F32)
    wide_steps(
        (kappa_ref, courant_ref, rows_ref, columns_ref, state),
        tracer, levels, tracers, levels, lambda k: fields_ref[0, k], store, None,
    )


def send_surface(late, below, static_ref, pack_ref, send_ref, ready):
    here = Place()
    model = here.model
    tracers = len(late)
    zonal, meridional = static_ref[ZONAL], static_ref[MERIDIONAL]
    weight = (1.0 - zonal) - meridional
    rows, cols = zonal.shape
    groups = cols // TILE
    lane = lane_iota((rows, cols))
    row = row_iota((rows, cols))
    kappa = static_ref[KAPPA]
    coupling = static_ref[COUPLING]
    group = lane // TILE
    tiles, edge_north, all_scaled = [], [], []
    share = (coupling * (1.0 - kappa), coupling * kappa)
    raw_east, factors = jnp.zeros((rows, cols), F32), jnp.zeros((rows, cols), F32)
    south_a, south_b = static_ref[SOUTH], static_ref[SOUTH + 1]
    own_north, own_east = [], jnp.zeros((rows, cols), F32)
    for tracer in range(tracers):
        parts = []
        for field in (late[tracer][0], below[tracer]):
            eastward, northward = zonal * field, meridional * field
            east = jnp.where(lane == cols - 1, 0.0, lane_roll(eastward, cols - 1))
            north = jnp.where(row == rows - 1, 0.0, next_row(northward))
            parts.append((eastward, northward, (weight * field + east) + north))
        (east0, north0, over), (east1, north1, under) = parts
        mixed = over + kappa * (under - over)
        all_scaled.append(coupling * mixed)
        edge_north.append(south_a[rows - 1 : rows] * north0[0:1] + south_b[rows - 1 : rows] * north1[0:1])
        for level, edge in enumerate((east0, east1)):
            place = lane == (tracer * 2 + level) * rows + row
            raw_east = jnp.where(place, jnp.broadcast_to(edge[:, 0:1], (rows, cols)), raw_east)
            factor = jnp.broadcast_to(share[level][:, cols - 1 : cols], (rows, cols))
            factors = jnp.where(place, factor, factors)
        for k, field in enumerate(late[tracer]):
            own_north.append(meridional[0:1] * field[0:1])
            column = jnp.broadcast_to((zonal * field)[:, 0:1], (rows, cols))
            spot = (tracer * len(late[tracer]) + k) * rows + row
            own_east = jnp.where(lane == spot, column, own_east)
    devices = send_ref.shape[0] // 2
    empty = [jnp.zeros((1, cols), F32)] * (2 * SLAB - 1)
    own_north = jnp.concatenate((own_north + empty)[: 2 * SLAB], axis=0)
    own_east = jnp.concatenate(empty + [jnp.sum(own_east, axis=0, keepdims=True)], axis=0)
    for device in range(devices):
        send_ref[model * devices + device] = own_north
    send_ref[model * devices + here.west] = own_east
    ready(0, model * devices)
    for scaled in all_scaled:
        blocks = []
        for c in range(groups):
            block = jnp.where(group == c, scaled, 0.0)
            shift = TILE
            while shift < cols:
                block = block + lane_roll(block, shift)
                shift *= 2
            blocks.append(block)
        tiles.append(jnp.concatenate(blocks, axis=0))
    edge_east = [jnp.sum(edge, axis=0, keepdims=True) for edge in (raw_east, factors)]
    empty = jnp.zeros((SLAB - 2, cols), F32)
    edges = jnp.concatenate(
        [empty, edge_north[0], edge_east[0], empty, edge_north[1], edge_east[1]], axis=0
    )
    table = jnp.concatenate(three_parts(jnp.concatenate(tiles, axis=1)), axis=0)
    height = pack_ref.shape[0] // (groups * PARTS)
    main_rows = height * PARTS // devices
    slot_group = (lane_iota((height, tracers * cols)) % cols) // TILE
    line = row_iota((2 * SLAB, cols))
    for part in range(PARTS):
        start = part * groups * height
        slots = jnp.dot(
            pack_ref[start : start + groups * height, :], table, preferred_element_type=F32
        )
        packed = jnp.zeros((height, tracers * cols), F32)
        for g in range(groups):
            packed = jnp.where(slot_group == g, slots[g * height : (g + 1) * height], packed)
        there = (1 - model) * devices + part * (devices // PARTS)
        for device in range(devices // PARTS):
            block = edges
            first, offset = (device * main_rows) // 8 * 8, (device * main_rows) % 8
            for tracer in range(tracers):
                rows8 = packed[first : first + 8, tracer * cols : (tracer + 1) * cols]
                shift = (tracer * SLAB - offset) % 8
                rows8 = pltpu.roll(rows8, shift, 0) if shift else rows8
                here_rows = (line >= tracer * SLAB) & (line < tracer * SLAB + main_rows)
                block = jnp.where(here_rows, rows8, block)
            send_ref[there + device] = block
        ready(1 + part, there)


def receive_surface(recv_ref, pick_ref, static_ref, surface):
    devices = recv_ref.shape[0] // 2
    rows, cols = surface[0].shape
    groups = cols // TILE
    tracers = len(surface)
    count = rows * groups
    other = (1 - Place().model) * devices
    upper = row_iota((2 * SLAB, cols)) < SLAB
    first, second = [], []
    for pair in range(devices // 2):
        one, two = recv_ref[other + 2 * pair], recv_ref[other + 2 * pair + 1]
        first.append(jnp.where(upper, one, pltpu.roll(two, SLAB, 0)))
        second.append(jnp.where(upper, pltpu.roll(one, SLAB, 0), two))
    slab = jnp.concatenate([jnp.concatenate(half, axis=0) for half in (first, second)], axis=1)
    found = picked(pick_ref[...], slab)

    def place(kind):
        start = LATE + tracers * STEPS + kind * groups
        return static_ref[start : start + groups].reshape(count, cols) > 0

    edge = found[2 * count : 3 * count, :cols] * found[3 * count :, cols:]
    edge = jnp.where(place(2), edge, 0.0)
    shape = (cols, tracers * cols)
    source, lane = row_iota(shape), lane_iota(shape)
    spread = (source // (2 * rows) == lane // cols) & (lane % TILE == TILE - 1)
    edge = spread_by(edge, spread.astype(F32).astype(BF16))
    main, north = place(0), place(1)
    group = lane_iota((rows, cols)) // TILE
    wet, coupling = static_ref[WET], static_ref[COUPLING]
    updated = []
    for tracer in range(tracers):
        spot = slice(tracer * cols, (tracer + 1) * cols)
        total = jnp.where(main, found[:count, spot], 0.0) + jnp.where(north, found[count : 2 * count, spot], 0.0)
        shift = TILE
        while shift < cols:
            total = total + lane_roll(total, shift)
            shift *= 2
        total = total + edge[:, spot]
        received = jnp.zeros((rows, cols), F32)
        for c in range(groups):
            received = jnp.where(group == c, total[c * rows : (c + 1) * rows], received)
        own = surface[tracer]
        updated.append(own + wet * (received - coupling * own))
    return updated


def upper_levels(recv_ref, late, early, static_ref):
    zonal, meridional = static_ref[ZONAL], static_ref[MERIDIONAL]
    weight = (1.0 - zonal) - meridional
    rows, cols = zonal.shape
    lane = lane_iota((rows, cols))
    row = row_iota((rows, cols))
    devices = recv_ref.shape[0] // 2
    here = Place()
    mine = here.model * devices
    from_east = recv_ref[mine + here.east]
    from_north = jnp.where(here.has_north, recv_ref[mine + here.north], 0.0)
    east_line = jnp.broadcast_to(from_east[from_east.shape[0] - 1 :], (rows, cols))
    stepped = []
    for tracer in range(len(late)):
        count = len(late[tracer])
        moved = []
        for k in range(count + len(early[tracer])):
            if k < count:
                field = late[tracer][k]
                index = tracer * count + k
                north_edge = from_north[index : index + 1]
                column = jnp.where(lane == index * rows + row, east_line, 0.0)
                east_edge = jnp.sum(column, axis=1, keepdims=True)
            else:
                field, north_edge, east_edge = early[tracer][k - count]
            east = jnp.where(lane == cols - 1, east_edge, lane_roll(zonal * field, cols - 1))
            north = jnp.where(row == rows - 1, north_edge, next_row(meridional * field))
            moved.append((weight * field + east) + north)
        out, above = [], None
        for k in range(len(moved) - 1):
            flux = static_ref[KAPPA + k] * (moved[k + 1] - moved[k])
            result = moved[k] + flux
            if k > 0:
                result = result - above
            out.append(result)
            above = flux
        stepped.append(out)
    return stepped


def early_levels(step, early_ref, tracer, tracers):
    if step < 2:
        return []
    found = []
    for j in range(2):
        line = ((step - 2) * tracers + tracer) * 2 + j
        norths = early_ref[early_ref.shape[0] - 1]
        found.append((early_ref[2 * line], norths[line : line + 1], early_ref[2 * line + 1]))
    return found


def first_pack_kernel(pack_ref, planes_ref, send_ref, *, tracers):
    late = [[planes_ref[LATE + tracer * STEPS + k] for k in range(STEPS)] for tracer in range(tracers)]
    send_surface(late, [values[1] for values in late], planes_ref, pack_ref, send_ref, lambda part, first: None)


def first_send_kernel(pack_ref, south_ref, static_in, send_ref, static_ref, *, tracers):
    for k in range(2):
        static_ref[SOUTH + k] = south_ref[k]
    devices = send_ref.shape[0] // 2
    rows, cols = static_in.shape[1:]
    factor = static_in[MERIDIONAL, 0:1, :]
    lines = []
    for tracer in range(tracers):
        north = [factor * static_in[LATE + tracer * STEPS + k, 0:1, :] for k in range(2)]
        lines.append(south_ref[0, rows - 1 : rows] * north[0] + south_ref[1, rows - 1 : rows] * north[1])
    row = row_iota((2 * SLAB, cols))
    edge = jnp.where(row == SLAB - 2, lines[0], jnp.where(row == 2 * SLAB - 2, lines[1], 0.0))
    model = Place().model
    for device in range(devices):
        there = (1 - model) * devices + device
        send_ref[there] = pack_ref[there] + edge
        here = model * devices + device
        send_ref[here] = pack_ref[here]


def exchange_kernel(
    static_in, recv_ref, pick_ref, pack_ref, *refs, step, tracers, count, unread=0
):
    early_ref, refs = (refs[0], refs[1:]) if step >= 2 else (None, refs)
    refs = refs[unread:]
    last = step == STEPS - 1
    refs = refs if last else refs[1:]
    static_ref = static_in if last else refs[0]
    late = [[static_ref[LATE + tracer * STEPS + k] for k in range(count)] for tracer in range(tracers)]
    early = [early_levels(step, early_ref, tracer, tracers) for tracer in range(tracers)]
    stepped = upper_levels(recv_ref, late, early, static_ref)
    surface = [values[0] for values in stepped]
    surface = receive_surface(recv_ref, pick_ref, static_ref, surface)
    for tracer in range(tracers):
        stepped[tracer][0] = surface[tracer]
    if last:
        (out_ref,) = refs
        for tracer in range(tracers):
            for k in range(STEPS):
                out_ref[tracer, k] = stepped[tracer][k]
        return
    _, send_ref, blocks_ref, sems = refs
    for tracer in range(tracers):
        for k, value in enumerate(stepped[tracer]):
            static_ref[LATE + tracer * STEPS + k] = value
    copies = []

    def ready(part, first):
        size = blocks_ref.shape[0] // (2 if part == 0 else 2 * PARTS)
        copies.append(
            pltpu.make_async_copy(
                blocks_ref.at[pl.ds(first, size)], send_ref.at[pl.ds(first, size)], sems.at[part]
            )
        )
        copies[-1].start()

    send_surface(stepped, [values[1] for values in stepped], static_ref, pack_ref, blocks_ref, ready)
    for copy in copies:
        copy.wait()


def whole(array):
    zeros = (0,) * array.ndim
    return pl.BlockSpec(array.shape, lambda i: zeros)


def top(array, levels):
    tracers, _, rows, cols = array.shape
    return pl.BlockSpec((tracers, levels, rows, cols), lambda i: (0, 0, 0, 0))


NEAR = pl.BlockSpec(memory_space=pltpu.VMEM)
FAR = pl.BlockSpec(memory_space=pltpu.HBM)
UNREAD = pl.BlockSpec(memory_space=pl.ANY)


def call(kernel, operands, specs, out_shape, out_specs, name, grid=(), aliases=None, scratch=(), us=1, mib=16):
    return pl.pallas_call(
        kernel,
        grid=grid,
        in_specs=specs,
        out_shape=out_shape,
        out_specs=out_specs,
        scratch_shapes=list(scratch),
        input_output_aliases=aliases or {},
        name=name,
        cost_estimate=pl.CostEstimate(flops=0, bytes_accessed=us * 3_000_000, transcendentals=0),
        compiler_params=pltpu.CompilerParams(vmem_limit_bytes=int(mib * 1024 * 1024)),
    )(*operands)


def shaped(*shape):
    return jax.ShapeDtypeStruct(shape, F32)


def tile_order(partner, rows, groups):
    count = rows * groups
    a = lax.broadcasted_iota(jnp.int32, (count, count), 0)
    b = lax.broadcasted_iota(jnp.int32, (count, count), 1)
    turn = (a == (b % rows) * groups + b // rows).astype(BF16)
    both = jnp.concatenate([partner // count, partner % count], axis=0)
    both = jnp.concatenate([both, jnp.zeros((6, count), jnp.int32)], axis=0).astype(F32).astype(BF16)
    lines = jnp.dot(both, turn, preferred_element_type=F32)
    columns = lax.dot_general(turn, both, (((0,), (1,)), ((), ())), preferred_element_type=F32)
    lines, columns = lines.astype(jnp.int32), columns.astype(jnp.int32)
    return lines[0:1], lines[1:2], columns[:, 0:1], columns[:, 1:2]


def write_tables(partner, pick_ref, pack_ref, planes_ref, start, rows, groups, n_lat, n_lon):
    count = rows * groups
    devices = n_lat * n_lon
    line_target, line_slot, target, slot = tile_order(partner, rows, groups)
    a = lax.broadcasted_iota(jnp.int32, (count, count), 0)
    b = lax.broadcasted_iota(jnp.int32, (count, count), 1)
    same = target == line_target
    came = jnp.sum((same & (line_slot < slot)).astype(F32), axis=1, keepdims=True).astype(jnp.int32)
    ahead = same & ((a % rows) * groups + a // rows < (b % rows) * groups + b // rows)
    sent = jnp.sum(ahead.astype(F32), axis=0, keepdims=True).astype(jnp.int32)

    row, group = slot // groups, slot % groups
    lat, lon = target // n_lon, target % n_lon
    north_ok = (row == rows - 1) & (lat < n_lat - 1)
    east_ok = group == groups - 1
    east_device = lat * n_lon + (lon + 1) % n_lon
    picks = (
        target * SLAB + came // groups,
        jnp.where(north_ok, (target + n_lon) * SLAB + SLAB - 2, -1),
        jnp.where(east_ok, east_device * SLAB + SLAB - 1, -1),
        jnp.where(east_ok, target * SLAB + SLAB - 1, -1),
    )
    index = lax.broadcasted_iota(jnp.int32, (count, pick_ref.shape[1]), 1) % (devices * SLAB)
    for kind, pick in enumerate(picks):
        pick_ref[kind * count : (kind + 1) * count, :] = (pick == index).astype(F32).astype(BF16)
    height = pack_ref.shape[0] // (groups * PARTS)
    main_rows = height * PARTS // devices
    per_part = devices // PARTS
    packing = (line_target // per_part) * (groups * height) + (sent % groups) * height
    packing = packing + (line_target % per_part) * main_rows + sent // groups
    slots = lax.broadcasted_iota(jnp.int32, (pack_ref.shape[0], count), 0)
    packing = (slots == packing).astype(F32).astype(BF16)
    for i in range(3):
        pack_ref[:, i * count : (i + 1) * count] = packing

    lane = lax.broadcasted_iota(jnp.int32, (count, groups * TILE), 1)
    places = (
        lane // TILE == came % groups,
        lane // TILE == group,
        (lane % rows == row) & (lane < 2 * 2 * rows),
    )
    for kind, place in enumerate(places):
        place = place.astype(F32)
        for c in range(groups):
            planes_ref[start + kind * groups + c] = place[c * rows : (c + 1) * rows]


def prepare_kernel(*refs, n_lat, n_lon):
    fields, kappa, courant, share_ref, wet_share_ref, partner, *tables, planes_ref, sems = refs
    tracers, _, rows, cols = fields.shape
    sources = [(kappa.at[0:STEPS], KAPPA, STEPS)]
    sources += [(fields.at[tracer, 0:STEPS], LATE + tracer * STEPS, STEPS) for tracer in range(tracers)]
    copies = [
        pltpu.make_async_copy(source, planes_ref.at[plane : plane + planes], sems.at[i])
        for i, (source, plane, planes) in enumerate(sources)
    ]
    for copy in copies:
        copy.start()
    write_tables(partner[...], *tables, planes_ref, LATE + tracers * STEPS, rows, cols // TILE, n_lat, n_lon)
    planes_ref[ZONAL] = courant[0]
    planes_ref[MERIDIONAL] = courant[1]
    planes_ref[COUPLING] = share_ref[0] + share_ref[1]
    planes_ref[WET] = (wet_share_ref[...] > 0).astype(F32)
    for k in (SOUTH, SOUTH + 1):
        planes_ref[k] = jnp.zeros((rows, cols), F32)
    for copy in copies:
        copy.wait()


def corner_kernel(after_ref, east_ref, rows_in, rows_ref, sems):
    cols = rows_ref.shape[2]
    tiles = east_ref.shape[1] // cols
    copies = [
        pltpu.make_async_copy(
            east_ref.at[0 : 2 * STEPS, tile * cols : (tile + 1) * cols],
            rows_ref.at[rows_ref.shape[0] - tiles + tile],
            sems.at[tile],
        )
        for tile in range(tiles)
    ]
    for copy in copies:
        copy.start()
    for copy in copies:
        copy.wait()


def halo_kernel(after_ref, fields_ref, kappa_ref, courant_ref, rows_ref, columns_ref):
    pack_halo(fields_ref, kappa_ref, courant_ref, rows_ref, columns_ref)


def local(adjoint, courant, diffusivity, coupling, partner, mask):
    fields = adjoint[0]
    courant, kappa, coupling, mask = courant[0], diffusivity[0], coupling[0], mask[0]
    tracers, levels, rows, cols = fields.shape
    groups = cols // TILE
    count = rows * groups
    n_lat, n_lon = lax.axis_size("lat"), lax.axis_size("lon")
    devices = n_lat * n_lon

    share = jnp.stack([coupling * (1.0 - kappa[0]), coupling * kappa[0]])
    wet_share = mask.astype(F32) * coupling
    from_south = lax.ppermute(share, "lat", [(i, (i + 1) % n_lat) for i in range(n_lat)])

    def exchanged(send):
        return lax.all_to_all(send, ("mp", "lat", "lon"), split_axis=0, concat_axis=0, tiled=True)

    main_rows = -(-max(2, 2 * count // devices) // groups)
    width = ((tracers + 1) * -(-levels // PACKED) + 2) * cols
    table_shapes = (
        jax.ShapeDtypeStruct((4 * count, 3 * devices * SLAB), BF16),
        jax.ShapeDtypeStruct((groups * devices * main_rows, 3 * count), BF16),
    )
    planes_shape = shaped(LATE + tracers * STEPS + 3 * groups, rows, cols)
    north_shape = shaped((tracers + 1) * (levels // 2) + 1 + width // cols, 2 * STEPS, cols)
    *tables, planes = call(
        functools.partial(prepare_kernel, n_lat=n_lat, n_lon=n_lon),
        (fields, kappa, courant, share, wet_share, partner),
        [FAR, FAR, NEAR, NEAR, NEAR, NEAR],
        (*table_shapes, planes_shape),
        (NEAR, NEAR, NEAR),
        "prepare",
        scratch=[pltpu.SemaphoreType.DMA((1 + tracers,))],
        us=2,
        mib=53,
    )
    send_shape = shaped(2 * devices, 2 * SLAB, cols)
    pack = call(
        functools.partial(first_pack_kernel, tracers=tracers),
        (tables[1], planes),
        [NEAR, NEAR],
        send_shape,
        NEAR,
        "first_pack",
    )
    send, planes = call(
        functools.partial(first_send_kernel, tracers=tracers),
        (pack, from_south, planes),
        [NEAR, NEAR, NEAR],
        (send_shape, planes_shape),
        (NEAR, NEAR),
        "first_send",
        aliases={2: 1},
    )
    recv = exchanged(send)
    halo_shapes = (north_shape, shaped(rows, width))
    north, east = call(
        halo_kernel,
        (send, fields, kappa, courant),
        [UNREAD, *(whole(a) for a in (fields, kappa, courant))],
        halo_shapes,
        tuple(whole(a) for a in halo_shapes),
        "halo",
        grid=(1,),
        us=2,
        mib=53,
    )
    east = lax.ppermute(east, "lon", [((i + 1) % n_lon, i) for i in range(n_lon)])
    tall = rows + 2 * STEPS

    def deep_levels(tracer, before, halo):
        block = pl.BlockSpec((1, levels, rows, cols), lambda i: (tracer, 0, 0, 0))
        return call(
            functools.partial(deep_kernel, tracer=tracer, tracers=tracers),
            (send, fields, *before, *halo),
            [UNREAD, block, *(UNREAD for _ in before), *(whole(a) for a in halo)],
            shaped(*fields.shape),
            block,
            "deep_levels",
            grid=(1,),
            aliases={2: 0} if before else None,
            scratch=[pltpu.VMEM((levels, tall, cols), F32)],
            us=4,
        )

    scratch = [pltpu.VMEM(send_shape.shape, F32), pltpu.SemaphoreType.DMA((1 + PARTS,))]
    reached = (STEPS, STEPS - 1, 2, 3)
    for step in range(STEPS):
        if step > 0:
            recv = exchanged(send)
        kernel = functools.partial(
            exchange_kernel, step=step, tracers=tracers, count=reached[step]
        )
        operands = (planes, recv, *tables)
        if step == 0:
            planes, send = call(
                kernel,
                (*operands, send),
                [*[NEAR] * 4, UNREAD],
                (planes_shape, send_shape),
                (NEAR, UNREAD),
                "exchange",
                aliases={0: 0, 4: 1},
                scratch=scratch,
            )
            north = call(
                corner_kernel,
                (send, east, north),
                [UNREAD, NEAR, UNREAD],
                north_shape,
                UNREAD,
                "corner",
                aliases={2: 0},
                scratch=[pltpu.SemaphoreType.DMA((width // cols,))],
            )
            north = lax.ppermute(north, "lat", [((i + 1) % n_lat, i) for i in range(n_lat)])
            halo = (kappa, courant, north, east)
        if step == 1:
            planes, send = call(
                kernel,
                (*operands, send),
                [*[NEAR] * 4, UNREAD],
                (planes_shape, send_shape),
                (NEAR, UNREAD),
                "exchange",
                aliases={0: 0, 4: 1},
                scratch=scratch,
            )
        if step == 2:
            early_shape = shaped((STEPS - 2) * tracers * 4 + 1, rows, cols)
            early = call(
                functools.partial(early_kernel, all_levels=levels),
                (fields, *halo),
                [
                    top(fields, UPPER),
                    pl.BlockSpec((UPPER, rows, cols), lambda i: (0, 0, 0)),
                    *(whole(a) for a in halo[1:]),
                ],
                early_shape,
                whole(early_shape),
                "early_levels",
                grid=(1,),
                scratch=[pltpu.VMEM((UPPER, tall, cols), F32)],
                us=2,
            )
            planes, send = call(
                kernel,
                (*operands, early, send),
                [*[NEAR] * 5, UNREAD],
                (planes_shape, send_shape),
                (NEAR, UNREAD),
                "exchange",
                aliases={0: 0, 5: 1},
                scratch=scratch,
            )
        if step == 3:
            before = ()
            for tracer in range(tracers):
                before = (deep_levels(tracer, before, halo),)
            (out,) = before
            operands = (*operands, early)
            return call(
                functools.partial(kernel, unread=1),
                (*operands, out),
                [*(whole(a) for a in operands), UNREAD],
                shaped(*fields.shape),
                top(fields, STEPS),
                "last_exchange",
                grid=(1,),
                aliases={len(operands): 0},
            )[None]


def solution(mesh):
    placed = (
        P("mp", None, None, "lat", "lon"),
        P("mp", None, "lat", "lon"),
        P("mp", None, "lat", "lon"),
        P("mp", "lat", "lon"),
        P("mp", ("lat", "lon")),
        P("mp", "lat", "lon"),
    )
    return jax.shard_map(
        local,
        mesh=mesh,
        in_specs=placed,
        out_specs=P("mp", None, None, "lat", "lon"),
        check_vma=False,
    )
```

```python
import functools

import jax
import jax.numpy as jnp
from jax import lax
from jax.experimental import pallas as pl
from jax.experimental.pallas import tpu as pltpu
from jax.sharding import PartitionSpec as P

TILE = 16
STEPS = 4
F32 = jnp.float32
BF16 = jnp.bfloat16
UPPER = 8
PARTS = 2
PACKED = 32
SLAB = 4
ZONAL, MERIDIONAL, KAPPA = 0, 1, 2
COUPLING = KAPPA + STEPS
WET = COUPLING + 1
SOUTH = WET + 1
LATE = SOUTH + 2


class Place:
    def __init__(self):
        n_lat, n_lon = lax.axis_size("lat"), lax.axis_size("lon")
        lat, lon = lax.axis_index("lat"), lax.axis_index("lon")
        self.model = lax.axis_index("mp")
        self.east = lat * n_lon + lax.rem(lon + 1, n_lon)
        self.west = lat * n_lon + lax.rem(lon + n_lon - 1, n_lon)
        self.north = lax.rem(lat + 1, n_lat) * n_lon + lon
        self.has_north = lat < n_lat - 1


def lane_iota(shape):
    return lax.broadcasted_iota(jnp.int32, shape, len(shape) - 1)


def row_iota(shape):
    return lax.broadcasted_iota(jnp.int32, shape, len(shape) - 2)


def lane_roll(value, shift):
    shift = shift % value.shape[-1]
    return value if shift == 0 else pltpu.roll(value, shift, 1)


def lanes_at(value, index):
    return jnp.take_along_axis(value, index, axis=1)


def next_row(value):
    return pltpu.roll(value, value.shape[0] - 1, 0)


def three_parts(value):
    high = value.astype(BF16)
    rest = value - high.astype(F32)
    middle = rest.astype(BF16)
    low = (rest - middle.astype(F32)).astype(BF16)
    return high, middle, low


def picked(one_hot, value):
    return jnp.dot(one_hot, jnp.concatenate(three_parts(value), axis=0), preferred_element_type=F32)


def spread_by(value, one_hot):
    one_hot = jnp.concatenate([one_hot] * 3, axis=0)
    return jnp.dot(jnp.concatenate(three_parts(value), axis=1), one_hot, preferred_element_type=F32)


def pack_halo(fields_ref, kappa_ref, courant_ref, rows_ref, columns_ref):
    tracers, levels, rows, cols = fields_ref.shape
    lane = lane_iota((rows, cols))
    upper = row_iota((2 * STEPS, cols)) < STEPS
    pairs = levels // 2

    def first_rows(read, count, which):
        for pair in range(pairs):
            one = read(2 * pair)
            two = read(2 * pair + 1) if 2 * pair + 1 < count else jnp.zeros_like(one)
            rows_ref[which * pairs + pair] = jnp.where(upper, one, pltpu.roll(two, STEPS, 0))

    def first_columns(read, count, start):
        for tile in range(-(-levels // PACKED)):
            gathered = jnp.zeros((rows, cols), F32)
            for k in range(tile * PACKED, min((tile + 1) * PACKED, count)):
                place = k % PACKED
                gathered = jnp.where(lane // STEPS == place, lane_roll(read(k), place * STEPS), gathered)
            spot = slice((start + tile) * cols, (start + tile + 1) * cols)
            columns_ref[:, spot] = gathered

    tiles = -(-levels // PACKED)
    for tracer in range(tracers):
        first_rows(lambda k: fields_ref[tracer, k, 0 : 2 * STEPS, :], levels, tracer)
        first_columns(lambda k: fields_ref[tracer, k], levels, tracer * tiles)
    first_rows(lambda k: kappa_ref[k, 0 : 2 * STEPS, :], levels - 1, tracers)
    first_columns(lambda k: kappa_ref[k], levels - 1, tracers * tiles)
    rows_ref[(tracers + 1) * pairs] = jnp.where(
        upper,
        courant_ref[0, 0 : 2 * STEPS, :],
        pltpu.roll(courant_ref[1, 0 : 2 * STEPS, :], STEPS, 0),
    )
    for which in range(2):
        repeated = jnp.where(lane < STEPS, courant_ref[which], 0.0)
        shift = STEPS
        while shift < cols:
            repeated = repeated + lane_roll(repeated, shift)
            shift *= 2
        spot = slice(((tracers + 1) * tiles + which) * cols, ((tracers + 1) * tiles + which + 1) * cols)
        columns_ref[:, spot] = repeated


def wide_steps(refs, tracer, levels, tracers, all_levels, first_field, store, each_step):
    kappa_ref, courant_ref, rows_ref, columns_ref, state = refs
    rows, cols = courant_ref.shape[1:]
    pairs = all_levels // 2
    tiles = -(-all_levels // PACKED)
    used = -(-levels // PACKED)
    tall = rows + 2 * STEPS
    has_north = Place().has_north
    lane = lane_iota((tall, cols))

    def with_rows(block, which, k):
        extra = rows_ref[which * pairs + k // 2]
        if k % 2:
            extra = pltpu.roll(extra, STEPS, 0)
        return jnp.concatenate([block, jnp.where(has_north, extra, 0.0)], axis=0)

    def strip(index):
        spot = slice(index * cols, (index + 1) * cols)
        corner = jnp.where(has_north, rows_ref[(tracers + 1) * pairs + 1 + index], 0.0)
        return jnp.concatenate([columns_ref[:, spot], corner], axis=0)

    last = rows_ref[(tracers + 1) * pairs]
    last = jnp.where(has_north, last, 0.0)
    zonal = jnp.concatenate([courant_ref[0], last], axis=0)
    meridional = jnp.concatenate([courant_ref[1], pltpu.roll(last, STEPS, 0)], axis=0)
    weight = (1.0 - zonal) - meridional
    side_zonal = strip((tracers + 1) * tiles)
    side_meridional = strip((tracers + 1) * tiles + 1)
    side_weight = (1.0 - side_zonal) - side_meridional
    side = [strip(tracer * tiles + i) for i in range(used)]
    side_kappa = [strip(tracers * tiles + i) for i in range(used)]
    end = (levels - (used - 1) * PACKED) * STEPS
    if levels < all_levels:
        side_kappa[-1] = jnp.where(lane < end, side_kappa[-1], 0.0)

    def lanes_on(tiles_in, shift):
        out = []
        for i, tile in enumerate(tiles_in):
            turned = lane_roll(tile, -shift)
            other = tiles_in[(i + 1 if shift > 0 else i - 1) % len(tiles_in)]
            if len(tiles_in) > 1:
                inside = lane < cols - shift if shift > 0 else lane >= -shift
                turned = jnp.where(inside, turned, lane_roll(other, -shift))
            out.append(turned)
        return out

    for step in range(STEPS):
        height = rows if step == STEPS - 1 else tall
        z, m, w = zonal[:height], meridional[:height], weight[:height]
        at_end = lane[:height] == cols - 1
        side_east = [side_zonal * tile for tile in side]

        def field_of(k):
            if step == 0:
                return with_rows(first_field(k), tracer, k)
            return state[k]

        def advected(k):
            field = field_of(k)
            edge = lane_roll(side_east[k // PACKED], cols - 1 - (k % PACKED) * STEPS)
            east = jnp.where(at_end, edge[:height], lane_roll((z * field[:height]), cols - 1))
            north = next_row(meridional * field)[:height]
            return (w * field[:height] + east) + north

        here = advected(0)
        above = None
        for k in range(levels):
            result = here
            if k + 1 < levels:
                below = advected(k + 1)
                kappa = kappa_ref[k]
                if height > rows:
                    kappa = with_rows(kappa, tracers, k)
                flux = kappa * (below - here)
                result = result + flux
            if k > 0:
                result = result - above
            if step == STEPS - 1:
                store(k, result)
            else:
                state[k] = result
            if k + 1 < levels:
                here, above = below, flux
        if step < STEPS - 1:
            east = lanes_on(side_east, 1)
            advected_side = [
                (side_weight * tile + turned) + next_row(side_meridional * tile)
                for tile, turned in zip(side, east)
            ]
            under = lanes_on(advected_side, STEPS)
            fluxes = [kap * (low - adv) for kap, low, adv in zip(side_kappa, under, advected_side)]
            over = lanes_on(fluxes, -STEPS)
            side = [(adv + flux) - up for adv, flux, up in zip(advected_side, fluxes, over)]
            if each_step is not None:
                each_step(step + 1, zonal, meridional, side_zonal, side)


def early_kernel(
    fields_ref, kappa_ref, courant_ref, rows_ref, columns_ref, early_ref, state, *, all_levels
):
    tracers, levels, rows, cols = fields_ref.shape
    refs = (kappa_ref, courant_ref, rows_ref, columns_ref, state)
    for tracer in range(tracers):

        def each_step(step, zonal, meridional, side_zonal, side):
            for j in range(2 if step >= 2 else 0):
                k = step + j
                field = state[k]
                line = ((step - 2) * tracers + tracer) * 2 + j
                early_ref[2 * line] = field[:rows]
                early_ref[2 * line + 1] = lane_roll(side_zonal * side[0], cols - 1 - k * STEPS)[:rows]
                early_ref[early_ref.shape[0] - 1, line : line + 1, :] = (
                    meridional[rows : rows + 1] * field[rows : rows + 1]
                )

        wide_steps(
            refs, tracer, levels, tracers, all_levels,
            lambda k: fields_ref[tracer, k], lambda k, value: None, each_step,
        )


def deep_kernel(after_ref, fields_ref, *refs, tracer, tracers):
    kappa_ref, courant_ref, rows_ref, columns_ref, out_ref, state = refs[-6:]
    levels = fields_ref.shape[1]

    def store(k, value):
        if k >= STEPS:
            out_ref[0, k] = value

    for k in range(STEPS):
        out_ref[0, k] = jnp.zeros(out_ref.shape[2:], F32)
    wide_steps(
        (kappa_ref, courant_ref, rows_ref, columns_ref, state),
        tracer, levels, tracers, levels, lambda k: fields_ref[0, k], store, None,
    )


def send_surface(late, below, static_ref, pack_ref, send_ref, ready):
    here = Place()
    model = here.model
    tracers = len(late)
    zonal, meridional = static_ref[ZONAL], static_ref[MERIDIONAL]
    weight = (1.0 - zonal) - meridional
    rows, cols = zonal.shape
    groups = cols // TILE
    lane = lane_iota((rows, cols))
    row = row_iota((rows, cols))
    kappa = static_ref[KAPPA]
    coupling = static_ref[COUPLING]
    group = lane // TILE
    tiles, edge_north, all_scaled = [], [], []
    share = (coupling * (1.0 - kappa), coupling * kappa)
    raw_east, factors = jnp.zeros((rows, cols), F32), jnp.zeros((rows, cols), F32)
    south_a, south_b = static_ref[SOUTH], static_ref[SOUTH + 1]
    own_north, own_east = [], jnp.zeros((rows, cols), F32)
    for tracer in range(tracers):
        parts = []
        for field in (late[tracer][0], below[tracer]):
            eastward, northward = zonal * field, meridional * field
            east = jnp.where(lane == cols - 1, 0.0, lane_roll(eastward, cols - 1))
            north = jnp.where(row == rows - 1, 0.0, next_row(northward))
            parts.append((eastward, northward, (weight * field + east) + north))
        (east0, north0, over), (east1, north1, under) = parts
        mixed = over + kappa * (under - over)
        all_scaled.append(coupling * mixed)
        edge_north.append(south_a[rows - 1 : rows] * north0[0:1] + south_b[rows - 1 : rows] * north1[0:1])
        for level, edge in enumerate((east0, east1)):
            place = lane == (tracer * 2 + level) * rows + row
            raw_east = jnp.where(place, jnp.broadcast_to(edge[:, 0:1], (rows, cols)), raw_east)
            factor = jnp.broadcast_to(share[level][:, cols - 1 : cols], (rows, cols))
            factors = jnp.where(place, factor, factors)
        for k, field in enumerate(late[tracer]):
            own_north.append(meridional[0:1] * field[0:1])
            column = jnp.broadcast_to((zonal * field)[:, 0:1], (rows, cols))
            spot = (tracer * len(late[tracer]) + k) * rows + row
            own_east = jnp.where(lane == spot, column, own_east)
    devices = send_ref.shape[0] // 2
    empty = [jnp.zeros((1, cols), F32)] * (2 * SLAB - 1)
    own_north = jnp.concatenate((own_north + empty)[: 2 * SLAB], axis=0)
    own_east = jnp.concatenate(empty + [jnp.sum(own_east, axis=0, keepdims=True)], axis=0)
    for device in range(devices):
        send_ref[model * devices + device] = own_north
    send_ref[model * devices + here.west] = own_east
    ready(0, model * devices)
    for scaled in all_scaled:
        blocks = [lanes_at(scaled, c * TILE + lane % TILE) for c in range(groups)]
        tiles.append(jnp.concatenate(blocks, axis=0))
    edge_east = [jnp.sum(edge, axis=0, keepdims=True) for edge in (raw_east, factors)]
    empty = jnp.zeros((SLAB - 2, cols), F32)
    edges = jnp.concatenate(
        [empty, edge_north[0], edge_east[0], empty, edge_north[1], edge_east[1]], axis=0
    )
    table = jnp.concatenate(three_parts(jnp.concatenate(tiles, axis=1)), axis=0)
    height = pack_ref.shape[0] // (groups * PARTS)
    main_rows = height * PARTS // devices
    slot_group = (lane_iota((height, tracers * cols)) % cols) // TILE
    line = row_iota((2 * SLAB, cols))
    for part in range(PARTS):
        start = part * groups * height
        slots = jnp.dot(
            pack_ref[start : start + groups * height, :], table, preferred_element_type=F32
        )
        packed = jnp.zeros((height, tracers * cols), F32)
        for g in range(groups):
            packed = jnp.where(slot_group == g, slots[g * height : (g + 1) * height], packed)
        there = (1 - model) * devices + part * (devices // PARTS)
        for device in range(devices // PARTS):
            block = edges
            first, offset = (device * main_rows) // 8 * 8, (device * main_rows) % 8
            for tracer in range(tracers):
                rows8 = packed[first : first + 8, tracer * cols : (tracer + 1) * cols]
                shift = (tracer * SLAB - offset) % 8
                rows8 = pltpu.roll(rows8, shift, 0) if shift else rows8
                here_rows = (line >= tracer * SLAB) & (line < tracer * SLAB + main_rows)
                block = jnp.where(here_rows, rows8, block)
            send_ref[there + device] = block
        ready(1 + part, there)


def receive_surface(recv_ref, pick_ref, static_ref, surface):
    devices = recv_ref.shape[0] // 2
    rows, cols = surface[0].shape
    groups = cols // TILE
    tracers = len(surface)
    count = rows * groups
    other = (1 - Place().model) * devices
    upper = row_iota((2 * SLAB, cols)) < SLAB
    first, second = [], []
    for pair in range(devices // 2):
        one, two = recv_ref[other + 2 * pair], recv_ref[other + 2 * pair + 1]
        first.append(jnp.where(upper, one, pltpu.roll(two, SLAB, 0)))
        second.append(jnp.where(upper, pltpu.roll(one, SLAB, 0), two))
    slab = jnp.concatenate([jnp.concatenate(half, axis=0) for half in (first, second)], axis=1)
    found = picked(pick_ref[...], slab)

    def place(kind):
        start = LATE + tracers * STEPS + kind * groups
        return static_ref[start : start + groups].reshape(count, cols)

    edge = found[2 * count : 3 * count, :cols] * found[3 * count :, cols:]
    edge = jnp.where(place(2) > 0, edge, 0.0)
    shape = (cols, tracers * cols)
    source, lane = row_iota(shape), lane_iota(shape)
    spread = (source // (2 * rows) == lane // cols) & (lane % TILE == TILE - 1)
    edge = spread_by(edge, spread.astype(F32).astype(BF16))
    main, north = place(0).astype(jnp.int32), place(1).astype(jnp.int32)
    group = lane_iota((rows, cols)) // TILE
    wet, coupling = static_ref[WET], static_ref[COUPLING]
    updated = []
    for tracer in range(tracers):
        spot = slice(tracer * cols, (tracer + 1) * cols)
        total = lanes_at(found[:count, spot], main) + lanes_at(found[count : 2 * count, spot], north)
        total = total + edge[:, spot]
        received = jnp.zeros((rows, cols), F32)
        for c in range(groups):
            received = jnp.where(group == c, total[c * rows : (c + 1) * rows], received)
        own = surface[tracer]
        updated.append(own + wet * (received - coupling * own))
    return updated


def upper_levels(recv_ref, late, early, static_ref):
    zonal, meridional = static_ref[ZONAL], static_ref[MERIDIONAL]
    weight = (1.0 - zonal) - meridional
    rows, cols = zonal.shape
    lane = lane_iota((rows, cols))
    row = row_iota((rows, cols))
    devices = recv_ref.shape[0] // 2
    here = Place()
    mine = here.model * devices
    from_east = recv_ref[mine + here.east]
    from_north = jnp.where(here.has_north, recv_ref[mine + here.north], 0.0)
    east_line = jnp.broadcast_to(from_east[from_east.shape[0] - 1 :], (rows, cols))
    stepped = []
    for tracer in range(len(late)):
        count = len(late[tracer])
        moved = []
        for k in range(count + len(early[tracer])):
            if k < count:
                field = late[tracer][k]
                index = tracer * count + k
                north_edge = from_north[index : index + 1]
                column = jnp.where(lane == index * rows + row, east_line, 0.0)
                east_edge = jnp.sum(column, axis=1, keepdims=True)
            else:
                field, north_edge, east_edge = early[tracer][k - count]
            east = jnp.where(lane == cols - 1, east_edge, lane_roll(zonal * field, cols - 1))
            north = jnp.where(row == rows - 1, north_edge, next_row(meridional * field))
            moved.append((weight * field + east) + north)
        out, above = [], None
        for k in range(len(moved) - 1):
            flux = static_ref[KAPPA + k] * (moved[k + 1] - moved[k])
            result = moved[k] + flux
            if k > 0:
                result = result - above
            out.append(result)
            above = flux
        stepped.append(out)
    return stepped


def early_levels(step, early_ref, tracer, tracers):
    if step < 2:
        return []
    found = []
    for j in range(2):
        line = ((step - 2) * tracers + tracer) * 2 + j
        norths = early_ref[early_ref.shape[0] - 1]
        found.append((early_ref[2 * line], norths[line : line + 1], early_ref[2 * line + 1]))
    return found


def first_pack_kernel(pack_ref, planes_ref, send_ref, *, tracers):
    late = [[planes_ref[LATE + tracer * STEPS + k] for k in range(STEPS)] for tracer in range(tracers)]
    send_surface(late, [values[1] for values in late], planes_ref, pack_ref, send_ref, lambda part, first: None)


def first_send_kernel(pack_ref, south_ref, static_in, send_ref, static_ref, *, tracers):
    for k in range(2):
        static_ref[SOUTH + k] = south_ref[k]
    devices = send_ref.shape[0] // 2
    rows, cols = static_in.shape[1:]
    factor = static_in[MERIDIONAL, 0:1, :]
    lines = []
    for tracer in range(tracers):
        north = [factor * static_in[LATE + tracer * STEPS + k, 0:1, :] for k in range(2)]
        lines.append(south_ref[0, rows - 1 : rows] * north[0] + south_ref[1, rows - 1 : rows] * north[1])
    row = row_iota((2 * SLAB, cols))
    edge = jnp.where(row == SLAB - 2, lines[0], jnp.where(row == 2 * SLAB - 2, lines[1], 0.0))
    model = Place().model
    for device in range(devices):
        there = (1 - model) * devices + device
        send_ref[there] = pack_ref[there] + edge
        here = model * devices + device
        send_ref[here] = pack_ref[here]


def exchange_kernel(
    static_in, recv_ref, pick_ref, pack_ref, *refs, step, tracers, count, unread=0
):
    early_ref, refs = (refs[0], refs[1:]) if step >= 2 else (None, refs)
    refs = refs[unread:]
    last = step == STEPS - 1
    refs = refs if last else refs[1:]
    static_ref = static_in if last else refs[0]
    late = [[static_ref[LATE + tracer * STEPS + k] for k in range(count)] for tracer in range(tracers)]
    early = [early_levels(step, early_ref, tracer, tracers) for tracer in range(tracers)]
    stepped = upper_levels(recv_ref, late, early, static_ref)
    surface = [values[0] for values in stepped]
    surface = receive_surface(recv_ref, pick_ref, static_ref, surface)
    for tracer in range(tracers):
        stepped[tracer][0] = surface[tracer]
    if last:
        (out_ref,) = refs
        for tracer in range(tracers):
            for k in range(STEPS):
                out_ref[tracer, k] = stepped[tracer][k]
        return
    _, send_ref, blocks_ref, sems = refs
    for tracer in range(tracers):
        for k, value in enumerate(stepped[tracer]):
            static_ref[LATE + tracer * STEPS + k] = value
    copies = []

    def ready(part, first):
        size = blocks_ref.shape[0] // (2 if part == 0 else 2 * PARTS)
        copies.append(
            pltpu.make_async_copy(
                blocks_ref.at[pl.ds(first, size)], send_ref.at[pl.ds(first, size)], sems.at[part]
            )
        )
        copies[-1].start()

    send_surface(stepped, [values[1] for values in stepped], static_ref, pack_ref, blocks_ref, ready)
    for copy in copies:
        copy.wait()


def whole(array):
    zeros = (0,) * array.ndim
    return pl.BlockSpec(array.shape, lambda i: zeros)


def top(array, levels):
    tracers, _, rows, cols = array.shape
    return pl.BlockSpec((tracers, levels, rows, cols), lambda i: (0, 0, 0, 0))


NEAR = pl.BlockSpec(memory_space=pltpu.VMEM)
FAR = pl.BlockSpec(memory_space=pltpu.HBM)
UNREAD = pl.BlockSpec(memory_space=pl.ANY)


def call(kernel, operands, specs, out_shape, out_specs, name, grid=(), aliases=None, scratch=(), us=1, mib=16):
    return pl.pallas_call(
        kernel,
        grid=grid,
        in_specs=specs,
        out_shape=out_shape,
        out_specs=out_specs,
        scratch_shapes=list(scratch),
        input_output_aliases=aliases or {},
        name=name,
        cost_estimate=pl.CostEstimate(flops=0, bytes_accessed=us * 3_000_000, transcendentals=0),
        compiler_params=pltpu.CompilerParams(vmem_limit_bytes=int(mib * 1024 * 1024)),
    )(*operands)


def shaped(*shape):
    return jax.ShapeDtypeStruct(shape, F32)


def tile_order(partner, rows, groups):
    count = rows * groups
    a = lax.broadcasted_iota(jnp.int32, (count, count), 0)
    b = lax.broadcasted_iota(jnp.int32, (count, count), 1)
    turn = (a == (b % rows) * groups + b // rows).astype(BF16)
    both = jnp.concatenate([partner // count, partner % count], axis=0)
    both = jnp.concatenate([both, jnp.zeros((6, count), jnp.int32)], axis=0).astype(F32).astype(BF16)
    lines = jnp.dot(both, turn, preferred_element_type=F32)
    columns = lax.dot_general(turn, both, (((0,), (1,)), ((), ())), preferred_element_type=F32)
    lines, columns = lines.astype(jnp.int32), columns.astype(jnp.int32)
    return lines[0:1], lines[1:2], columns[:, 0:1], columns[:, 1:2]


def write_tables(partner, pick_ref, pack_ref, planes_ref, start, rows, groups, n_lat, n_lon):
    count = rows * groups
    devices = n_lat * n_lon
    line_target, line_slot, target, slot = tile_order(partner, rows, groups)
    a = lax.broadcasted_iota(jnp.int32, (count, count), 0)
    b = lax.broadcasted_iota(jnp.int32, (count, count), 1)
    same = target == line_target
    came = jnp.sum((same & (line_slot < slot)).astype(F32), axis=1, keepdims=True).astype(jnp.int32)
    ahead = same & ((a % rows) * groups + a // rows < (b % rows) * groups + b // rows)
    sent = jnp.sum(ahead.astype(F32), axis=0, keepdims=True).astype(jnp.int32)

    row, group = slot // groups, slot % groups
    lat, lon = target // n_lon, target % n_lon
    north_ok = (row == rows - 1) & (lat < n_lat - 1)
    east_ok = group == groups - 1
    east_device = lat * n_lon + (lon + 1) % n_lon
    picks = (
        target * SLAB + came // groups,
        jnp.where(north_ok, (target + n_lon) * SLAB + SLAB - 2, -1),
        jnp.where(east_ok, east_device * SLAB + SLAB - 1, -1),
        jnp.where(east_ok, target * SLAB + SLAB - 1, -1),
    )
    index = lax.broadcasted_iota(jnp.int32, (count, pick_ref.shape[1]), 1) % (devices * SLAB)
    for kind, pick in enumerate(picks):
        pick_ref[kind * count : (kind + 1) * count, :] = (pick == index).astype(F32).astype(BF16)
    height = pack_ref.shape[0] // (groups * PARTS)
    main_rows = height * PARTS // devices
    per_part = devices // PARTS
    packing = (line_target // per_part) * (groups * height) + (sent % groups) * height
    packing = packing + (line_target % per_part) * main_rows + sent // groups
    slots = lax.broadcasted_iota(jnp.int32, (pack_ref.shape[0], count), 0)
    packing = (slots == packing).astype(F32).astype(BF16)
    for i in range(3):
        pack_ref[:, i * count : (i + 1) * count] = packing

    lane = lax.broadcasted_iota(jnp.int32, (count, groups * TILE), 1)
    places = (
        (came % groups) * TILE + lane % TILE,
        group * TILE + lane % TILE,
        (lane % rows == row) & (lane < 2 * 2 * rows),
    )
    for kind, place in enumerate(places):
        place = place.astype(F32)
        for c in range(groups):
            planes_ref[start + kind * groups + c] = place[c * rows : (c + 1) * rows]


def prepare_kernel(*refs, n_lat, n_lon):
    fields, kappa, courant, share_ref, wet_share_ref, partner, *tables, planes_ref, sems = refs
    tracers, _, rows, cols = fields.shape
    sources = [(kappa.at[0:STEPS], KAPPA, STEPS)]
    sources += [(fields.at[tracer, 0:STEPS], LATE + tracer * STEPS, STEPS) for tracer in range(tracers)]
    copies = [
        pltpu.make_async_copy(source, planes_ref.at[plane : plane + planes], sems.at[i])
        for i, (source, plane, planes) in enumerate(sources)
    ]
    for copy in copies:
        copy.start()
    write_tables(partner[...], *tables, planes_ref, LATE + tracers * STEPS, rows, cols // TILE, n_lat, n_lon)
    planes_ref[ZONAL] = courant[0]
    planes_ref[MERIDIONAL] = courant[1]
    planes_ref[COUPLING] = share_ref[0] + share_ref[1]
    planes_ref[WET] = (wet_share_ref[...] > 0).astype(F32)
    for k in (SOUTH, SOUTH + 1):
        planes_ref[k] = jnp.zeros((rows, cols), F32)
    for copy in copies:
        copy.wait()


def corner_kernel(after_ref, east_ref, rows_in, rows_ref, sems):
    cols = rows_ref.shape[2]
    tiles = east_ref.shape[1] // cols
    copies = [
        pltpu.make_async_copy(
            east_ref.at[0 : 2 * STEPS, tile * cols : (tile + 1) * cols],
            rows_ref.at[rows_ref.shape[0] - tiles + tile],
            sems.at[tile],
        )
        for tile in range(tiles)
    ]
    for copy in copies:
        copy.start()
    for copy in copies:
        copy.wait()


def halo_kernel(after_ref, fields_ref, kappa_ref, courant_ref, rows_ref, columns_ref):
    pack_halo(fields_ref, kappa_ref, courant_ref, rows_ref, columns_ref)


def local(adjoint, courant, diffusivity, coupling, partner, mask):
    fields = adjoint[0]
    courant, kappa, coupling, mask = courant[0], diffusivity[0], coupling[0], mask[0]
    tracers, levels, rows, cols = fields.shape
    groups = cols // TILE
    count = rows * groups
    n_lat, n_lon = lax.axis_size("lat"), lax.axis_size("lon")
    devices = n_lat * n_lon

    share = jnp.stack([coupling * (1.0 - kappa[0]), coupling * kappa[0]])
    wet_share = mask.astype(F32) * coupling
    from_south = lax.ppermute(share, "lat", [(i, (i + 1) % n_lat) for i in range(n_lat)])

    def exchanged(send):
        return lax.all_to_all(send, ("mp", "lat", "lon"), split_axis=0, concat_axis=0, tiled=True)

    main_rows = -(-max(2, 2 * count // devices) // groups)
    width = ((tracers + 1) * -(-levels // PACKED) + 2) * cols
    table_shapes = (
        jax.ShapeDtypeStruct((4 * count, 3 * devices * SLAB), BF16),
        jax.ShapeDtypeStruct((groups * devices * main_rows, 3 * count), BF16),
    )
    planes_shape = shaped(LATE + tracers * STEPS + 3 * groups, rows, cols)
    north_shape = shaped((tracers + 1) * (levels // 2) + 1 + width // cols, 2 * STEPS, cols)
    *tables, planes = call(
        functools.partial(prepare_kernel, n_lat=n_lat, n_lon=n_lon),
        (fields, kappa, courant, share, wet_share, partner),
        [FAR, FAR, NEAR, NEAR, NEAR, NEAR],
        (*table_shapes, planes_shape),
        (NEAR, NEAR, NEAR),
        "prepare",
        scratch=[pltpu.SemaphoreType.DMA((1 + tracers,))],
        us=2,
        mib=53,
    )
    send_shape = shaped(2 * devices, 2 * SLAB, cols)
    pack = call(
        functools.partial(first_pack_kernel, tracers=tracers),
        (tables[1], planes),
        [NEAR, NEAR],
        send_shape,
        NEAR,
        "first_pack",
    )
    send, planes = call(
        functools.partial(first_send_kernel, tracers=tracers),
        (pack, from_south, planes),
        [NEAR, NEAR, NEAR],
        (send_shape, planes_shape),
        (NEAR, NEAR),
        "first_send",
        aliases={2: 1},
    )
    recv = exchanged(send)
    halo_shapes = (north_shape, shaped(rows, width))
    north, east = call(
        halo_kernel,
        (send, fields, kappa, courant),
        [UNREAD, *(whole(a) for a in (fields, kappa, courant))],
        halo_shapes,
        tuple(whole(a) for a in halo_shapes),
        "halo",
        grid=(1,),
        us=2,
        mib=53,
    )
    east = lax.ppermute(east, "lon", [((i + 1) % n_lon, i) for i in range(n_lon)])
    tall = rows + 2 * STEPS

    def deep_levels(tracer, before, halo):
        block = pl.BlockSpec((1, levels, rows, cols), lambda i: (tracer, 0, 0, 0))
        return call(
            functools.partial(deep_kernel, tracer=tracer, tracers=tracers),
            (send, fields, *before, *halo),
            [UNREAD, block, *(UNREAD for _ in before), *(whole(a) for a in halo)],
            shaped(*fields.shape),
            block,
            "deep_levels",
            grid=(1,),
            aliases={2: 0} if before else None,
            scratch=[pltpu.VMEM((levels, tall, cols), F32)],
            us=4,
        )

    scratch = [pltpu.VMEM(send_shape.shape, F32), pltpu.SemaphoreType.DMA((1 + PARTS,))]
    reached = (STEPS, STEPS - 1, 2, 3)
    for step in range(STEPS):
        if step > 0:
            recv = exchanged(send)
        kernel = functools.partial(
            exchange_kernel, step=step, tracers=tracers, count=reached[step]
        )
        operands = (planes, recv, *tables)
        if step == 0:
            planes, send = call(
                kernel,
                (*operands, send),
                [*[NEAR] * 4, UNREAD],
                (planes_shape, send_shape),
                (NEAR, UNREAD),
                "exchange",
                aliases={0: 0, 4: 1},
                scratch=scratch,
            )
            north = call(
                corner_kernel,
                (send, east, north),
                [UNREAD, NEAR, UNREAD],
                north_shape,
                UNREAD,
                "corner",
                aliases={2: 0},
                scratch=[pltpu.SemaphoreType.DMA((width // cols,))],
            )
            north = lax.ppermute(north, "lat", [((i + 1) % n_lat, i) for i in range(n_lat)])
            halo = (kappa, courant, north, east)
        if step == 1:
            planes, send = call(
                kernel,
                (*operands, send),
                [*[NEAR] * 4, UNREAD],
                (planes_shape, send_shape),
                (NEAR, UNREAD),
                "exchange",
                aliases={0: 0, 4: 1},
                scratch=scratch,
            )
        if step == 2:
            early_shape = shaped((STEPS - 2) * tracers * 4 + 1, rows, cols)
            early = call(
                functools.partial(early_kernel, all_levels=levels),
                (fields, *halo),
                [
                    top(fields, UPPER),
                    pl.BlockSpec((UPPER, rows, cols), lambda i: (0, 0, 0)),
                    *(whole(a) for a in halo[1:]),
                ],
                early_shape,
                whole(early_shape),
                "early_levels",
                grid=(1,),
                scratch=[pltpu.VMEM((UPPER, tall, cols), F32)],
                us=2,
            )
            planes, send = call(
                kernel,
                (*operands, early, send),
                [*[NEAR] * 5, UNREAD],
                (planes_shape, send_shape),
                (NEAR, UNREAD),
                "exchange",
                aliases={0: 0, 5: 1},
                scratch=scratch,
            )
        if step == 3:
            before = ()
            for tracer in range(tracers):
                before = (deep_levels(tracer, before, halo),)
            (out,) = before
            operands = (*operands, early)
            return call(
                functools.partial(kernel, unread=1),
                (*operands, out),
                [*(whole(a) for a in operands), UNREAD],
                shaped(*fields.shape),
                top(fields, STEPS),
                "last_exchange",
                grid=(1,),
                aliases={len(operands): 0},
            )[None]


def solution(mesh):
    placed = (
        P("mp", None, None, "lat", "lon"),
        P("mp", None, "lat", "lon"),
        P("mp", None, "lat", "lon"),
        P("mp", "lat", "lon"),
        P("mp", ("lat", "lon")),
        P("mp", "lat", "lon"),
    )
    return jax.shard_map(
        local,
        mesh=mesh,
        in_specs=placed,
        out_specs=P("mp", None, None, "lat", "lon"),
        check_vma=False,
    )
```

```python
import functools

import jax
import jax.numpy as jnp
from jax import lax
from jax.experimental import pallas as pl
from jax.experimental.pallas import tpu as pltpu
from jax.sharding import PartitionSpec as P

TILE = 16
STEPS = 4
F32 = jnp.float32
BF16 = jnp.bfloat16
UPPER = 8
PARTS = 2
PACKED = 32
SLAB = 4
ZONAL, MERIDIONAL, KAPPA = 0, 1, 2
COUPLING = KAPPA + STEPS
WET = COUPLING + 1
SOUTH = WET + 1
LATE = SOUTH + 2


class Place:
    def __init__(self):
        n_lat, n_lon = lax.axis_size("lat"), lax.axis_size("lon")
        lat, lon = lax.axis_index("lat"), lax.axis_index("lon")
        self.model = lax.axis_index("mp")
        self.east = lat * n_lon + lax.rem(lon + 1, n_lon)
        self.west = lat * n_lon + lax.rem(lon + n_lon - 1, n_lon)
        self.north = lax.rem(lat + 1, n_lat) * n_lon + lon
        self.has_north = lat < n_lat - 1


def lane_iota(shape):
    return lax.broadcasted_iota(jnp.int32, shape, len(shape) - 1)


def row_iota(shape):
    return lax.broadcasted_iota(jnp.int32, shape, len(shape) - 2)


def lane_roll(value, shift):
    shift = shift % value.shape[-1]
    return value if shift == 0 else pltpu.roll(value, shift, 1)


def lanes_at(value, index):
    return jnp.take_along_axis(value, index, axis=1)


def next_row(value):
    return pltpu.roll(value, value.shape[0] - 1, 0)


def three_parts(value):
    high = value.astype(BF16)
    rest = value - high.astype(F32)
    middle = rest.astype(BF16)
    low = (rest - middle.astype(F32)).astype(BF16)
    return high, middle, low


def picked(one_hot, value):
    return jnp.dot(one_hot, jnp.concatenate(three_parts(value), axis=0), preferred_element_type=F32)


def spread_by(value, one_hot):
    one_hot = jnp.concatenate([one_hot] * 3, axis=0)
    return jnp.dot(jnp.concatenate(three_parts(value), axis=1), one_hot, preferred_element_type=F32)


def pack_halo(fields_ref, kappa_ref, courant_ref, rows_ref, columns_ref):
    tracers, levels, rows, cols = fields_ref.shape
    lane = lane_iota((rows, cols))
    upper = row_iota((2 * STEPS, cols)) < STEPS
    pairs = levels // 2

    def first_rows(read, count, which):
        for pair in range(pairs):
            one = read(2 * pair)
            two = read(2 * pair + 1) if 2 * pair + 1 < count else jnp.zeros_like(one)
            rows_ref[which * pairs + pair] = jnp.where(upper, one, pltpu.roll(two, STEPS, 0))

    def first_columns(read, count, start):
        for tile in range(-(-levels // PACKED)):
            gathered = jnp.zeros((rows, cols), F32)
            for k in range(tile * PACKED, min((tile + 1) * PACKED, count)):
                place = k % PACKED
                gathered = jnp.where(lane // STEPS == place, lane_roll(read(k), place * STEPS), gathered)
            spot = slice((start + tile) * cols, (start + tile + 1) * cols)
            columns_ref[:, spot] = gathered

    tiles = -(-levels // PACKED)
    for tracer in range(tracers):
        first_rows(lambda k: fields_ref[tracer, k, 0 : 2 * STEPS, :], levels, tracer)
        first_columns(lambda k: fields_ref[tracer, k], levels, tracer * tiles)
    first_rows(lambda k: kappa_ref[k, 0 : 2 * STEPS, :], levels - 1, tracers)
    first_columns(lambda k: kappa_ref[k], levels - 1, tracers * tiles)
    rows_ref[(tracers + 1) * pairs] = jnp.where(
        upper,
        courant_ref[0, 0 : 2 * STEPS, :],
        pltpu.roll(courant_ref[1, 0 : 2 * STEPS, :], STEPS, 0),
    )
    for which in range(2):
        repeated = jnp.where(lane < STEPS, courant_ref[which], 0.0)
        shift = STEPS
        while shift < cols:
            repeated = repeated + lane_roll(repeated, shift)
            shift *= 2
        spot = slice(((tracers + 1) * tiles + which) * cols, ((tracers + 1) * tiles + which + 1) * cols)
        columns_ref[:, spot] = repeated


def wide_steps(refs, tracer, levels, tracers, all_levels, first_field, store, each_step):
    kappa_ref, courant_ref, rows_ref, columns_ref, state = refs
    rows, cols = courant_ref.shape[1:]
    pairs = all_levels // 2
    tiles = -(-all_levels // PACKED)
    used = -(-levels // PACKED)
    tall = rows + 2 * STEPS
    has_north = Place().has_north
    lane = lane_iota((tall, cols))

    def with_rows(block, which, k):
        extra = rows_ref[which * pairs + k // 2]
        if k % 2:
            extra = pltpu.roll(extra, STEPS, 0)
        return jnp.concatenate([block, jnp.where(has_north, extra, 0.0)], axis=0)

    def strip(index):
        spot = slice(index * cols, (index + 1) * cols)
        corner = jnp.where(has_north, rows_ref[(tracers + 1) * pairs + 1 + index], 0.0)
        return jnp.concatenate([columns_ref[:, spot], corner], axis=0)

    last = rows_ref[(tracers + 1) * pairs]
    last = jnp.where(has_north, last, 0.0)
    zonal = jnp.concatenate([courant_ref[0], last], axis=0)
    meridional = jnp.concatenate([courant_ref[1], pltpu.roll(last, STEPS, 0)], axis=0)
    weight = (1.0 - zonal) - meridional
    side_zonal = strip((tracers + 1) * tiles)
    side_meridional = strip((tracers + 1) * tiles + 1)
    side_weight = (1.0 - side_zonal) - side_meridional
    side = [strip(tracer * tiles + i) for i in range(used)]
    side_kappa = [strip(tracers * tiles + i) for i in range(used)]
    end = (levels - (used - 1) * PACKED) * STEPS
    if levels < all_levels:
        side_kappa[-1] = jnp.where(lane < end, side_kappa[-1], 0.0)

    def lanes_on(tiles_in, shift):
        out = []
        for i, tile in enumerate(tiles_in):
            turned = lane_roll(tile, -shift)
            other = tiles_in[(i + 1 if shift > 0 else i - 1) % len(tiles_in)]
            if len(tiles_in) > 1:
                inside = lane < cols - shift if shift > 0 else lane >= -shift
                turned = jnp.where(inside, turned, lane_roll(other, -shift))
            out.append(turned)
        return out

    for step in range(STEPS):
        height = rows if step == STEPS - 1 else tall
        z, m, w = zonal[:height], meridional[:height], weight[:height]
        at_end = lane[:height] == cols - 1
        side_east = [side_zonal * tile for tile in side]

        def field_of(k):
            if step == 0:
                return with_rows(first_field(k), tracer, k)
            return state[k]

        def advected(k):
            field = field_of(k)
            edge = lane_roll(side_east[k // PACKED], cols - 1 - (k % PACKED) * STEPS)
            east = jnp.where(at_end, edge[:height], lane_roll((z * field[:height]), cols - 1))
            north = next_row(meridional * field)[:height]
            return (w * field[:height] + east) + north

        here = advected(0)
        above = None
        for k in range(levels):
            result = here
            if k + 1 < levels:
                below = advected(k + 1)
                kappa = kappa_ref[k]
                if height > rows:
                    kappa = with_rows(kappa, tracers, k)
                flux = kappa * (below - here)
                result = result + flux
            if k > 0:
                result = result - above
            if step == STEPS - 1:
                store(k, result)
            else:
                state[k] = result
            if k + 1 < levels:
                here, above = below, flux
        if step < STEPS - 1:
            east = lanes_on(side_east, 1)
            advected_side = [
                (side_weight * tile + turned) + next_row(side_meridional * tile)
                for tile, turned in zip(side, east)
            ]
            under = lanes_on(advected_side, STEPS)
            fluxes = [kap * (low - adv) for kap, low, adv in zip(side_kappa, under, advected_side)]
            over = lanes_on(fluxes, -STEPS)
            side = [(adv + flux) - up for adv, flux, up in zip(advected_side, fluxes, over)]
            if each_step is not None:
                each_step(step + 1, zonal, meridional, side_zonal, side)


def early_kernel(
    fields_ref, kappa_ref, courant_ref, rows_ref, columns_ref, early_ref, state, *, all_levels
):
    tracers, levels, rows, cols = fields_ref.shape
    refs = (kappa_ref, courant_ref, rows_ref, columns_ref, state)
    for tracer in range(tracers):

        def each_step(step, zonal, meridional, side_zonal, side):
            for j in range(2 if step >= 2 else 0):
                k = step + j
                field = state[k]
                line = ((step - 2) * tracers + tracer) * 2 + j
                early_ref[2 * line] = field[:rows]
                early_ref[2 * line + 1] = lane_roll(side_zonal * side[0], cols - 1 - k * STEPS)[:rows]
                early_ref[early_ref.shape[0] - 1, line : line + 1, :] = (
                    meridional[rows : rows + 1] * field[rows : rows + 1]
                )

        wide_steps(
            refs, tracer, levels, tracers, all_levels,
            lambda k: fields_ref[tracer, k], lambda k, value: None, each_step,
        )


def deep_kernel(after_ref, fields_ref, *refs, tracer, tracers):
    kappa_ref, courant_ref, rows_ref, columns_ref, out_ref, state = refs[-6:]
    levels = fields_ref.shape[1]

    def store(k, value):
        if k >= STEPS:
            out_ref[0, k] = value

    for k in range(STEPS):
        out_ref[0, k] = jnp.zeros(out_ref.shape[2:], F32)
    wide_steps(
        (kappa_ref, courant_ref, rows_ref, columns_ref, state),
        tracer, levels, tracers, levels, lambda k: fields_ref[0, k], store, None,
    )


def send_surface(late, below, static_ref, pack_ref, send_ref, ready):
    here = Place()
    model = here.model
    tracers = len(late)
    zonal, meridional = static_ref[ZONAL], static_ref[MERIDIONAL]
    weight = (1.0 - zonal) - meridional
    rows, cols = zonal.shape
    groups = cols // TILE
    lane = lane_iota((rows, cols))
    row = row_iota((rows, cols))
    kappa = static_ref[KAPPA]
    coupling = static_ref[COUPLING]
    group = lane // TILE
    tiles, edge_north, all_scaled = [], [], []
    share = (coupling * (1.0 - kappa), coupling * kappa)
    raw_east, factors = jnp.zeros((rows, cols), F32), jnp.zeros((rows, cols), F32)
    south_a, south_b = static_ref[SOUTH], static_ref[SOUTH + 1]
    own_north, own_east = [], jnp.zeros((rows, cols), F32)
    for tracer in range(tracers):
        parts = []
        for field in (late[tracer][0], below[tracer]):
            eastward, northward = zonal * field, meridional * field
            east = jnp.where(lane == cols - 1, 0.0, lane_roll(eastward, cols - 1))
            north = jnp.where(row == rows - 1, 0.0, next_row(northward))
            parts.append((eastward, northward, (weight * field + east) + north))
        (east0, north0, over), (east1, north1, under) = parts
        mixed = over + kappa * (under - over)
        all_scaled.append(coupling * mixed)
        edge_north.append(south_a[rows - 1 : rows] * north0[0:1] + south_b[rows - 1 : rows] * north1[0:1])
        for level, edge in enumerate((east0, east1)):
            place = lane == (tracer * 2 + level) * rows + row
            raw_east = jnp.where(place, jnp.broadcast_to(edge[:, 0:1], (rows, cols)), raw_east)
            factor = jnp.broadcast_to(share[level][:, cols - 1 : cols], (rows, cols))
            factors = jnp.where(place, factor, factors)
        for k, field in enumerate(late[tracer]):
            own_north.append(meridional[0:1] * field[0:1])
            column = jnp.broadcast_to((zonal * field)[:, 0:1], (rows, cols))
            spot = (tracer * len(late[tracer]) + k) * rows + row
            own_east = jnp.where(lane == spot, column, own_east)
    devices = send_ref.shape[0] // 2
    empty = [jnp.zeros((1, cols), F32)] * (2 * SLAB - 1)
    own_north = jnp.concatenate((own_north + empty)[: 2 * SLAB], axis=0)
    own_east = jnp.concatenate(empty + [jnp.sum(own_east, axis=0, keepdims=True)], axis=0)
    for device in range(devices):
        send_ref[model * devices + device] = own_north
    send_ref[model * devices + here.west] = own_east
    ready(0, model * devices)
    for scaled in all_scaled:
        blocks = [lanes_at(scaled, c * TILE + lane % TILE) for c in range(groups)]
        tiles.append(jnp.concatenate(blocks, axis=0))
    edge_east = [jnp.sum(edge, axis=0, keepdims=True) for edge in (raw_east, factors)]
    empty = jnp.zeros((SLAB - 2, cols), F32)
    edges = jnp.concatenate(
        [empty, edge_north[0], edge_east[0], empty, edge_north[1], edge_east[1]], axis=0
    )
    table = jnp.concatenate(three_parts(jnp.concatenate(tiles, axis=1)), axis=0)
    height = pack_ref.shape[0] // (groups * PARTS)
    main_rows = height * PARTS // devices
    slot_group = (lane_iota((height, tracers * cols)) % cols) // TILE
    line = row_iota((2 * SLAB, cols))
    for part in range(PARTS):
        start = part * groups * height
        slots = jnp.dot(
            pack_ref[start : start + groups * height, :], table, preferred_element_type=F32
        )
        packed = jnp.zeros((height, tracers * cols), F32)
        for g in range(groups):
            packed = jnp.where(slot_group == g, slots[g * height : (g + 1) * height], packed)
        there = (1 - model) * devices + part * (devices // PARTS)
        for device in range(devices // PARTS):
            block = edges
            first, offset = (device * main_rows) // 8 * 8, (device * main_rows) % 8
            for tracer in range(tracers):
                rows8 = packed[first : first + 8, tracer * cols : (tracer + 1) * cols]
                shift = (tracer * SLAB - offset) % 8
                rows8 = pltpu.roll(rows8, shift, 0) if shift else rows8
                here_rows = (line >= tracer * SLAB) & (line < tracer * SLAB + main_rows)
                block = jnp.where(here_rows, rows8, block)
            send_ref[there + device] = block
        ready(1 + part, there)


def receive_surface(recv_ref, pick_ref, static_ref, surface):
    devices = recv_ref.shape[0] // 2
    rows, cols = surface[0].shape
    groups = cols // TILE
    tracers = len(surface)
    count = rows * groups
    other = (1 - Place().model) * devices
    upper = row_iota((2 * SLAB, cols)) < SLAB
    first, second = [], []
    for pair in range(devices // 2):
        one, two = recv_ref[other + 2 * pair], recv_ref[other + 2 * pair + 1]
        first.append(jnp.where(upper, one, pltpu.roll(two, SLAB, 0)))
        second.append(jnp.where(upper, pltpu.roll(one, SLAB, 0), two))
    slab = jnp.concatenate([jnp.concatenate(half, axis=0) for half in (first, second)], axis=1)
    found = picked(pick_ref[...], slab)

    def place(kind):
        start = LATE + tracers * STEPS + kind * groups
        return static_ref[start : start + groups].reshape(count, cols)

    edge = found[2 * count : 3 * count, :cols] * found[3 * count :, cols:]
    edge = jnp.where(place(2) > 0, edge, 0.0)
    shape = (cols, tracers * cols)
    source, lane = row_iota(shape), lane_iota(shape)
    spread = (source // (2 * rows) == lane // cols) & (lane % TILE == TILE - 1)
    edge = spread_by(edge, spread.astype(F32).astype(BF16))
    main, north = place(0).astype(jnp.int32), place(1).astype(jnp.int32)
    group = lane_iota((rows, cols)) // TILE
    wet, coupling = static_ref[WET], static_ref[COUPLING]
    updated = []
    for tracer in range(tracers):
        spot = slice(tracer * cols, (tracer + 1) * cols)
        total = lanes_at(found[:count, spot], main) + lanes_at(found[count : 2 * count, spot], north)
        total = total + edge[:, spot]
        received = jnp.zeros((rows, cols), F32)
        for c in range(groups):
            received = jnp.where(group == c, total[c * rows : (c + 1) * rows], received)
        own = surface[tracer]
        updated.append(own + wet * (received - coupling * own))
    return updated


def upper_levels(recv_ref, late, early, static_ref):
    zonal, meridional = static_ref[ZONAL], static_ref[MERIDIONAL]
    weight = (1.0 - zonal) - meridional
    rows, cols = zonal.shape
    lane = lane_iota((rows, cols))
    row = row_iota((rows, cols))
    devices = recv_ref.shape[0] // 2
    here = Place()
    mine = here.model * devices
    from_east = recv_ref[mine + here.east]
    from_north = jnp.where(here.has_north, recv_ref[mine + here.north], 0.0)
    east_line = jnp.broadcast_to(from_east[from_east.shape[0] - 1 :], (rows, cols))
    stepped = []
    for tracer in range(len(late)):
        count = len(late[tracer])
        moved = []
        for k in range(count + len(early[tracer])):
            if k < count:
                field = late[tracer][k]
                index = tracer * count + k
                north_edge = from_north[index : index + 1]
                column = jnp.where(lane == index * rows + row, east_line, 0.0)
                east_edge = jnp.sum(column, axis=1, keepdims=True)
            else:
                field, north_edge, east_edge = early[tracer][k - count]
            east = jnp.where(lane == cols - 1, east_edge, lane_roll(zonal * field, cols - 1))
            north = jnp.where(row == rows - 1, north_edge, next_row(meridional * field))
            moved.append((weight * field + east) + north)
        out, above = [], None
        for k in range(len(moved) - 1):
            flux = static_ref[KAPPA + k] * (moved[k + 1] - moved[k])
            result = moved[k] + flux
            if k > 0:
                result = result - above
            out.append(result)
            above = flux
        stepped.append(out)
    return stepped


def early_levels(step, early_ref, tracer, tracers):
    if step < 2:
        return []
    found = []
    for j in range(2):
        line = ((step - 2) * tracers + tracer) * 2 + j
        norths = early_ref[early_ref.shape[0] - 1]
        found.append((early_ref[2 * line], norths[line : line + 1], early_ref[2 * line + 1]))
    return found


def first_pack_kernel(pack_ref, planes_ref, send_ref, *, tracers):
    late = [[planes_ref[LATE + tracer * STEPS + k] for k in range(STEPS)] for tracer in range(tracers)]
    send_surface(late, [values[1] for values in late], planes_ref, pack_ref, send_ref, lambda part, first: None)


def first_send_kernel(pack_ref, south_ref, static_in, send_ref, static_ref, *, tracers):
    for k in range(2):
        static_ref[SOUTH + k] = south_ref[k]
    devices = send_ref.shape[0] // 2
    rows, cols = static_in.shape[1:]
    factor = static_in[MERIDIONAL, 0:1, :]
    lines = []
    for tracer in range(tracers):
        north = [factor * static_in[LATE + tracer * STEPS + k, 0:1, :] for k in range(2)]
        lines.append(south_ref[0, rows - 1 : rows] * north[0] + south_ref[1, rows - 1 : rows] * north[1])
    row = row_iota((2 * SLAB, cols))
    edge = jnp.where(row == SLAB - 2, lines[0], jnp.where(row == 2 * SLAB - 2, lines[1], 0.0))
    model = Place().model
    for device in range(devices):
        there = (1 - model) * devices + device
        send_ref[there] = pack_ref[there] + edge
        here = model * devices + device
        send_ref[here] = pack_ref[here]


def exchange_kernel(
    static_in, recv_ref, pick_ref, pack_ref, *refs, step, tracers, count, unread=0
):
    early_ref, refs = (refs[0], refs[1:]) if step >= 2 else (None, refs)
    refs = refs[unread:]
    last = step == STEPS - 1
    refs = refs if last else refs[1:]
    static_ref = static_in if last else refs[0]
    late = [[static_ref[LATE + tracer * STEPS + k] for k in range(count)] for tracer in range(tracers)]
    early = [early_levels(step, early_ref, tracer, tracers) for tracer in range(tracers)]
    stepped = upper_levels(recv_ref, late, early, static_ref)
    surface = [values[0] for values in stepped]
    surface = receive_surface(recv_ref, pick_ref, static_ref, surface)
    for tracer in range(tracers):
        stepped[tracer][0] = surface[tracer]
    if last:
        (out_ref,) = refs
        for tracer in range(tracers):
            for k in range(STEPS):
                out_ref[tracer, k] = stepped[tracer][k]
        return
    _, send_ref, blocks_ref, sems = refs
    for tracer in range(tracers):
        for k, value in enumerate(stepped[tracer]):
            static_ref[LATE + tracer * STEPS + k] = value
    copies = []

    def ready(part, first):
        size = blocks_ref.shape[0] // (2 if part == 0 else 2 * PARTS)
        copies.append(
            pltpu.make_async_copy(
                blocks_ref.at[pl.ds(first, size)], send_ref.at[pl.ds(first, size)], sems.at[part]
            )
        )
        copies[-1].start()

    send_surface(stepped, [values[1] for values in stepped], static_ref, pack_ref, blocks_ref, ready)
    for copy in copies:
        copy.wait()


def whole(array):
    zeros = (0,) * array.ndim
    return pl.BlockSpec(array.shape, lambda i: zeros)


def top(array, levels):
    tracers, _, rows, cols = array.shape
    return pl.BlockSpec((tracers, levels, rows, cols), lambda i: (0, 0, 0, 0))


NEAR = pl.BlockSpec(memory_space=pltpu.VMEM)
FAR = pl.BlockSpec(memory_space=pltpu.HBM)
UNREAD = pl.BlockSpec(memory_space=pl.ANY)


def call(kernel, operands, specs, out_shape, out_specs, name, grid=(), aliases=None, scratch=(), us=1, mib=16):
    return pl.pallas_call(
        kernel,
        grid=grid,
        in_specs=specs,
        out_shape=out_shape,
        out_specs=out_specs,
        scratch_shapes=list(scratch),
        input_output_aliases=aliases or {},
        name=name,
        cost_estimate=pl.CostEstimate(flops=0, bytes_accessed=us * 3_000_000, transcendentals=0),
        compiler_params=pltpu.CompilerParams(vmem_limit_bytes=int(mib * 1024 * 1024)),
    )(*operands)


def shaped(*shape):
    return jax.ShapeDtypeStruct(shape, F32)


def tile_order(partner, rows, groups):
    count = rows * groups
    a = lax.broadcasted_iota(jnp.int32, (count, count), 0)
    b = lax.broadcasted_iota(jnp.int32, (count, count), 1)
    turn = (a == (b % rows) * groups + b // rows).astype(BF16)
    both = jnp.concatenate([partner // count, partner % count], axis=0)
    both = jnp.concatenate([both, jnp.zeros((6, count), jnp.int32)], axis=0).astype(F32).astype(BF16)
    lines = jnp.dot(both, turn, preferred_element_type=F32)
    columns = lax.dot_general(turn, both, (((0,), (1,)), ((), ())), preferred_element_type=F32)
    lines, columns = lines.astype(jnp.int32), columns.astype(jnp.int32)
    return lines[0:1], lines[1:2], columns[:, 0:1], columns[:, 1:2]


def write_tables(partner, pick_ref, pack_ref, planes_ref, start, rows, groups, n_lat, n_lon):
    count = rows * groups
    devices = n_lat * n_lon
    line_target, line_slot, target, slot = tile_order(partner, rows, groups)
    a = lax.broadcasted_iota(jnp.int32, (count, count), 0)
    b = lax.broadcasted_iota(jnp.int32, (count, count), 1)
    same = target == line_target
    came = jnp.sum((same & (line_slot < slot)).astype(F32), axis=1, keepdims=True).astype(jnp.int32)
    ahead = same & ((a % rows) * groups + a // rows < (b % rows) * groups + b // rows)
    sent = jnp.sum(ahead.astype(F32), axis=0, keepdims=True).astype(jnp.int32)

    row, group = slot // groups, slot % groups
    lat, lon = target // n_lon, target % n_lon
    north_ok = (row == rows - 1) & (lat < n_lat - 1)
    east_ok = group == groups - 1
    east_device = lat * n_lon + (lon + 1) % n_lon
    picks = (
        target * SLAB + came // groups,
        jnp.where(north_ok, (target + n_lon) * SLAB + SLAB - 2, -1),
        jnp.where(east_ok, east_device * SLAB + SLAB - 1, -1),
        jnp.where(east_ok, target * SLAB + SLAB - 1, -1),
    )
    index = lax.broadcasted_iota(jnp.int32, (count, pick_ref.shape[1]), 1) % (devices * SLAB)
    for kind, pick in enumerate(picks):
        pick_ref[kind * count : (kind + 1) * count, :] = (pick == index).astype(F32).astype(BF16)
    height = pack_ref.shape[0] // (groups * PARTS)
    main_rows = height * PARTS // devices
    per_part = devices // PARTS
    packing = (line_target // per_part) * (groups * height) + (sent % groups) * height
    packing = packing + (line_target % per_part) * main_rows + sent // groups
    slots = lax.broadcasted_iota(jnp.int32, (pack_ref.shape[0], count), 0)
    packing = (slots == packing).astype(F32).astype(BF16)
    for i in range(3):
        pack_ref[:, i * count : (i + 1) * count] = packing

    lane = lax.broadcasted_iota(jnp.int32, (count, groups * TILE), 1)
    places = (
        (came % groups) * TILE + lane % TILE,
        group * TILE + lane % TILE,
        (lane % rows == row) & (lane < 2 * 2 * rows),
    )
    for kind, place in enumerate(places):
        place = place.astype(F32)
        for c in range(groups):
            planes_ref[start + kind * groups + c] = place[c * rows : (c + 1) * rows]


def prepare_kernel(*refs, n_lat, n_lon):
    fields, kappa, courant, share_ref, wet_share_ref, partner, *tables, planes_ref, sems = refs
    tracers, _, rows, cols = fields.shape
    sources = [(kappa.at[0:STEPS], KAPPA, STEPS)]
    sources += [(fields.at[tracer, 0:STEPS], LATE + tracer * STEPS, STEPS) for tracer in range(tracers)]
    copies = [
        pltpu.make_async_copy(source, planes_ref.at[plane : plane + planes], sems.at[i])
        for i, (source, plane, planes) in enumerate(sources)
    ]
    for copy in copies:
        copy.start()
    write_tables(partner[...], *tables, planes_ref, LATE + tracers * STEPS, rows, cols // TILE, n_lat, n_lon)
    planes_ref[ZONAL] = courant[0]
    planes_ref[MERIDIONAL] = courant[1]
    planes_ref[COUPLING] = share_ref[0] + share_ref[1]
    planes_ref[WET] = (wet_share_ref[...] > 0).astype(F32)
    for k in (SOUTH, SOUTH + 1):
        planes_ref[k] = jnp.zeros((rows, cols), F32)
    for copy in copies:
        copy.wait()


def corner_kernel(after_ref, east_ref, rows_in, rows_ref, sems):
    cols = rows_ref.shape[2]
    tiles = east_ref.shape[1] // cols
    copies = [
        pltpu.make_async_copy(
            east_ref.at[0 : 2 * STEPS, tile * cols : (tile + 1) * cols],
            rows_ref.at[rows_ref.shape[0] - tiles + tile],
            sems.at[tile],
        )
        for tile in range(tiles)
    ]
    for copy in copies:
        copy.start()
    for copy in copies:
        copy.wait()


def halo_kernel(after_ref, fields_ref, kappa_ref, courant_ref, rows_ref, columns_ref):
    pack_halo(fields_ref, kappa_ref, courant_ref, rows_ref, columns_ref)


def local(adjoint, courant, diffusivity, coupling, partner, mask):
    fields = adjoint[0]
    courant, kappa, coupling, mask = courant[0], diffusivity[0], coupling[0], mask[0]
    tracers, levels, rows, cols = fields.shape
    groups = cols // TILE
    count = rows * groups
    n_lat, n_lon = lax.axis_size("lat"), lax.axis_size("lon")
    devices = n_lat * n_lon

    share = jnp.stack([coupling * (1.0 - kappa[0]), coupling * kappa[0]])
    wet_share = mask.astype(F32) * coupling
    from_south = lax.ppermute(share, "lat", [(i, (i + 1) % n_lat) for i in range(n_lat)])

    def exchanged(send):
        return lax.all_to_all(send, ("mp", "lat", "lon"), split_axis=0, concat_axis=0, tiled=True)

    main_rows = -(-max(2, 2 * count // devices) // groups)
    width = ((tracers + 1) * -(-levels // PACKED) + 2) * cols
    table_shapes = (
        jax.ShapeDtypeStruct((4 * count, 3 * devices * SLAB), BF16),
        jax.ShapeDtypeStruct((groups * devices * main_rows, 3 * count), BF16),
    )
    planes_shape = shaped(LATE + tracers * STEPS + 3 * groups, rows, cols)
    north_shape = shaped((tracers + 1) * (levels // 2) + 1 + width // cols, 2 * STEPS, cols)
    *tables, planes = call(
        functools.partial(prepare_kernel, n_lat=n_lat, n_lon=n_lon),
        (fields, kappa, courant, share, wet_share, partner),
        [FAR, FAR, NEAR, NEAR, NEAR, NEAR],
        (*table_shapes, planes_shape),
        (NEAR, NEAR, NEAR),
        "prepare",
        scratch=[pltpu.SemaphoreType.DMA((1 + tracers,))],
        us=2,
        mib=53,
    )
    send_shape = shaped(2 * devices, 2 * SLAB, cols)
    pack = call(
        functools.partial(first_pack_kernel, tracers=tracers),
        (tables[1], planes),
        [NEAR, NEAR],
        send_shape,
        NEAR,
        "first_pack",
    )
    send, planes = call(
        functools.partial(first_send_kernel, tracers=tracers),
        (pack, from_south, planes),
        [NEAR, NEAR, NEAR],
        (send_shape, planes_shape),
        (NEAR, NEAR),
        "first_send",
        aliases={2: 1},
    )
    recv = exchanged(send)
    halo_shapes = (north_shape, shaped(rows, width))
    north, east = call(
        halo_kernel,
        (send, fields, kappa, courant),
        [UNREAD, *(whole(a) for a in (fields, kappa, courant))],
        halo_shapes,
        tuple(whole(a) for a in halo_shapes),
        "halo",
        grid=(1,),
        us=2,
        mib=16,
    )
    east = lax.ppermute(east, "lon", [((i + 1) % n_lon, i) for i in range(n_lon)])
    tall = rows + 2 * STEPS

    def deep_levels(tracer, before, halo):
        block = pl.BlockSpec((1, levels, rows, cols), lambda i: (tracer, 0, 0, 0))
        return call(
            functools.partial(deep_kernel, tracer=tracer, tracers=tracers),
            (send, fields, *before, *halo),
            [UNREAD, block, *(UNREAD for _ in before), *(whole(a) for a in halo)],
            shaped(*fields.shape),
            block,
            "deep_levels",
            grid=(1,),
            aliases={2: 0} if before else None,
            scratch=[pltpu.VMEM((levels, tall, cols), F32)],
            us=4,
        )

    scratch = [pltpu.VMEM(send_shape.shape, F32), pltpu.SemaphoreType.DMA((1 + PARTS,))]
    reached = (STEPS, STEPS - 1, 2, 3)
    for step in range(STEPS):
        if step > 0:
            recv = exchanged(send)
        kernel = functools.partial(
            exchange_kernel, step=step, tracers=tracers, count=reached[step]
        )
        operands = (planes, recv, *tables)
        if step == 0:
            planes, send = call(
                kernel,
                (*operands, send),
                [*[NEAR] * 4, UNREAD],
                (planes_shape, send_shape),
                (NEAR, UNREAD),
                "exchange",
                aliases={0: 0, 4: 1},
                scratch=scratch,
            )
            north = call(
                corner_kernel,
                (send, east, north),
                [UNREAD, NEAR, UNREAD],
                north_shape,
                UNREAD,
                "corner",
                aliases={2: 0},
                scratch=[pltpu.SemaphoreType.DMA((width // cols,))],
            )
            north = lax.ppermute(north, "lat", [((i + 1) % n_lat, i) for i in range(n_lat)])
            halo = (kappa, courant, north, east)
        if step == 1:
            planes, send = call(
                kernel,
                (*operands, send),
                [*[NEAR] * 4, UNREAD],
                (planes_shape, send_shape),
                (NEAR, UNREAD),
                "exchange",
                aliases={0: 0, 4: 1},
                scratch=scratch,
            )
        if step == 2:
            early_shape = shaped((STEPS - 2) * tracers * 4 + 1, rows, cols)
            early = call(
                functools.partial(early_kernel, all_levels=levels),
                (fields, *halo),
                [
                    top(fields, UPPER),
                    pl.BlockSpec((UPPER, rows, cols), lambda i: (0, 0, 0)),
                    *(whole(a) for a in halo[1:]),
                ],
                early_shape,
                whole(early_shape),
                "early_levels",
                grid=(1,),
                scratch=[pltpu.VMEM((UPPER, tall, cols), F32)],
                us=2,
            )
            planes, send = call(
                kernel,
                (*operands, early, send),
                [*[NEAR] * 5, UNREAD],
                (planes_shape, send_shape),
                (NEAR, UNREAD),
                "exchange",
                aliases={0: 0, 5: 1},
                scratch=scratch,
            )
        if step == 3:
            before = ()
            for tracer in range(tracers):
                before = (deep_levels(tracer, before, halo),)
            (out,) = before
            operands = (*operands, early)
            return call(
                functools.partial(kernel, unread=1),
                (*operands, out),
                [*(whole(a) for a in operands), UNREAD],
                shaped(*fields.shape),
                top(fields, STEPS),
                "last_exchange",
                grid=(1,),
                aliases={len(operands): 0},
            )[None]


def solution(mesh):
    placed = (
        P("mp", None, None, "lat", "lon"),
        P("mp", None, "lat", "lon"),
        P("mp", None, "lat", "lon"),
        P("mp", "lat", "lon"),
        P("mp", ("lat", "lon")),
        P("mp", "lat", "lon"),
    )
    return jax.shard_map(
        local,
        mesh=mesh,
        in_specs=placed,
        out_specs=P("mp", None, None, "lat", "lon"),
        check_vma=False,
    )
```

```python
import functools

import jax
import jax.numpy as jnp
from jax import lax
from jax.experimental import pallas as pl
from jax.experimental.pallas import tpu as pltpu
from jax.sharding import PartitionSpec as P

TILE = 16
STEPS = 4
F32 = jnp.float32
BF16 = jnp.bfloat16
UPPER = 8
PARTS = 2
PACKED = 32
SLAB = 4
ZONAL, MERIDIONAL, KAPPA = 0, 1, 2
COUPLING = KAPPA + STEPS
WET = COUPLING + 1
SOUTH = WET + 1
LATE = SOUTH + 2


class Place:
    def __init__(self):
        n_lat, n_lon = lax.axis_size("lat"), lax.axis_size("lon")
        lat, lon = lax.axis_index("lat"), lax.axis_index("lon")
        self.model = lax.axis_index("mp")
        self.east = lat * n_lon + lax.rem(lon + 1, n_lon)
        self.west = lat * n_lon + lax.rem(lon + n_lon - 1, n_lon)
        self.north = lax.rem(lat + 1, n_lat) * n_lon + lon
        self.has_north = lat < n_lat - 1


def lane_iota(shape):
    return lax.broadcasted_iota(jnp.int32, shape, len(shape) - 1)


def row_iota(shape):
    return lax.broadcasted_iota(jnp.int32, shape, len(shape) - 2)


def lane_roll(value, shift):
    shift = shift % value.shape[-1]
    return value if shift == 0 else pltpu.roll(value, shift, 1)


def lanes_at(value, index):
    return jnp.take_along_axis(value, index, axis=1)


def next_row(value):
    return pltpu.roll(value, value.shape[0] - 1, 0)


def two_parts(value):
    high = value.astype(BF16)
    return high, (value - high.astype(F32)).astype(BF16)


def picked(one_hot, value):
    return jnp.dot(one_hot, jnp.concatenate(two_parts(value), axis=0), preferred_element_type=F32)


def spread_by(value, one_hot):
    one_hot = jnp.concatenate([one_hot] * 2, axis=0)
    return jnp.dot(jnp.concatenate(two_parts(value), axis=1), one_hot, preferred_element_type=F32)


def pack_halo(fields_ref, kappa_ref, courant_ref, rows_ref, columns_ref):
    tracers, levels, rows, cols = fields_ref.shape
    lane = lane_iota((rows, cols))
    upper = row_iota((2 * STEPS, cols)) < STEPS
    pairs = levels // 2

    def first_rows(read, count, which):
        for pair in range(pairs):
            one = read(2 * pair)
            two = read(2 * pair + 1) if 2 * pair + 1 < count else jnp.zeros_like(one)
            rows_ref[which * pairs + pair] = jnp.where(upper, one, pltpu.roll(two, STEPS, 0))

    def first_columns(read, count, start):
        for tile in range(-(-levels // PACKED)):
            gathered = jnp.zeros((rows, cols), F32)
            for k in range(tile * PACKED, min((tile + 1) * PACKED, count)):
                place = k % PACKED
                gathered = jnp.where(lane // STEPS == place, lane_roll(read(k), place * STEPS), gathered)
            spot = slice((start + tile) * cols, (start + tile + 1) * cols)
            columns_ref[:, spot] = gathered

    tiles = -(-levels // PACKED)
    for tracer in range(tracers):
        first_rows(lambda k: fields_ref[tracer, k, 0 : 2 * STEPS, :], levels, tracer)
        first_columns(lambda k: fields_ref[tracer, k], levels, tracer * tiles)
    first_rows(lambda k: kappa_ref[k, 0 : 2 * STEPS, :], levels - 1, tracers)
    first_columns(lambda k: kappa_ref[k], levels - 1, tracers * tiles)
    rows_ref[(tracers + 1) * pairs] = jnp.where(
        upper,
        courant_ref[0, 0 : 2 * STEPS, :],
        pltpu.roll(courant_ref[1, 0 : 2 * STEPS, :], STEPS, 0),
    )
    for which in range(2):
        repeated = jnp.where(lane < STEPS, courant_ref[which], 0.0)
        shift = STEPS
        while shift < cols:
            repeated = repeated + lane_roll(repeated, shift)
            shift *= 2
        spot = slice(((tracers + 1) * tiles + which) * cols, ((tracers + 1) * tiles + which + 1) * cols)
        columns_ref[:, spot] = repeated


def wide_steps(refs, tracer, levels, tracers, all_levels, first_field, store, each_step):
    kappa_ref, courant_ref, rows_ref, columns_ref, state = refs
    rows, cols = courant_ref.shape[1:]
    pairs = all_levels // 2
    tiles = -(-all_levels // PACKED)
    used = -(-levels // PACKED)
    tall = rows + 2 * STEPS
    has_north = Place().has_north
    lane = lane_iota((tall, cols))

    def with_rows(block, which, k):
        extra = rows_ref[which * pairs + k // 2]
        if k % 2:
            extra = pltpu.roll(extra, STEPS, 0)
        return jnp.concatenate([block, jnp.where(has_north, extra, 0.0)], axis=0)

    def strip(index):
        spot = slice(index * cols, (index + 1) * cols)
        corner = jnp.where(has_north, rows_ref[(tracers + 1) * pairs + 1 + index], 0.0)
        return jnp.concatenate([columns_ref[:, spot], corner], axis=0)

    last = rows_ref[(tracers + 1) * pairs]
    last = jnp.where(has_north, last, 0.0)
    zonal = jnp.concatenate([courant_ref[0], last], axis=0)
    meridional = jnp.concatenate([courant_ref[1], pltpu.roll(last, STEPS, 0)], axis=0)
    weight = (1.0 - zonal) - meridional
    side_zonal = strip((tracers + 1) * tiles)
    side_meridional = strip((tracers + 1) * tiles + 1)
    side_weight = (1.0 - side_zonal) - side_meridional
    side = [strip(tracer * tiles + i) for i in range(used)]
    side_kappa = [strip(tracers * tiles + i) for i in range(used)]
    end = (levels - (used - 1) * PACKED) * STEPS
    if levels < all_levels:
        side_kappa[-1] = jnp.where(lane < end, side_kappa[-1], 0.0)

    def lanes_on(tiles_in, shift):
        out = []
        for i, tile in enumerate(tiles_in):
            turned = lane_roll(tile, -shift)
            other = tiles_in[(i + 1 if shift > 0 else i - 1) % len(tiles_in)]
            if len(tiles_in) > 1:
                inside = lane < cols - shift if shift > 0 else lane >= -shift
                turned = jnp.where(inside, turned, lane_roll(other, -shift))
            out.append(turned)
        return out

    for step in range(STEPS):
        height = rows if step == STEPS - 1 else tall
        z, m, w = zonal[:height], meridional[:height], weight[:height]
        at_end = lane[:height] == cols - 1
        side_east = [side_zonal * tile for tile in side]

        def field_of(k):
            if step == 0:
                return with_rows(first_field(k), tracer, k)
            return state[k]

        def advected(k):
            field = field_of(k)
            edge = lane_roll(side_east[k // PACKED], cols - 1 - (k % PACKED) * STEPS)
            east = jnp.where(at_end, edge[:height], lane_roll((z * field[:height]), cols - 1))
            north = next_row(meridional * field)[:height]
            return (w * field[:height] + east) + north

        here = advected(0)
        above = None
        for k in range(levels):
            result = here
            if k + 1 < levels:
                below = advected(k + 1)
                kappa = kappa_ref[k]
                if height > rows:
                    kappa = with_rows(kappa, tracers, k)
                flux = kappa * (below - here)
                result = result + flux
            if k > 0:
                result = result - above
            if step == STEPS - 1:
                store(k, result)
            else:
                state[k] = result
            if k + 1 < levels:
                here, above = below, flux
        if step < STEPS - 1:
            east = lanes_on(side_east, 1)
            advected_side = [
                (side_weight * tile + turned) + next_row(side_meridional * tile)
                for tile, turned in zip(side, east)
            ]
            under = lanes_on(advected_side, STEPS)
            fluxes = [kap * (low - adv) for kap, low, adv in zip(side_kappa, under, advected_side)]
            over = lanes_on(fluxes, -STEPS)
            side = [(adv + flux) - up for adv, flux, up in zip(advected_side, fluxes, over)]
            if each_step is not None:
                each_step(step + 1, zonal, meridional, side_zonal, side)


def early_kernel(
    fields_ref, kappa_ref, courant_ref, rows_ref, columns_ref, early_ref, state, *, all_levels
):
    tracers, levels, rows, cols = fields_ref.shape
    refs = (kappa_ref, courant_ref, rows_ref, columns_ref, state)
    for tracer in range(tracers):

        def each_step(step, zonal, meridional, side_zonal, side):
            for j in range(2 if step >= 2 else 0):
                k = step + j
                field = state[k]
                line = ((step - 2) * tracers + tracer) * 2 + j
                early_ref[2 * line] = field[:rows]
                early_ref[2 * line + 1] = lane_roll(side_zonal * side[0], cols - 1 - k * STEPS)[:rows]
                early_ref[early_ref.shape[0] - 1, line : line + 1, :] = (
                    meridional[rows : rows + 1] * field[rows : rows + 1]
                )

        wide_steps(
            refs, tracer, levels, tracers, all_levels,
            lambda k: fields_ref[tracer, k], lambda k, value: None, each_step,
        )


def deep_kernel(after_ref, fields_ref, *refs, tracer, tracers):
    kappa_ref, courant_ref, rows_ref, columns_ref, out_ref, state = refs[-6:]
    levels = fields_ref.shape[1]

    def store(k, value):
        if k >= STEPS:
            out_ref[0, k] = value

    for k in range(STEPS):
        out_ref[0, k] = jnp.zeros(out_ref.shape[2:], F32)
    wide_steps(
        (kappa_ref, courant_ref, rows_ref, columns_ref, state),
        tracer, levels, tracers, levels, lambda k: fields_ref[0, k], store, None,
    )


def send_surface(late, below, static_ref, pack_ref, send_ref, ready):
    here = Place()
    model = here.model
    tracers = len(late)
    zonal, meridional = static_ref[ZONAL], static_ref[MERIDIONAL]
    weight = (1.0 - zonal) - meridional
    rows, cols = zonal.shape
    groups = cols // TILE
    lane = lane_iota((rows, cols))
    row = row_iota((rows, cols))
    kappa = static_ref[KAPPA]
    coupling = static_ref[COUPLING]
    group = lane // TILE
    tiles, edge_north, all_scaled = [], [], []
    share = (coupling * (1.0 - kappa), coupling * kappa)
    raw_east, factors = jnp.zeros((rows, cols), F32), jnp.zeros((rows, cols), F32)
    south_a, south_b = static_ref[SOUTH], static_ref[SOUTH + 1]
    own_north, own_east = [], jnp.zeros((rows, cols), F32)
    for tracer in range(tracers):
        parts = []
        for field in (late[tracer][0], below[tracer]):
            eastward, northward = zonal * field, meridional * field
            east = jnp.where(lane == cols - 1, 0.0, lane_roll(eastward, cols - 1))
            north = jnp.where(row == rows - 1, 0.0, next_row(northward))
            parts.append((eastward, northward, (weight * field + east) + north))
        (east0, north0, over), (east1, north1, under) = parts
        mixed = over + kappa * (under - over)
        all_scaled.append(coupling * mixed)
        edge_north.append(south_a[rows - 1 : rows] * north0[0:1] + south_b[rows - 1 : rows] * north1[0:1])
        for level, edge in enumerate((east0, east1)):
            place = lane == (tracer * 2 + level) * rows + row
            raw_east = jnp.where(place, jnp.broadcast_to(edge[:, 0:1], (rows, cols)), raw_east)
            factor = jnp.broadcast_to(share[level][:, cols - 1 : cols], (rows, cols))
            factors = jnp.where(place, factor, factors)
        for k, field in enumerate(late[tracer]):
            own_north.append(meridional[0:1] * field[0:1])
            column = jnp.broadcast_to((zonal * field)[:, 0:1], (rows, cols))
            spot = (tracer * len(late[tracer]) + k) * rows + row
            own_east = jnp.where(lane == spot, column, own_east)
    devices = send_ref.shape[0] // 2
    empty = [jnp.zeros((1, cols), F32)] * (2 * SLAB - 1)
    own_north = jnp.concatenate((own_north + empty)[: 2 * SLAB], axis=0)
    own_east = jnp.concatenate(empty + [jnp.sum(own_east, axis=0, keepdims=True)], axis=0)
    for device in range(devices):
        send_ref[model * devices + device] = own_north
    send_ref[model * devices + here.west] = own_east
    ready(0, model * devices)
    for scaled in all_scaled:
        blocks = [lanes_at(scaled, c * TILE + lane % TILE) for c in range(groups)]
        tiles.append(jnp.concatenate(blocks, axis=0))
    edge_east = [jnp.sum(edge, axis=0, keepdims=True) for edge in (raw_east, factors)]
    empty = jnp.zeros((SLAB - 2, cols), F32)
    edges = jnp.concatenate(
        [empty, edge_north[0], edge_east[0], empty, edge_north[1], edge_east[1]], axis=0
    )
    table = jnp.concatenate(two_parts(jnp.concatenate(tiles, axis=1)), axis=0)
    height = pack_ref.shape[0] // (groups * PARTS)
    main_rows = height * PARTS // devices
    slot_group = (lane_iota((height, tracers * cols)) % cols) // TILE
    line = row_iota((2 * SLAB, cols))
    for part in range(PARTS):
        start = part * groups * height
        slots = jnp.dot(
            pack_ref[start : start + groups * height, :], table, preferred_element_type=F32
        )
        packed = jnp.zeros((height, tracers * cols), F32)
        for g in range(groups):
            packed = jnp.where(slot_group == g, slots[g * height : (g + 1) * height], packed)
        there = (1 - model) * devices + part * (devices // PARTS)
        for device in range(devices // PARTS):
            block = edges
            first, offset = (device * main_rows) // 8 * 8, (device * main_rows) % 8
            for tracer in range(tracers):
                rows8 = packed[first : first + 8, tracer * cols : (tracer + 1) * cols]
                shift = (tracer * SLAB - offset) % 8
                rows8 = pltpu.roll(rows8, shift, 0) if shift else rows8
                here_rows = (line >= tracer * SLAB) & (line < tracer * SLAB + main_rows)
                block = jnp.where(here_rows, rows8, block)
            send_ref[there + device] = block
        ready(1 + part, there)


def receive_surface(recv_ref, pick_ref, static_ref, surface):
    devices = recv_ref.shape[0] // 2
    rows, cols = surface[0].shape
    groups = cols // TILE
    tracers = len(surface)
    count = rows * groups
    other = (1 - Place().model) * devices
    upper = row_iota((2 * SLAB, cols)) < SLAB
    first, second = [], []
    for pair in range(devices // 2):
        one, two = recv_ref[other + 2 * pair], recv_ref[other + 2 * pair + 1]
        first.append(jnp.where(upper, one, pltpu.roll(two, SLAB, 0)))
        second.append(jnp.where(upper, pltpu.roll(one, SLAB, 0), two))
    slab = jnp.concatenate([jnp.concatenate(half, axis=0) for half in (first, second)], axis=1)
    found = picked(pick_ref[...], slab)

    def place(kind):
        start = LATE + tracers * STEPS + kind * groups
        return static_ref[start : start + groups].reshape(count, cols)

    edge = found[2 * count : 3 * count, :cols] * found[3 * count :, cols:]
    edge = jnp.where(place(2) > 0, edge, 0.0)
    shape = (cols, tracers * cols)
    source, lane = row_iota(shape), lane_iota(shape)
    spread = (source // (2 * rows) == lane // cols) & (lane % TILE == TILE - 1)
    edge = spread_by(edge, spread.astype(F32).astype(BF16))
    main, north = place(0).astype(jnp.int32), place(1).astype(jnp.int32)
    group = lane_iota((rows, cols)) // TILE
    wet, coupling = static_ref[WET], static_ref[COUPLING]
    updated = []
    for tracer in range(tracers):
        spot = slice(tracer * cols, (tracer + 1) * cols)
        total = lanes_at(found[:count, spot], main) + lanes_at(found[count : 2 * count, spot], north)
        total = total + edge[:, spot]
        received = jnp.zeros((rows, cols), F32)
        for c in range(groups):
            received = jnp.where(group == c, total[c * rows : (c + 1) * rows], received)
        own = surface[tracer]
        updated.append(own + wet * (received - coupling * own))
    return updated


def upper_levels(recv_ref, late, early, static_ref):
    zonal, meridional = static_ref[ZONAL], static_ref[MERIDIONAL]
    weight = (1.0 - zonal) - meridional
    rows, cols = zonal.shape
    lane = lane_iota((rows, cols))
    row = row_iota((rows, cols))
    devices = recv_ref.shape[0] // 2
    here = Place()
    mine = here.model * devices
    from_east = recv_ref[mine + here.east]
    from_north = jnp.where(here.has_north, recv_ref[mine + here.north], 0.0)
    east_line = jnp.broadcast_to(from_east[from_east.shape[0] - 1 :], (rows, cols))
    stepped = []
    for tracer in range(len(late)):
        count = len(late[tracer])
        moved = []
        for k in range(count + len(early[tracer])):
            if k < count:
                field = late[tracer][k]
                index = tracer * count + k
                north_edge = from_north[index : index + 1]
                column = jnp.where(lane == index * rows + row, east_line, 0.0)
                east_edge = jnp.sum(column, axis=1, keepdims=True)
            else:
                field, north_edge, east_edge = early[tracer][k - count]
            east = jnp.where(lane == cols - 1, east_edge, lane_roll(zonal * field, cols - 1))
            north = jnp.where(row == rows - 1, north_edge, next_row(meridional * field))
            moved.append((weight * field + east) + north)
        out, above = [], None
        for k in range(len(moved) - 1):
            flux = static_ref[KAPPA + k] * (moved[k + 1] - moved[k])
            result = moved[k] + flux
            if k > 0:
                result = result - above
            out.append(result)
            above = flux
        stepped.append(out)
    return stepped


def early_levels(step, early_ref, tracer, tracers):
    if step < 2:
        return []
    found = []
    for j in range(2):
        line = ((step - 2) * tracers + tracer) * 2 + j
        norths = early_ref[early_ref.shape[0] - 1]
        found.append((early_ref[2 * line], norths[line : line + 1], early_ref[2 * line + 1]))
    return found


def first_pack_kernel(pack_ref, planes_ref, send_ref, *, tracers):
    late = [[planes_ref[LATE + tracer * STEPS + k] for k in range(STEPS)] for tracer in range(tracers)]
    send_surface(late, [values[1] for values in late], planes_ref, pack_ref, send_ref, lambda part, first: None)


def first_send_kernel(pack_ref, south_ref, static_in, send_ref, static_ref, *, tracers):
    for k in range(2):
        static_ref[SOUTH + k] = south_ref[k]
    devices = send_ref.shape[0] // 2
    rows, cols = static_in.shape[1:]
    factor = static_in[MERIDIONAL, 0:1, :]
    lines = []
    for tracer in range(tracers):
        north = [factor * static_in[LATE + tracer * STEPS + k, 0:1, :] for k in range(2)]
        lines.append(south_ref[0, rows - 1 : rows] * north[0] + south_ref[1, rows - 1 : rows] * north[1])
    row = row_iota((2 * SLAB, cols))
    edge = jnp.where(row == SLAB - 2, lines[0], jnp.where(row == 2 * SLAB - 2, lines[1], 0.0))
    model = Place().model
    for device in range(devices):
        there = (1 - model) * devices + device
        send_ref[there] = pack_ref[there] + edge
        here = model * devices + device
        send_ref[here] = pack_ref[here]


def exchange_kernel(
    static_in, recv_ref, pick_ref, pack_ref, *refs, step, tracers, count, unread=0
):
    early_ref, refs = (refs[0], refs[1:]) if step >= 2 else (None, refs)
    refs = refs[unread:]
    last = step == STEPS - 1
    refs = refs if last else refs[1:]
    static_ref = static_in if last else refs[0]
    late = [[static_ref[LATE + tracer * STEPS + k] for k in range(count)] for tracer in range(tracers)]
    early = [early_levels(step, early_ref, tracer, tracers) for tracer in range(tracers)]
    stepped = upper_levels(recv_ref, late, early, static_ref)
    surface = [values[0] for values in stepped]
    surface = receive_surface(recv_ref, pick_ref, static_ref, surface)
    for tracer in range(tracers):
        stepped[tracer][0] = surface[tracer]
    if last:
        (out_ref,) = refs
        for tracer in range(tracers):
            for k in range(STEPS):
                out_ref[tracer, k] = stepped[tracer][k]
        return
    _, send_ref, blocks_ref, sems = refs
    for tracer in range(tracers):
        for k, value in enumerate(stepped[tracer]):
            static_ref[LATE + tracer * STEPS + k] = value
    copies = []

    def ready(part, first):
        size = blocks_ref.shape[0] // (2 if part == 0 else 2 * PARTS)
        copies.append(
            pltpu.make_async_copy(
                blocks_ref.at[pl.ds(first, size)], send_ref.at[pl.ds(first, size)], sems.at[part]
            )
        )
        copies[-1].start()

    send_surface(stepped, [values[1] for values in stepped], static_ref, pack_ref, blocks_ref, ready)
    for copy in copies:
        copy.wait()


def whole(array):
    zeros = (0,) * array.ndim
    return pl.BlockSpec(array.shape, lambda i: zeros)


def top(array, levels):
    tracers, _, rows, cols = array.shape
    return pl.BlockSpec((tracers, levels, rows, cols), lambda i: (0, 0, 0, 0))


NEAR = pl.BlockSpec(memory_space=pltpu.VMEM)
FAR = pl.BlockSpec(memory_space=pltpu.HBM)
UNREAD = pl.BlockSpec(memory_space=pl.ANY)


def call(kernel, operands, specs, out_shape, out_specs, name, grid=(), aliases=None, scratch=(), us=1, mib=16):
    return pl.pallas_call(
        kernel,
        grid=grid,
        in_specs=specs,
        out_shape=out_shape,
        out_specs=out_specs,
        scratch_shapes=list(scratch),
        input_output_aliases=aliases or {},
        name=name,
        cost_estimate=pl.CostEstimate(flops=0, bytes_accessed=us * 3_000_000, transcendentals=0),
        compiler_params=pltpu.CompilerParams(vmem_limit_bytes=int(mib * 1024 * 1024)),
    )(*operands)


def shaped(*shape):
    return jax.ShapeDtypeStruct(shape, F32)


def tile_order(partner, rows, groups):
    count = rows * groups
    a = lax.broadcasted_iota(jnp.int32, (count, count), 0)
    b = lax.broadcasted_iota(jnp.int32, (count, count), 1)
    turn = (a == (b % rows) * groups + b // rows).astype(BF16)
    both = jnp.concatenate([partner // count, partner % count], axis=0)
    both = jnp.concatenate([both, jnp.zeros((6, count), jnp.int32)], axis=0).astype(F32).astype(BF16)
    lines = jnp.dot(both, turn, preferred_element_type=F32)
    columns = lax.dot_general(turn, both, (((0,), (1,)), ((), ())), preferred_element_type=F32)
    lines, columns = lines.astype(jnp.int32), columns.astype(jnp.int32)
    return lines[0:1], lines[1:2], columns[:, 0:1], columns[:, 1:2]


def write_tables(partner, pick_ref, pack_ref, planes_ref, start, rows, groups, n_lat, n_lon):
    count = rows * groups
    devices = n_lat * n_lon
    line_target, line_slot, target, slot = tile_order(partner, rows, groups)
    a = lax.broadcasted_iota(jnp.int32, (count, count), 0)
    b = lax.broadcasted_iota(jnp.int32, (count, count), 1)
    same = target == line_target
    came = jnp.sum((same & (line_slot < slot)).astype(F32), axis=1, keepdims=True).astype(jnp.int32)
    ahead = same & ((a % rows) * groups + a // rows < (b % rows) * groups + b // rows)
    sent = jnp.sum(ahead.astype(F32), axis=0, keepdims=True).astype(jnp.int32)

    row, group = slot // groups, slot % groups
    lat, lon = target // n_lon, target % n_lon
    north_ok = (row == rows - 1) & (lat < n_lat - 1)
    east_ok = group == groups - 1
    east_device = lat * n_lon + (lon + 1) % n_lon
    picks = (
        target * SLAB + came // groups,
        jnp.where(north_ok, (target + n_lon) * SLAB + SLAB - 2, -1),
        jnp.where(east_ok, east_device * SLAB + SLAB - 1, -1),
        jnp.where(east_ok, target * SLAB + SLAB - 1, -1),
    )
    index = lax.broadcasted_iota(jnp.int32, (count, pick_ref.shape[1]), 1) % (devices * SLAB)
    for kind, pick in enumerate(picks):
        pick_ref[kind * count : (kind + 1) * count, :] = (pick == index).astype(F32).astype(BF16)
    height = pack_ref.shape[0] // (groups * PARTS)
    main_rows = height * PARTS // devices
    per_part = devices // PARTS
    packing = (line_target // per_part) * (groups * height) + (sent % groups) * height
    packing = packing + (line_target % per_part) * main_rows + sent // groups
    slots = lax.broadcasted_iota(jnp.int32, (pack_ref.shape[0], count), 0)
    packing = (slots == packing).astype(F32).astype(BF16)
    for i in range(2):
        pack_ref[:, i * count : (i + 1) * count] = packing

    lane = lax.broadcasted_iota(jnp.int32, (count, groups * TILE), 1)
    places = (
        (came % groups) * TILE + lane % TILE,
        group * TILE + lane % TILE,
        (lane % rows == row) & (lane < 2 * 2 * rows),
    )
    for kind, place in enumerate(places):
        place = place.astype(F32)
        for c in range(groups):
            planes_ref[start + kind * groups + c] = place[c * rows : (c + 1) * rows]


def prepare_kernel(*refs, n_lat, n_lon):
    fields, kappa, courant, share_ref, wet_share_ref, partner, *tables, planes_ref, sems = refs
    tracers, _, rows, cols = fields.shape
    sources = [(kappa.at[0:STEPS], KAPPA, STEPS)]
    sources += [(fields.at[tracer, 0:STEPS], LATE + tracer * STEPS, STEPS) for tracer in range(tracers)]
    copies = [
        pltpu.make_async_copy(source, planes_ref.at[plane : plane + planes], sems.at[i])
        for i, (source, plane, planes) in enumerate(sources)
    ]
    for copy in copies:
        copy.start()
    write_tables(partner[...], *tables, planes_ref, LATE + tracers * STEPS, rows, cols // TILE, n_lat, n_lon)
    planes_ref[ZONAL] = courant[0]
    planes_ref[MERIDIONAL] = courant[1]
    planes_ref[COUPLING] = share_ref[0] + share_ref[1]
    planes_ref[WET] = (wet_share_ref[...] > 0).astype(F32)
    for k in (SOUTH, SOUTH + 1):
        planes_ref[k] = jnp.zeros((rows, cols), F32)
    for copy in copies:
        copy.wait()


def corner_kernel(after_ref, east_ref, rows_in, rows_ref, sems):
    cols = rows_ref.shape[2]
    tiles = east_ref.shape[1] // cols
    copies = [
        pltpu.make_async_copy(
            east_ref.at[0 : 2 * STEPS, tile * cols : (tile + 1) * cols],
            rows_ref.at[rows_ref.shape[0] - tiles + tile],
            sems.at[tile],
        )
        for tile in range(tiles)
    ]
    for copy in copies:
        copy.start()
    for copy in copies:
        copy.wait()


def halo_kernel(after_ref, fields_ref, kappa_ref, courant_ref, rows_ref, columns_ref):
    pack_halo(fields_ref, kappa_ref, courant_ref, rows_ref, columns_ref)


def local(adjoint, courant, diffusivity, coupling, partner, mask):
    fields = adjoint[0]
    courant, kappa, coupling, mask = courant[0], diffusivity[0], coupling[0], mask[0]
    tracers, levels, rows, cols = fields.shape
    groups = cols // TILE
    count = rows * groups
    n_lat, n_lon = lax.axis_size("lat"), lax.axis_size("lon")
    devices = n_lat * n_lon

    share = jnp.stack([coupling * (1.0 - kappa[0]), coupling * kappa[0]])
    wet_share = mask.astype(F32) * coupling
    from_south = lax.ppermute(share, "lat", [(i, (i + 1) % n_lat) for i in range(n_lat)])

    def exchanged(send):
        return lax.all_to_all(send, ("mp", "lat", "lon"), split_axis=0, concat_axis=0, tiled=True)

    main_rows = -(-max(2, 2 * count // devices) // groups)
    width = ((tracers + 1) * -(-levels // PACKED) + 2) * cols
    table_shapes = (
        jax.ShapeDtypeStruct((4 * count, 2 * devices * SLAB), BF16),
        jax.ShapeDtypeStruct((groups * devices * main_rows, 2 * count), BF16),
    )
    planes_shape = shaped(LATE + tracers * STEPS + 3 * groups, rows, cols)
    north_shape = shaped((tracers + 1) * (levels // 2) + 1 + width // cols, 2 * STEPS, cols)
    *tables, planes = call(
        functools.partial(prepare_kernel, n_lat=n_lat, n_lon=n_lon),
        (fields, kappa, courant, share, wet_share, partner),
        [FAR, FAR, NEAR, NEAR, NEAR, NEAR],
        (*table_shapes, planes_shape),
        (NEAR, NEAR, NEAR),
        "prepare",
        scratch=[pltpu.SemaphoreType.DMA((1 + tracers,))],
        us=2,
        mib=53,
    )
    send_shape = shaped(2 * devices, 2 * SLAB, cols)
    pack = call(
        functools.partial(first_pack_kernel, tracers=tracers),
        (tables[1], planes),
        [NEAR, NEAR],
        send_shape,
        NEAR,
        "first_pack",
    )
    send, planes = call(
        functools.partial(first_send_kernel, tracers=tracers),
        (pack, from_south, planes),
        [NEAR, NEAR, NEAR],
        (send_shape, planes_shape),
        (NEAR, NEAR),
        "first_send",
        aliases={2: 1},
    )
    recv = exchanged(send)
    halo_shapes = (north_shape, shaped(rows, width))
    north, east = call(
        halo_kernel,
        (send, fields, kappa, courant),
        [UNREAD, *(whole(a) for a in (fields, kappa, courant))],
        halo_shapes,
        tuple(whole(a) for a in halo_shapes),
        "halo",
        grid=(1,),
        us=2,
        mib=16,
    )
    east = lax.ppermute(east, "lon", [((i + 1) % n_lon, i) for i in range(n_lon)])
    tall = rows + 2 * STEPS

    def deep_levels(tracer, before, halo):
        block = pl.BlockSpec((1, levels, rows, cols), lambda i: (tracer, 0, 0, 0))
        return call(
            functools.partial(deep_kernel, tracer=tracer, tracers=tracers),
            (send, fields, *before, *halo),
            [UNREAD, block, *(UNREAD for _ in before), *(whole(a) for a in halo)],
            shaped(*fields.shape),
            block,
            "deep_levels",
            grid=(1,),
            aliases={2: 0} if before else None,
            scratch=[pltpu.VMEM((levels, tall, cols), F32)],
            us=4,
        )

    scratch = [pltpu.VMEM(send_shape.shape, F32), pltpu.SemaphoreType.DMA((1 + PARTS,))]
    reached = (STEPS, STEPS - 1, 2, 3)
    for step in range(STEPS):
        if step > 0:
            recv = exchanged(send)
        kernel = functools.partial(
            exchange_kernel, step=step, tracers=tracers, count=reached[step]
        )
        operands = (planes, recv, *tables)
        if step == 0:
            planes, send = call(
                kernel,
                (*operands, send),
                [*[NEAR] * 4, UNREAD],
                (planes_shape, send_shape),
                (NEAR, UNREAD),
                "exchange",
                aliases={0: 0, 4: 1},
                scratch=scratch,
            )
            north = call(
                corner_kernel,
                (send, east, north),
                [UNREAD, NEAR, UNREAD],
                north_shape,
                UNREAD,
                "corner",
                aliases={2: 0},
                scratch=[pltpu.SemaphoreType.DMA((width // cols,))],
            )
            north = lax.ppermute(north, "lat", [((i + 1) % n_lat, i) for i in range(n_lat)])
            halo = (kappa, courant, north, east)
        if step == 1:
            planes, send = call(
                kernel,
                (*operands, send),
                [*[NEAR] * 4, UNREAD],
                (planes_shape, send_shape),
                (NEAR, UNREAD),
                "exchange",
                aliases={0: 0, 4: 1},
                scratch=scratch,
            )
        if step == 2:
            early_shape = shaped((STEPS - 2) * tracers * 4 + 1, rows, cols)
            early = call(
                functools.partial(early_kernel, all_levels=levels),
                (fields, *halo),
                [
                    top(fields, UPPER),
                    pl.BlockSpec((UPPER, rows, cols), lambda i: (0, 0, 0)),
                    *(whole(a) for a in halo[1:]),
                ],
                early_shape,
                whole(early_shape),
                "early_levels",
                grid=(1,),
                scratch=[pltpu.VMEM((UPPER, tall, cols), F32)],
                us=2,
            )
            planes, send = call(
                kernel,
                (*operands, early, send),
                [*[NEAR] * 5, UNREAD],
                (planes_shape, send_shape),
                (NEAR, UNREAD),
                "exchange",
                aliases={0: 0, 5: 1},
                scratch=scratch,
            )
        if step == 3:
            before = ()
            for tracer in range(tracers):
                before = (deep_levels(tracer, before, halo),)
            (out,) = before
            operands = (*operands, early)
            return call(
                functools.partial(kernel, unread=1),
                (*operands, out),
                [*(whole(a) for a in operands), UNREAD],
                shaped(*fields.shape),
                top(fields, STEPS),
                "last_exchange",
                grid=(1,),
                aliases={len(operands): 0},
            )[None]


def solution(mesh):
    placed = (
        P("mp", None, None, "lat", "lon"),
        P("mp", None, "lat", "lon"),
        P("mp", None, "lat", "lon"),
        P("mp", "lat", "lon"),
        P("mp", ("lat", "lon")),
        P("mp", "lat", "lon"),
    )
    return jax.shard_map(
        local,
        mesh=mesh,
        in_specs=placed,
        out_specs=P("mp", None, None, "lat", "lon"),
        check_vma=False,
    )
```
